32 devices in a mesh: dp: 8 (over y, x, core), mp: 4 (over z).
Axes of the slice: x: 2, y: 2, z: 4, core: 2. Of those that a mesh axis runs over, the one named last changes fastest.
Arguments:
- inputs: bfloat16 [8, 1024, 1024], P('dp', 'mp'), may hold values from -6 to 6
- block_size: int32 [8], P('dp'), may hold values from 256 to 512, as said below
- gain_attn: float32 [1024], replicated, may hold values from 0.5 to 1.5
- qkv_weight: bfloat16 [1024, 3, 1024], P(None, None, 'mp'), may hold values from -0.1875 to 0.1875
- ssm_rate: float32 [1024, 16], P('mp'), may hold values from 0.001 to 0.1
- ssm_coef: float32 [1024, 16], P('mp'), may hold values from -0.15 to 0.15
- ssm_skip: float32 [1024], P('mp'), may hold values from -3 to 3
- out_weight: bfloat16 [1024, 1024], P('mp'), may hold values from -1.5 to 1.5
- gain_mlp: float32 [1024], replicated, may hold values from 0.5 to 1.5
- up_weight: bfloat16 [1024, 4096], P(None, 'mp'), may hold values from -0.1875 to 0.1875
- down_weight: bfloat16 [4096, 1024], P('mp'), may hold values from -0.09375 to 0.09375
- cotangent: bfloat16 [8, 1024, 1024], P('dp', 'mp'), may hold values from -6 to 6
Outputs:
- output: bfloat16 [8, 1024, 1024], P('dp', 'mp')
- input_grad: float32 [8, 1024, 1024], P('dp', 'mp')
- gain_attn_grad: float32 [1024], replicated
- qkv_weight_grad: float32 [1024, 3, 1024], P(None, None, 'mp')
- ssm_rate_grad: float32 [1024, 16], P('mp')
- ssm_coef_grad: float32 [1024, 16], P('mp')
- ssm_skip_grad: float32 [1024], P('mp')
- out_weight_grad: float32 [1024, 1024], P('mp')
- gain_mlp_grad: float32 [1024], replicated
- up_weight_grad: float32 [1024, 4096], P(None, 'mp')
- down_weight_grad: float32 [4096, 1024], P('mp')
The draws below stay inside these ranges and needn't reach their ends.
Inputs may be any that keep to these rules, and one draw needn't show every extreme that they name: `block_size`: each row's attention blocks hold 256 or 512 tokens, and both lengths occur among the rows.
All inputs are finite; a program needn't handle non-finite values.
Results may differ from the reference program's by a relative error of at most 0.014.
Values may be sent and summed in bfloat16 or wider, within the bound.
No kernel may reach another device: no remote copies, remote signals or barrier semaphores. Data moves between devices by JAX's collectives and lax.ppermute only.
A program may use at most 192 MiB of HBM per device.

```python
import math
import jax
import jax.numpy as jnp
from jax import lax

D = 1024
HEADS = 8
HD = 128
FF = 4096
NSTATE = 16
CTX = 128
BLOCK = 256
SSM_BLOCK = 128
LEN = 1024
ROWS = 8


def draw_block_size(key, part):
    pick_key = jax.random.fold_in(key, 11)
    order_key = jax.random.fold_in(key, 12)
    picks = jax.random.randint(pick_key, (ROWS,), 0, 2)
    order = jax.random.permutation(order_key, ROWS)
    picks = picks.at[order[0]].set(1).at[order[1]].set(0)
    return (BLOCK * (1 + picks)).astype(jnp.int32)


def steps_of(stream_key, dims, split, smallest, top_value):
    def one(dim, blocks):
        heights = jax.random.uniform(jax.random.fold_in(jax.random.fold_in(stream_key, 6), dim), (blocks,), jnp.float32, smallest / len(split), top_value / len(split))
        return jnp.repeat(jnp.exp(heights), dims[dim] // blocks).reshape((-1,) + (1,) * (len(dims) - dim - 1))

    level = one(*split[0])
    for cut in split[1:]:
        level = level * one(*cut)
    return level


def noise(own_key, shape, deviation, reach, split=(), kind=jnp.bfloat16):
    values = deviation * jax.random.normal(own_key, shape, jnp.float32)
    if split:
        values = values * steps_of(own_key, shape, split, -0.22, 0.18)
    return jnp.clip(values, -reach, reach).astype(kind)


def setup_inputs(seed: int = 0) -> dict:
    streams_of = jax.random.split(jax.random.key(seed), 13)
    inputs = noise(streams_of[0], (ROWS, LEN, D), 1.0, 6.0, ((0, 8), (1, 4)))
    block_size = draw_block_size(jax.random.fold_in(streams_of[12], 71), 0)
    gain_attn = jnp.clip(1.0 + 0.1 * jax.random.normal(streams_of[2], (D,), jnp.float32), 0.5, 1.5)
    qkv_weight = noise(streams_of[3], (D, 3, D), D ** -0.5, 0.1875, ((2, 4),))
    ssm_rate = jnp.clip(jnp.exp(math.log(0.1) - 4.6051702 * jax.random.uniform(streams_of[4], (D, NSTATE), jnp.float32) ** steps_of(streams_of[4], (D, NSTATE), ((0, 4),), -0.2, 0.2)), 0.001, 0.1)
    ssm_coef = noise(streams_of[5], (D, NSTATE), 0.025, 0.15, ((0, 4),), jnp.float32)
    ssm_skip = noise(streams_of[6], (D,), 1.0, 3.0, ((0, 4),), jnp.float32)
    out_weight = noise(streams_of[7], (D, D), (D // 64) ** -0.5, 1.5, ((0, 4),))
    gain_mlp = jnp.clip(1.0 + 0.1 * jax.random.normal(streams_of[8], (D,), jnp.float32), 0.5, 1.5)
    up_weight = noise(streams_of[9], (D, FF), D ** -0.5, 0.1875, ((1, 4),))
    down_weight = noise(streams_of[10], (FF, D), FF ** -0.5, 0.09375, ((0, 4),))
    cotangent = noise(streams_of[11], (ROWS, LEN, D), 1.0, 6.0, ((0, 8), (1, 4)))
    return {"inputs": inputs, "block_size": block_size, "gain_attn": gain_attn, "qkv_weight": qkv_weight, "ssm_rate": ssm_rate, "ssm_coef": ssm_coef, "ssm_skip": ssm_skip, "out_weight": out_weight, "gain_mlp": gain_mlp, "up_weight": up_weight, "down_weight": down_weight, "cotangent": cotangent}


@jax.custom_vjp
def low(v):
    return lax.optimization_barrier(v.astype(jnp.bfloat16)).astype(jnp.float32)

@jax.custom_vjp
def low_back(v):
    return v

def low_keep(v):
    return (low(v), None)

def low_pass(kept, grad):
    return (grad,)

def back_keep(v):
    return (v, None)

def back_low(kept, grad):
    return (low(grad),)
low.defvjp(low_keep, low_pass)
low_back.defvjp(back_keep, back_low)
epsilon = 1e-05
masked_score = -1e+30
highest = lax.Precision.HIGHEST

def layer_norm(values, row_gain):
    row_mean = lax.optimization_barrier(jnp.mean(values, axis=-1, keepdims=True))
    centred = values - row_mean
    spread = lax.optimization_barrier(jnp.mean(centred * centred, axis=-1, keepdims=True))
    return centred * lax.rsqrt(spread + epsilon) * row_gain

def ssm_mix(signal, rates, coefs, skips):
    total_rows, channels = signal.shape
    blocks = total_rows // SSM_BLOCK
    rate_t = rates.T
    coef_t = coefs.T
    lag_steps = jnp.arange(SSM_BLOCK, dtype=jnp.float32)
    kernel = lax.optimization_barrier(jnp.sum(coef_t * jnp.exp(-lag_steps[:, None, None] * rate_t), axis=1))
    offsets = jnp.arange(SSM_BLOCK, dtype=jnp.int32)[:, None] - jnp.arange(SSM_BLOCK, dtype=jnp.int32)[None, :]
    lag_ids = jnp.arange(SSM_BLOCK, dtype=jnp.int32)
    lag_table = (offsets[:, :, None] == lag_ids[None, None, :]).astype(jnp.float32).reshape(SSM_BLOCK * SSM_BLOCK, SSM_BLOCK)
    toeplitz = jnp.dot(lag_table, kernel, precision=highest).reshape(SSM_BLOCK, SSM_BLOCK, channels)
    pieces = signal.reshape(blocks, SSM_BLOCK, channels)
    inside = jnp.einsum('ijc,bjc->bic', toeplitz, pieces, precision=highest)
    end_power = jnp.exp(-(SSM_BLOCK - 1.0 - lag_steps)[:, None, None] * rate_t)
    local_state = jnp.einsum('jnc,bjc->bnc', end_power, pieces, precision=highest)
    block_ids = jnp.arange(blocks, dtype=jnp.int32)
    block_gaps = block_ids[:, None] - block_ids[None, :] - 1
    earlier = (block_gaps >= 0)[:, :, None, None]
    gap_steps = (SSM_BLOCK * jnp.maximum(block_gaps, 0)).astype(jnp.float32)
    carried = jnp.where(earlier, jnp.exp(-gap_steps[:, :, None, None] * rate_t), 0.0)
    prior_state = jnp.einsum('abnc,bnc->anc', carried, local_state, precision=highest)
    in_power = coef_t * jnp.exp(-(lag_steps + 1.0)[:, None, None] * rate_t)
    outside = jnp.einsum('inc,bnc->bic', in_power, prior_state, precision=highest)
    return (inside + outside).reshape(total_rows, channels) + skips * signal

def key_mask(tile_start, block_len):
    tile_len = 2 * BLOCK
    query_pos = tile_start + jnp.arange(tile_len, dtype=jnp.int32)
    block_start = query_pos // block_len * block_len
    key_pos = jnp.concatenate([tile_start - CTX + jnp.arange(CTX, dtype=jnp.int32), tile_start + BLOCK - CTX + jnp.arange(CTX, dtype=jnp.int32), tile_start + jnp.arange(tile_len, dtype=jnp.int32)])
    from_context = jnp.arange(2 * CTX + tile_len, dtype=jnp.int32) < 2 * CTX
    context_ok = (key_pos[None] >= block_start[:, None] - CTX) & (key_pos[None] < block_start[:, None]) & (key_pos[None] >= 0)
    own_ok = (key_pos[None] >= block_start[:, None]) & (key_pos[None] <= query_pos[:, None])
    return jnp.where(from_context[None], context_ok, own_ok)

def forward_row(params, row_values, block_len):
    gain_one, qkv_full, rates, coefs, skips, out_full, gain_two, up_full, down_full = params
    total_rows = row_values.shape[0]
    tile_len = 2 * BLOCK
    tile_count = total_rows // tile_len
    score_scale = 1.0 / math.sqrt(HD)
    normed_one = low(layer_norm(row_values, gain_one))
    qkv = jnp.dot(normed_one, qkv_full.reshape(D, 3 * D), precision=highest).reshape(total_rows, 3, HEADS, HD)
    queries = low_back(low(qkv[:, 0]))
    key_rows = low_back(low(qkv[:, 1]))
    value_rows = low_back(low(qkv[:, 2]))
    context = low(ssm_mix(normed_one, rates, coefs, skips)).reshape(total_rows, HEADS, HD)
    shifted = jnp.concatenate([jnp.zeros((CTX, HEADS, HD), jnp.float32), context[:total_rows - CTX]], axis=0)
    ctx_first = shifted.reshape(tile_count, tile_len, HEADS, HD)[:, :CTX]
    ctx_second = context.reshape(tile_count, tile_len, HEADS, HD)[:, BLOCK - CTX:BLOCK]
    starts = jnp.arange(tile_count, dtype=jnp.int32) * tile_len

    def one_tile(tile_item):
        tile_q, tile_k, tile_v, first_ctx, second_ctx, tile_start = tile_item
        all_keys = jnp.concatenate([first_ctx, second_ctx, tile_k], axis=0)
        all_values = jnp.concatenate([first_ctx, second_ctx, tile_v], axis=0)
        scores = low_back(jnp.einsum('ihd,jhd->hij', tile_q, all_keys, precision=highest) * score_scale)
        scores = jnp.where(key_mask(tile_start, block_len)[None], scores, masked_score)
        row_max = lax.optimization_barrier(jnp.max(scores, axis=-1, keepdims=True))
        weights = jnp.exp(scores - row_max)
        prob_rows = weights / lax.optimization_barrier(jnp.sum(weights, axis=-1, keepdims=True))
        mixed_out = jnp.einsum('hij,jhd->ihd', low(prob_rows), all_values, precision=highest)
        return low_back(low(mixed_out))
    attended = lax.map(jax.checkpoint(one_tile), (queries.reshape(tile_count, tile_len, HEADS, HD), key_rows.reshape(tile_count, tile_len, HEADS, HD), value_rows.reshape(tile_count, tile_len, HEADS, HD), ctx_first, ctx_second, starts)).reshape(total_rows, D)
    middle = row_values + low_back(jnp.dot(attended, out_full, precision=highest))
    normed_two = low(layer_norm(middle, gain_two))
    gate = low_back(jnp.dot(normed_two, up_full, precision=highest))
    activated = low(jax.nn.gelu(gate, approximate=False))
    return middle + low_back(jnp.dot(activated, down_full, precision=highest))

def reference(inputs, block_size, gain_attn, qkv_weight, ssm_rate, ssm_coef, ssm_skip, out_weight, gain_mlp, up_weight, down_weight, cotangent):
    params = (gain_attn.astype(jnp.float32), qkv_weight.astype(jnp.float32), ssm_rate.astype(jnp.float32), ssm_coef.astype(jnp.float32), ssm_skip.astype(jnp.float32), out_weight.astype(jnp.float32), gain_mlp.astype(jnp.float32), up_weight.astype(jnp.float32), down_weight.astype(jnp.float32))

    def per_row(gradients, row_item):
        row_values, block_len, cot_rows = row_item

        def forward_here(weights_all, row_here):
            return forward_row(weights_all, row_here, block_len)
        result, pullback = jax.vjp(forward_here, params, row_values.astype(jnp.float32))
        param_grads, row_grad = pullback(cot_rows.astype(jnp.float32))
        gradients = jax.tree.map(jnp.add, gradients, param_grads)
        return (gradients, (result.astype(jnp.bfloat16), row_grad))
    zero_grads = jax.tree.map(jnp.zeros_like, params)
    gradients, (output, input_grad) = lax.scan(per_row, zero_grads, (inputs, block_size, cotangent))
    gain_one_g, qkv_g, rate_g, coef_g, skip_g, out_g, gain_two_g, up_g, down_g = gradients
    return (output, input_grad, gain_one_g, qkv_g, rate_g, coef_g, skip_g, out_g, gain_two_g, up_g, down_g)
```

```python
from functools import partial
import math

import jax
import jax.numpy as jnp
from jax import lax
from jax.experimental import pallas as pl
from jax.experimental.pallas import tpu as pltpu
from jax.sharding import PartitionSpec as P

HD = 128
CTX = 128
GROUP = 8

f32 = jnp.float32
bf16 = jnp.bfloat16
epsilon = 1e-05
masked_score = -1e30
score_scale = 1.0 / math.sqrt(HD)
VMEM_LIMIT = 56 * 1024 * 1024

NT = (((1,), (1,)), ((), ()))
TN = (((0,), (0,)), ((), ()))
NN = (((1,), (0,)), ((), ()))


def mm(a, b, dims=NN):
    return lax.dot_general(a, b, dims, preferred_element_type=f32)


def call(kernel, out_shape, scratch=(), n_scalar=0, flops=0, moved=0):
    specs = [pl.BlockSpec(memory_space=pltpu.SMEM)] * n_scalar

    def run(*args):
        in_specs = specs + [pl.BlockSpec(memory_space=pltpu.VMEM)] * (len(args) - n_scalar)
        out_specs = jax.tree.map(lambda s: pl.BlockSpec(memory_space=pltpu.VMEM), out_shape)
        return pl.pallas_call(
            kernel,
            out_shape=out_shape,
            in_specs=in_specs,
            out_specs=out_specs,
            scratch_shapes=scratch,
            compiler_params=pltpu.CompilerParams(vmem_limit_bytes=VMEM_LIMIT),
            cost_estimate=pl.CostEstimate(flops=flops, bytes_accessed=moved, transcendentals=0),
        )(*args)

    return run


def shape(dims, dtype=f32):
    return jax.ShapeDtypeStruct(dims, dtype)


def ssm_forward(x_ref, rate_ref, coef_ref, skip_ref, win_ref, state_ref, xs):
    xs[...] = x_ref[...].astype(f32)
    decay = jnp.exp(-rate_ref[...])
    coef = coef_ref[...]
    skip = skip_ref[...]
    zero = jnp.zeros_like(decay)

    def step(eight, carry, window):
        state, slope = carry
        x8 = xs[pl.ds(pl.multiple_of(eight * 8, 8), 8), :]
        rows = []
        for k in range(8):
            slope = decay * (slope + state)
            state = decay * state + x8[k : k + 1]
            if window is not None:
                rows.append(jnp.sum(coef * state, axis=0, keepdims=True))
        if window is not None:
            at = pl.multiple_of((eight - (2 * window + 1) * 16) * 8, 8)
            win_ref[window, pl.ds(at, 8), :] = jnp.concatenate(rows, axis=0) + skip * x8
        return state, slope

    carry = (zero, zero)
    for chunk in range(4):
        window = chunk // 2 if chunk % 2 else None
        carry = lax.fori_loop(
            chunk * 16, chunk * 16 + 16, partial(step, window=window), carry
        )
    state_ref[0] = carry[0]
    state_ref[1] = carry[1]


def ssm_carry_in(local_ref, enter_ref, rate_ref, coef_ref, out_ref, acc):
    rate = rate_ref[...]
    decay = jnp.exp(-rate)
    coef = coef_ref[...]

    def step(eight, state):
        rows = []
        for k in range(8):
            rows.append(jnp.sum(coef * state, axis=0, keepdims=True))
            state = decay * state
        acc[pl.ds(pl.multiple_of(eight * 8, 8), 8), :] = jnp.concatenate(rows, axis=0)
        return state

    lax.fori_loop(0, 16, step, enter_ref[...] * jnp.exp(-129.0 * rate))
    out_ref[...] = (local_ref[...] + acc[...]).astype(bf16)


def ssm_adjoint_exit(grad_ref, rate_ref, out_ref):
    rate = rate_ref[...]
    decay = jnp.exp(-rate)

    def step(j, adj):
        eight = 15 - j
        g8 = grad_ref[pl.ds(pl.multiple_of(eight * 8, 8), 8), :]
        for k in range(7, -1, -1):
            adj = decay * adj + g8[k : k + 1]
        return adj

    adj = lax.fori_loop(0, 16, step, jnp.zeros_like(rate))
    out_ref[...] = adj * jnp.exp(-128.0 * rate)


def ssm_signal_grad(near_ref, far_ref, enter_ref, rate_ref, coef_ref, skip_ref, out_ref):
    decay = jnp.exp(-rate_ref[...])
    coef = coef_ref[...]
    skip = skip_ref[...]

    def step(j, adj, chunk):
        eight = 15 - j
        local = pl.multiple_of(eight * 8, 8)
        if chunk % 2:
            g8 = (near_ref, far_ref)[chunk // 2][pl.ds(local, 8), :]
        rows = [None] * 8
        for k in range(7, -1, -1):
            adj = decay * adj
            if chunk % 2:
                adj = adj + g8[k : k + 1]
            rows[k] = jnp.sum(coef * adj, axis=0, keepdims=True)
        y8 = jnp.concatenate(rows, axis=0)
        if chunk % 2:
            y8 = y8 + skip * g8
        out_ref[pl.ds(pl.multiple_of(chunk * 128 + eight * 8, 8), 8), :] = y8
        return adj

    adj = enter_ref[...]
    for chunk in (3, 2, 1, 0):
        adj = lax.fori_loop(0, 16, partial(step, chunk=chunk), adj)


def ssm_param_grad(
    x_ref, near_ref, far_ref, enter_ref, rate_ref, coef_ref, out_ref, skip_out_ref, xs
):
    xs[...] = x_ref[...].astype(f32)
    decay = jnp.exp(-rate_ref[...])
    zero = jnp.zeros_like(decay)

    def step(eight, carry, chunk):
        state, slope, for_coef, for_rate = carry
        x8 = xs[pl.ds(pl.multiple_of(eight * 8 + chunk * 128, 8), 8), :]
        if chunk % 2:
            g8 = (near_ref, far_ref)[chunk // 2][pl.ds(pl.multiple_of(eight * 8, 8), 8), :]
        for k in range(8):
            slope = decay * (slope + state)
            state = decay * state + x8[k : k + 1]
            if chunk % 2:
                for_coef = for_coef + state * g8[k : k + 1]
                for_rate = for_rate + slope * g8[k : k + 1]
        return state, slope, for_coef, for_rate

    carry = (enter_ref[0], enter_ref[1], zero, zero)
    for chunk in range(4):
        carry = lax.fori_loop(0, 16, partial(step, chunk=chunk), carry)
    out_ref[0] = -coef_ref[...] * carry[3]
    out_ref[1] = carry[2]
    skip_out_ref[...] = jnp.sum(xs[128:256] * near_ref[...], axis=0, keepdims=True) + jnp.sum(
        xs[384:512] * far_ref[...], axis=0, keepdims=True
    )


def causal(scores):
    rows = lax.broadcasted_iota(jnp.int32, scores.shape, 0)
    cols = lax.broadcasted_iota(jnp.int32, scores.shape, 1)
    return jnp.where(cols <= rows, scores, masked_score)


def softmax_parts(parts):
    top = parts[0].max(axis=-1, keepdims=True)
    for part in parts[1:]:
        top = jnp.maximum(top, part.max(axis=-1, keepdims=True))
    weights = [jnp.exp(part - top) for part in parts]
    total = weights[0].sum(axis=-1, keepdims=True)
    for weight in weights[1:]:
        total = total + weight.sum(axis=-1, keepdims=True)
    return [weight / total for weight in weights]


def block_probs(query, key, first, second, whole, late):
    q0, q1 = query[:256], query[256:]
    k0, k1 = key[:256], key[256:]
    has_first = late > 0
    is_whole = whole > 0
    chosen = jnp.where(is_whole, first, second)
    chosen_ok = jnp.logical_or(jnp.logical_not(is_whole), has_first)
    s00 = causal(mm(q0, k0, NT) * score_scale)
    s0c = jnp.where(has_first, mm(q0, first, NT) * score_scale, masked_score)
    s11 = causal(mm(q1, k1, NT) * score_scale)
    s10 = jnp.where(is_whole, mm(q1, k0, NT) * score_scale, masked_score)
    s1c = jnp.where(chosen_ok, mm(q1, chosen, NT) * score_scale, masked_score)
    return softmax_parts([s00, s0c]), softmax_parts([s11, s10, s1c]), chosen


def attention_forward(flag_ref, qkv_ref, first_ref, second_ref, out_ref):
    channels = first_ref.shape[1]
    for head in range(channels // HD):
        at = head * HD
        query = qkv_ref[:, at : at + HD]
        key = qkv_ref[:, channels + at : channels + at + HD]
        value = qkv_ref[:, 2 * channels + at : 2 * channels + at + HD]
        first = first_ref[:, at : at + HD]
        second = second_ref[:, at : at + HD]
        (p00, p0c), (p11, p10, p1c), chosen = block_probs(
            query, key, first, second, flag_ref[0], flag_ref[1]
        )
        v0, v1 = value[:256], value[256:]
        out_ref[:256, at : at + HD] = (
            mm(p00.astype(bf16), v0) + mm(p0c.astype(bf16), first)
        ).astype(bf16)
        out_ref[256:, at : at + HD] = (
            mm(p11.astype(bf16), v1) + mm(p10.astype(bf16), v0) + mm(p1c.astype(bf16), chosen)
        ).astype(bf16)


def attention_backward(
    flag_ref, qkv_ref, first_ref, second_ref, grad_ref, out_ref, first_out_ref, second_out_ref
):
    channels = first_ref.shape[1]
    is_whole = flag_ref[0] > 0
    for head in range(channels // HD):
        at = head * HD
        query = qkv_ref[:, at : at + HD]
        key = qkv_ref[:, channels + at : channels + at + HD]
        value = qkv_ref[:, 2 * channels + at : 2 * channels + at + HD]
        first = first_ref[:, at : at + HD]
        second = second_ref[:, at : at + HD]
        grad = grad_ref[:, at : at + HD]
        early, later, chosen = block_probs(
            query, key, first, second, flag_ref[0], flag_ref[1]
        )
        q0, q1 = query[:256], query[256:]
        k0, k1 = key[:256], key[256:]
        v0, v1 = value[:256], value[256:]
        g0, g1 = grad[:256], grad[256:]

        def score_grads(probs, rows, values):
            prob_grads = [mm(rows, v, NT) for v in values]
            centre = sum(
                (p * d).sum(axis=-1, keepdims=True) for p, d in zip(probs, prob_grads)
            )
            return [(p * (d - centre)).astype(bf16) for p, d in zip(probs, prob_grads)]

        d00, d0c = score_grads(early, g0, (v0, first))
        d11, d10, d1c = score_grads(later, g1, (v1, v0, chosen))
        p00, p0c = [p.astype(bf16) for p in early]
        p11, p10, p1c = [p.astype(bf16) for p in later]
        out_ref[:256, at : at + HD] = ((mm(d00, k0) + mm(d0c, first)) * score_scale).astype(bf16)
        out_ref[256:, at : at + HD] = (
            (mm(d11, k1) + mm(d10, k0) + mm(d1c, chosen)) * score_scale
        ).astype(bf16)
        at_k = channels + at
        out_ref[:256, at_k : at_k + HD] = (
            (mm(d00, q0, TN) + mm(d10, q1, TN)) * score_scale
        ).astype(bf16)
        out_ref[256:, at_k : at_k + HD] = (mm(d11, q1, TN) * score_scale).astype(bf16)
        at_v = 2 * channels + at
        out_ref[:256, at_v : at_v + HD] = (mm(p00, g0, TN) + mm(p10, g1, TN)).astype(bf16)
        out_ref[256:, at_v : at_v + HD] = mm(p11, g1, TN).astype(bf16)
        from_early = mm(d0c, q0, TN) * score_scale + mm(p0c, g0, TN)
        from_later = mm(d1c, q1, TN) * score_scale + mm(p1c, g1, TN)
        first_out_ref[:, at : at + HD] = from_early + jnp.where(is_whole, from_later, 0.0)
        second_out_ref[:, at : at + HD] = jnp.where(is_whole, 0.0, from_later)


def feed_forward(
    n_ref, c_ref, up0_ref, up1_ref, down0_ref, down1_ref, act_ref, gate_ref,
    down_own_ref, down_send_ref, back_own_ref, back_send_ref, acc_down, acc_back,
):
    step = pl.program_id(0)
    steps = pl.num_programs(0)
    half = n_ref.shape[0] // 2

    @pl.when(step == 0)
    def _():
        acc_down[...] = jnp.zeros_like(acc_down)
        acc_back[...] = jnp.zeros_like(acc_back)

    def body(up_ref, down_ref):
        up = up_ref[...]
        down = down_ref[...]
        gate = mm(n_ref[...], up)
        cdf = 0.5 * (1.0 + lax.erf(gate * (1.0 / math.sqrt(2.0))))
        act = (gate * cdf).astype(bf16)
        slope = cdf + gate * jnp.exp(-0.5 * gate * gate) * (1.0 / math.sqrt(2.0 * math.pi))
        act_ref[...] = act
        acc_down[...] += mm(act, down)
        grad = (mm(c_ref[...], down, NT) * slope).astype(bf16)
        gate_ref[...] = grad
        acc_back[...] += mm(grad, up, NT)

    @pl.when(step < steps // 2)
    def _():
        body(up0_ref, down0_ref)

    @pl.when(step >= steps // 2)
    def _():
        body(up1_ref, down1_ref)

    @pl.when(step == steps - 1)
    def _():
        down_own_ref[...] = acc_down[:half]
        down_send_ref[...] = acc_down[half:].astype(bf16)
        back_own_ref[...] = acc_back[:half]
        back_send_ref[...] = acc_back[half:].astype(bf16)


def run_feed_forward(rows, cot, up0, up1, down0, down1):
    tokens, width = rows.shape
    hidden = up0.shape[1]
    block = 512
    per = hidden // block
    half = tokens // 2

    def slot0(j):
        return jnp.minimum(j, per - 1)

    def slot1(j):
        return jnp.maximum(j - per, 0)

    whole = pl.BlockSpec((tokens, width), lambda j: (0, 0))
    part = pl.BlockSpec((half, width), lambda j: (0, 0))
    return pl.pallas_call(
        feed_forward,
        grid=(2 * per,),
        out_shape=(
            shape((tokens, 2 * hidden), bf16),
            shape((tokens, 2 * hidden), bf16),
            shape((half, width)),
            shape((half, width), bf16),
            shape((half, width)),
            shape((half, width), bf16),
        ),
        in_specs=[
            whole,
            whole,
            pl.BlockSpec((width, block), lambda j: (0, slot0(j))),
            pl.BlockSpec((width, block), lambda j: (0, slot1(j))),
            pl.BlockSpec((block, width), lambda j: (slot0(j), 0)),
            pl.BlockSpec((block, width), lambda j: (slot1(j), 0)),
        ],
        out_specs=(
            pl.BlockSpec((tokens, block), lambda j: (0, j)),
            pl.BlockSpec((tokens, block), lambda j: (0, j)),
            part,
            part,
            part,
            part,
        ),
        scratch_shapes=[pltpu.VMEM((tokens, width), f32), pltpu.VMEM((tokens, width), f32)],
        compiler_params=pltpu.CompilerParams(
            vmem_limit_bytes=VMEM_LIMIT, dimension_semantics=("arbitrary",)
        ),
        cost_estimate=pl.CostEstimate(
            flops=2 * 4 * tokens * width * 2 * hidden,
            bytes_accessed=16 * 1024 * 1024,
            transcendentals=0,
        ),
    )(rows, cot, up0, up1, down0, down1)


def weight_grad(place_ref, *refs, plan, n_args):
    args, (keep_ref, send_ref) = refs[:n_args], refs[n_args:]
    place = place_ref[0]
    rows = keep_ref.shape[2]
    for mat, pieces in enumerate(plan):
        for lhs_at, rhs_at, lhs_col, rhs_col, cols, out_col in pieces:
            rhs = args[rhs_at][:, rhs_col : rhs_col + cols]
            for pair in range(GROUP // 2):
                start = lhs_col + pair * 2 * rows
                block = mm(args[lhs_at][:, start : start + 2 * rows], rhs, TN).astype(bf16)
                for side in range(2):
                    target = jnp.bitwise_xor(place, 2 * pair + side)
                    slot = target // 2
                    value = block[side * rows : (side + 1) * rows]

                    @pl.when(target % 2 == 0)
                    def _():
                        keep_ref[mat, slot, :, out_col : out_col + cols] = value

                    @pl.when(target % 2 == 1)
                    def _():
                        send_ref[mat, slot, :, out_col : out_col + cols] = value


def run_weight_grad(place, args, plan, rows=128, cols=1024):
    out = shape((len(plan), GROUP // 2, rows, cols), bf16)
    tokens = args[0].shape[0]
    return call(
        partial(weight_grad, plan=plan, n_args=len(args)),
        (out, out),
        n_scalar=1,
        flops=2 * len(plan) * tokens * GROUP * rows * cols,
        moved=4 * len(plan) * GROUP * rows * cols,
    )(place, *args)


def normalise(values):
    mean = jnp.mean(values, axis=-1, keepdims=True)
    centred = values - mean
    spread = jnp.mean(centred * centred, axis=-1, keepdims=True)
    inverse = lax.rsqrt(spread + epsilon)
    return centred * inverse, inverse


def normalise_back(grad, gain, hat, inverse):
    inner = grad * gain
    back = (
        inner
        - jnp.mean(inner, axis=-1, keepdims=True)
        - hat * jnp.mean(inner * hat, axis=-1, keepdims=True)
    ) * inverse
    return back, jnp.sum(grad * hat, axis=0)


def per_device(
    inputs,
    block_size,
    gain_attn,
    qkv_weight,
    ssm_rate,
    ssm_coef,
    ssm_skip,
    out_weight,
    gain_mlp,
    up_weight,
    down_weight,
    cotangent,
    dp_size,
):
    z = lax.axis_index("mp")
    place = jnp.bitwise_and(lax.axis_index("dp"), GROUP - 1)
    odd = jnp.bitwise_and(z, 1)
    late = jnp.right_shift(z, 1)
    is_odd = odd > 0
    is_late = late > 0
    groups = [[g * GROUP + k for k in range(GROUP)] for g in range(dp_size // GROUP)]
    groups = groups if len(groups) > 1 else None

    def swap_mp(value, mask):
        return lax.ppermute(value, "mp", [(k, k ^ mask) for k in range(4)])

    def swap_dp(value, mask):
        return lax.ppermute(value, "dp", [(k, k ^ mask) for k in range(dp_size)])

    def gather(value):
        return lax.all_gather(value, "dp", axis=0, tiled=True, axis_index_groups=groups)

    def by_position(own, other):
        return jnp.where(
            is_odd, jnp.concatenate([other, own], 0), jnp.concatenate([own, other], 0)
        )

    def halves(tile):
        size = tile.shape[0] // 2
        own = lax.dynamic_slice_in_dim(tile, odd * size, size, 0)
        other = lax.dynamic_slice_in_dim(tile, (1 - odd) * size, size, 0)
        return own, other

    def swap_slots(value):
        size = value.shape[-1] // 2
        return jnp.concatenate([value[..., size:], value[..., :size]], -1)

    model_dim = inputs.shape[2]
    channels = qkv_weight.shape[2]
    rows = model_dim // GROUP
    row = inputs[0].astype(f32)
    cot = cotangent[0]
    whole = (block_size[0] > 2 * CTX).astype(jnp.int32)
    flags = jnp.stack([whole, late])
    place_arg = place.reshape(1)

    attn_slice = jnp.concatenate(
        [
            lax.dynamic_slice_in_dim(qkv_weight, place * rows, rows, 0).reshape(rows, 3 * channels),
            lax.dynamic_slice_in_dim(out_weight, place * rows, rows, 1).T,
        ],
        1,
    )
    attn_far = gather(swap_mp(attn_slice, 2))
    mlp_rows = up_weight.shape[0] // GROUP
    mlp_slice = jnp.concatenate(
        [
            lax.dynamic_slice_in_dim(up_weight, place * mlp_rows, mlp_rows, 0),
            lax.dynamic_slice_in_dim(down_weight, place * mlp_rows, mlp_rows, 0),
        ],
        0,
    )
    ssm_pack = jnp.concatenate(
        [ssm_rate.T, ssm_coef.T, ssm_skip[None], jnp.zeros((7, channels), f32)], 0
    )
    ssm_both = jnp.concatenate([ssm_pack, swap_mp(ssm_pack, 2)], 1)
    rate_t, coef_t, skip_t = ssm_both[:16], ssm_both[16:32], ssm_both[32:33]

    hat_one, inverse_one = normalise(row)
    normed_one = (hat_one * gain_attn).astype(bf16)
    tile_one = by_position(normed_one, swap_mp(normed_one, 1))
    tokens = tile_one.shape[0]
    wide = 2 * channels

    z_far = jnp.bitwise_xor(z, 2)
    signal = jnp.concatenate(
        [
            lax.dynamic_slice_in_dim(tile_one, z * channels, channels, 1),
            lax.dynamic_slice_in_dim(tile_one, z_far * channels, channels, 1),
        ],
        1,
    )
    windows, exit_state = call(
        ssm_forward,
        (shape((2, CTX, wide)), shape((2, 16, wide))),
        scratch=[pltpu.VMEM((tokens, wide), f32)],
        flops=4 * tokens * wide * 64,
        moved=4 * tokens * wide,
    )(signal, rate_t, coef_t, skip_t)
    handed = jnp.concatenate([exit_state.reshape(32, wide), windows[1]], 0)
    handed = swap_slots(lax.ppermute(handed, "mp", [(0, 2), (1, 3)]))
    enter_state = handed[:32].reshape(2, 16, wide)
    ctx_first = handed[32:].astype(bf16)
    ctx_second = call(
        ssm_carry_in,
        shape((CTX, wide), bf16),
        scratch=[pltpu.VMEM((CTX, wide), f32)],
        flops=CTX * wide * 64,
        moved=CTX * wide * 8,
    )(windows[0], enter_state[0], rate_t, coef_t)

    near_qkv = qkv_weight.reshape(model_dim, 3 * channels)
    far_qkv = attn_far[:, : 3 * channels]
    far_out = attn_far[:, 3 * channels :]
    cot_tile = jnp.concatenate([cot, swap_mp(cot, 1)], 0)
    mlp_far = gather(swap_mp(mlp_slice, 2)).reshape(GROUP, 2, mlp_rows, up_weight.shape[1])
    up_far = mlp_far[:, 0].reshape(up_weight.shape)
    down_far = mlp_far[:, 1].reshape(down_weight.shape)

    def attend(qkv, slot):
        at = slot * channels
        return call(
            attention_forward,
            shape((tokens, channels), bf16),
            n_scalar=1,
            flops=4 * tokens * channels * 512,
            moved=2 * tokens * channels * 4,
        )(flags, qkv, ctx_first[:, at : at + channels], ctx_second[:, at : at + channels])

    qkv_near = mm(tile_one, near_qkv).astype(bf16)
    attended_near = attend(qkv_near, 0)
    qkv_far = mm(tile_one, far_qkv).astype(bf16)
    attended_far = attend(qkv_far, 1)
    projected = mm(attended_near, out_weight) + mm(attended_far, far_out, NT)
    out_own, out_other = halves(projected)
    middle = row + out_own + swap_mp(out_other.astype(bf16), 1).astype(f32)

    hat_two, inverse_two = normalise(middle)
    normed_two = (hat_two * gain_mlp).astype(bf16)
    tile_two = jnp.concatenate([normed_two, swap_mp(normed_two, 1)], 0)
    activated, gate_grad, down_own, down_send, back_own, back_send = run_feed_forward(
        tile_two, cot_tile, up_weight, up_far, down_weight, down_far
    )
    normed_two_grad = back_own + swap_mp(back_send, 1).astype(f32)
    result = middle + down_own + swap_mp(down_send, 1).astype(f32)
    output = result.astype(bf16)[None]
    middle_back, gain_mlp_grad = normalise_back(normed_two_grad, gain_mlp, hat_two, inverse_two)
    middle_grad = cot.astype(f32) + middle_back
    attn_grad = middle_grad.astype(bf16)
    tile_back = by_position(attn_grad, swap_mp(attn_grad, 1))

    def reduce_over_plane(keep, send):
        total = keep.astype(f32) + swap_dp(send, 1).astype(f32)
        own = total[:, 0]
        for slot in range(1, GROUP // 2):
            own = own + swap_dp(total[:, slot].astype(bf16), 2 * slot).astype(f32)
        count = own.shape[0] // 2
        own = own[:count] + swap_mp(own[count:].astype(bf16), 2).astype(f32)
        mask = GROUP
        while mask < dp_size:
            own = own + swap_dp(own.astype(bf16), mask).astype(f32)
            mask *= 2
        own = own.astype(bf16)
        full = gather(own.reshape(count * own.shape[1], own.shape[2]))
        full = full.reshape(GROUP, count, own.shape[1], own.shape[2])
        return [
            full[:, k].reshape(GROUP * own.shape[1], own.shape[2]).astype(f32)
            for k in range(count)
        ]

    hidden = up_weight.shape[1]
    up_plan = [[(0, 1, 0, s * hidden, hidden, 0)] for s in range(2)]
    down_plan = [[(2, 3, s * hidden, 0, hidden, 0)] for s in range(2)]
    mlp_plan = [up_plan[0], down_plan[0], up_plan[1], down_plan[1]]
    mlp_keep, mlp_send = run_weight_grad(
        place_arg, (tile_two, gate_grad, activated, cot_tile), mlp_plan
    )
    up_grad, down_grad = reduce_over_plane(mlp_keep, mlp_send)

    attended_grad_near = mm(tile_back, out_weight, NT).astype(bf16)
    attended_grad_far = mm(tile_back, far_out).astype(bf16)

    def attend_back(qkv, grad, slot):
        at = slot * channels
        return call(
            attention_backward,
            (
                shape((tokens, 3 * channels), bf16),
                shape((CTX, channels)),
                shape((CTX, channels)),
            ),
            n_scalar=1,
            flops=10 * tokens * channels * 512,
            moved=2 * tokens * channels * 8,
        )(flags, qkv, ctx_first[:, at : at + channels], ctx_second[:, at : at + channels], grad)

    dqkv_near, first_near, second_near = attend_back(qkv_near, attended_grad_near, 0)
    dqkv_far, first_far, second_far = attend_back(qkv_far, attended_grad_far, 1)
    second_grad = jnp.concatenate([second_near, second_far], 1)
    exit_adjoint = call(
        ssm_adjoint_exit, shape((16, wide)), flops=CTX * wide * 32, moved=CTX * wide * 4
    )(second_grad, rate_t)
    returned = jnp.concatenate(
        [exit_adjoint, jnp.concatenate([first_near, first_far], 1)], 0
    )
    returned = swap_slots(lax.ppermute(returned, "mp", [(2, 0), (3, 1)]))
    enter_adjoint, last_grad = returned[:16], returned[16:]
    signal_grad = call(
        ssm_signal_grad,
        shape((tokens, wide)),
        flops=tokens * wide * 64,
        moved=tokens * wide * 4,
    )(second_grad, last_grad, enter_adjoint, rate_t, coef_t, skip_t)
    param_grad, skip_grad = call(
        ssm_param_grad,
        (shape((2, 16, wide)), shape((1, wide))),
        scratch=[pltpu.VMEM((tokens, wide), f32)],
        flops=tokens * wide * 96,
        moved=tokens * wide * 4,
    )(signal, second_grad, last_grad, enter_state, rate_t, coef_t)

    placed = jnp.concatenate(
        [
            jnp.where(
                z == b,
                signal_grad[:, :channels],
                jnp.where(z_far == b, signal_grad[:, channels:], 0.0),
            )
            for b in range(4)
        ],
        1,
    )
    one_back = mm(dqkv_near, near_qkv, NT) + mm(dqkv_far, far_qkv, NT) + placed
    one_own, one_other = halves(one_back)
    normed_one_grad = one_own + swap_mp(one_other.astype(bf16), 1).astype(f32)
    input_back, gain_attn_grad = normalise_back(normed_one_grad, gain_attn, hat_one, inverse_one)
    input_grad = (middle_grad + input_back)[None]

    attn_plan = [
        [(0, 1, 0, 0, 3 * channels, 0), (2, 3, 0, 0, channels, 3 * channels)],
        [(0, 4, 0, 0, 3 * channels, 0), (2, 5, 0, 0, channels, 3 * channels)],
    ]
    attn_keep, attn_send = run_weight_grad(
        place_arg,
        (tile_one, dqkv_near, tile_back, attended_near, dqkv_far, attended_far),
        attn_plan,
    )
    (attn_full,) = reduce_over_plane(attn_keep, attn_send)
    qkv_grad = attn_full[:, : 3 * channels].reshape(model_dim, 3, channels)
    out_grad = attn_full[:, 3 * channels :].T

    small = jnp.concatenate([param_grad.reshape(32, wide), skip_grad], 0)
    small = small[:, :channels] + swap_mp(small[:, channels:], 2)
    gains = jnp.stack([gain_attn_grad, gain_mlp_grad])
    for mask in (1, 2):
        gains = gains + swap_mp(gains, mask)
    packed = jnp.concatenate([small, gains.reshape(-1, channels)], 0)
    mask = 1
    while mask < dp_size:
        packed = packed + swap_dp(packed, mask)
        mask *= 2
    rate_grad = packed[:16].T
    coef_grad = packed[16:32].T
    skip_sum = packed[32]
    gains = packed[33:].reshape(2, model_dim)
    return (
        output,
        input_grad,
        gains[0],
        qkv_grad,
        rate_grad,
        coef_grad,
        skip_sum,
        out_grad,
        gains[1],
        up_grad,
        down_grad,
    )


def solution(mesh):
    return jax.shard_map(
        partial(per_device, dp_size=mesh.shape["dp"]),
        mesh=mesh,
        in_specs=(
            P("dp", "mp", None),
            P("dp"),
            P(),
            P(None, None, "mp"),
            P("mp", None),
            P("mp", None),
            P("mp"),
            P("mp", None),
            P(),
            P(None, "mp"),
            P("mp", None),
            P("dp", "mp", None),
        ),
        out_specs=(
            P("dp", "mp", None),
            P("dp", "mp", None),
            P(),
            P(None, None, "mp"),
            P("mp", None),
            P("mp", None),
            P("mp"),
            P("mp", None),
            P(),
            P(None, "mp"),
            P("mp", None),
        ),
        check_vma=False,
    )
```

```python
from functools import partial
import math

import jax
import jax.numpy as jnp
from jax import lax
from jax.experimental import pallas as pl
from jax.experimental.pallas import tpu as pltpu
from jax.sharding import PartitionSpec as P

HD = 128
CTX = 128
HALF = 256
STATES = 16
GROUP = 8

f32 = jnp.float32
bf16 = jnp.bfloat16
epsilon = 1e-05
masked_score = -1e30
score_scale = 1.0 / math.sqrt(HD)
VMEM_LIMIT = 16 * 1024 * 1024

NT = (((1,), (1,)), ((), ()))
TN = (((0,), (0,)), ((), ()))
NN = (((1,), (0,)), ((), ()))

WHOLE, LATE, ODD, NEAR, FAR, PLACE = range(6)


def mm(a, b, dims=NN):
    return lax.dot_general(a, b, dims, preferred_element_type=f32)


def shape(dims, dtype=f32):
    return jax.ShapeDtypeStruct(dims, dtype)


def call(kernel, out_shape, scratch=()):
    def run(flags, *args):
        vmem = pl.BlockSpec(memory_space=pltpu.VMEM)
        return pl.pallas_call(
            kernel,
            out_shape=out_shape,
            in_specs=[pl.BlockSpec(memory_space=pltpu.SMEM)] + [vmem] * len(args),
            out_specs=jax.tree.map(lambda _: vmem, out_shape),
            scratch_shapes=scratch,
            compiler_params=pltpu.CompilerParams(vmem_limit_bytes=VMEM_LIMIT),
            cost_estimate=pl.CostEstimate(flops=0, bytes_accessed=0, transcendentals=0),
        )(flags, *args)

    return run


SENT = (1, 5, 3, 7, 0, 4, 2, 6)


def in_sent_order(flag_ref, value_ref, out_ref, masks=SENT):
    width = value_ref.shape[1] // GROUP
    for k, mask in enumerate(masks):
        source = jnp.bitwise_xor(flag_ref[PLACE], mask)
        out_ref[:, k * width : (k + 1) * width] = value_ref[:, aligned(source * width, width)]


def aligned(start, size):
    return pl.ds(pl.multiple_of(start, size), size)


def cut_slices(flag_ref, qkv_ref, out_ref, up_ref, down_ref, attn_ref, mlp_ref):
    channels = qkv_ref.shape[2]
    rows = attn_ref.shape[0]
    for part in range(3):
        attn_ref[:, part * channels : (part + 1) * channels] = qkv_ref[part]
    attn_ref[:, 3 * channels :] = out_ref[...].T
    mlp_ref[:rows, :] = up_ref[...]
    mlp_ref[rows:, :] = down_ref[...]


def run_cut_slices(flags, qkv_parts, out_weight, up_weight, down_weight):
    channels = qkv_parts.shape[2]
    width = out_weight.shape[1]
    rows = width // GROUP
    here = lambda j, flag_ref: (flag_ref[PLACE], 0)
    return pl.pallas_call(
        cut_slices,
        grid_spec=pltpu.PrefetchScalarGridSpec(
            num_scalar_prefetch=1,
            grid=(1,),
            in_specs=[
                pl.BlockSpec((3, rows, channels), lambda j, flag_ref: (0, flag_ref[PLACE], 0)),
                pl.BlockSpec((channels, rows), lambda j, flag_ref: (0, flag_ref[PLACE])),
                pl.BlockSpec((rows, width), here),
                pl.BlockSpec((rows, width), here),
            ],
            out_specs=(
                pl.BlockSpec((rows, 4 * channels), lambda j, flag_ref: (0, 0)),
                pl.BlockSpec((2 * rows, width), lambda j, flag_ref: (0, 0)),
            ),
        ),
        out_shape=(shape((rows, 4 * channels), bf16), shape((2 * rows, width), bf16)),
        compiler_params=pltpu.CompilerParams(vmem_limit_bytes=VMEM_LIMIT),
        cost_estimate=pl.CostEstimate(flops=0, bytes_accessed=0, transcendentals=0),
    )(flags, qkv_parts, out_weight, up_weight, down_weight)


def normalise(values):
    mean = jnp.mean(values, axis=-1, keepdims=True)
    centred = values - mean
    spread = jnp.mean(centred * centred, axis=-1, keepdims=True)
    inverse = lax.rsqrt(spread + epsilon)
    return centred * inverse, inverse


def normalise_back(grad, gain, hat, inverse):
    inner = grad * gain
    return (
        inner
        - jnp.mean(inner, axis=-1, keepdims=True)
        - hat * jnp.mean(inner * hat, axis=-1, keepdims=True)
    ) * inverse


def by_rows(body, rows, block=64):
    for k in range(rows // block):
        body(slice(k * block, (k + 1) * block))


def norm_one(flag_ref, x_ref, gain_ref, out_ref):
    def body(at):
        hat, _ = normalise(x_ref[at, :].astype(f32))
        out_ref[at, :] = (hat * gain_ref[...]).astype(bf16)

    by_rows(body, x_ref.shape[0])


def norm_two(flag_ref, x_ref, own_ref, received_ref, gain_ref, middle_ref, out_ref):
    def body(at):
        middle = x_ref[at, :].astype(f32) + own_ref[at, :] + received_ref[at, :].astype(f32)
        middle_ref[at, :] = middle
        hat, _ = normalise(middle)
        out_ref[at, :] = (hat * gain_ref[...]).astype(bf16)

    by_rows(body, x_ref.shape[0])


def norm_two_back(
    flag_ref, middle_ref, own_ref, received_ref, cot_ref, gain_ref, grad_ref, low_ref, gain_out_ref
):
    sums = []

    def body(at):
        hat, inverse = normalise(middle_ref[at, :])
        grad = own_ref[at, :] + received_ref[at, :].astype(f32)
        sums.append(jnp.sum(grad * hat, axis=0, keepdims=True))
        total = cot_ref[at, :].astype(f32) + normalise_back(grad, gain_ref[...], hat, inverse)
        grad_ref[at, :] = total
        low_ref[at, :] = total.astype(bf16)

    by_rows(body, middle_ref.shape[0])
    gain_out_ref[...] = sum(sums)


def norm_one_back(
    flag_ref, x_ref, own_ref, received_ref, middle_ref, gain_ref, gain_two_grad_ref, grad_ref,
    gain_out_ref,
):
    sums = []

    def body(at):
        hat, inverse = normalise(x_ref[at, :].astype(f32))
        grad = own_ref[at, :] + received_ref[at, :].astype(f32)
        sums.append(jnp.sum(grad * hat, axis=0, keepdims=True))
        grad_ref[at, :] = middle_ref[at, :] + normalise_back(grad, gain_ref[...], hat, inverse)

    by_rows(body, x_ref.shape[0])
    width = gain_out_ref.shape[1]
    pieces = x_ref.shape[1] // width
    for which, value in enumerate((sum(sums), gain_two_grad_ref[...])):
        for k in range(pieces):
            row = which * pieces + k
            gain_out_ref[row : row + 1, :] = value[:, k * width : (k + 1) * width]


def split_three(value):
    high = value.astype(bf16)
    rest = value - high.astype(f32)
    middle = rest.astype(bf16)
    return [high, middle, (rest - middle.astype(f32)).astype(bf16)]


def join_three(ref, start, lanes):
    parts = [ref[start + k * STATES : start + (k + 1) * STATES, lanes] for k in range(3)]
    return (parts[0].astype(f32) + parts[1].astype(f32)) + parts[2].astype(f32)


def load_signal(flag_ref, tile_ref, xs):
    channels = xs.shape[1] // 2
    for half in range(2):
        source = jnp.bitwise_xor(flag_ref[ODD], half)
        for slot, name in enumerate((NEAR, FAR)):
            xs[half * HALF : (half + 1) * HALF, slot * channels : (slot + 1) * channels] = tile_ref[
                source, :, aligned(flag_ref[name] * channels, channels)
            ].astype(f32)


def ssm_forward(
    flag_ref, own_ref, other_ref, rate_ref, coef_ref, skip_ref, tile_ref, sent_ref,
    second_ref, handed_ref, xs,
):
    tile_ref[0] = own_ref[...]
    tile_ref[1] = other_ref[...]
    in_sent_order(flag_ref, own_ref, sent_ref.at[0])
    in_sent_order(flag_ref, other_ref, sent_ref.at[1])
    load_signal(flag_ref, tile_ref, xs)
    decay = jnp.exp(-rate_ref[...])
    coef = coef_ref[...]
    skip = skip_ref[...]
    zero = jnp.zeros_like(decay)

    def step(eight, carry, chunk):
        state, slope = carry
        x8 = xs[aligned((chunk * 16 + eight) * 8, 8), :]
        rows = []
        for k in range(8):
            slope = decay * (slope + state)
            state = decay * state + x8[k : k + 1]
            if chunk % 2:
                rows.append(jnp.sum(coef * state, axis=0, keepdims=True))
        if chunk % 2:
            y8 = jnp.concatenate(rows, axis=0) + skip * x8
            at = aligned(eight * 8, 8)
            if chunk == 1:
                second_ref[at, :] = y8
            else:
                xs[at, :] = y8
        return state, slope

    carry = (zero, zero)
    for chunk in range(4):
        carry = lax.fori_loop(0, 16, partial(step, chunk=chunk), carry)
    handed_ref[:CTX, :] = xs[:CTX, :].astype(bf16)
    for k, part in enumerate(split_three(carry[0]) + split_three(carry[1])):
        handed_ref[CTX + k * STATES : CTX + (k + 1) * STATES, :] = part


def project(flag_ref, tile_ref, weight_ref, qkv_ref):
    for half in range(2):
        qkv_ref[half] = mm(tile_ref[half], weight_ref[...]).astype(bf16)


def ssm_carry_in(
    flag_ref, local_ref, handed_ref, rate_ref, coef_ref, first_ref, second_ref, enter_ref, acc
):
    channels = rate_ref.shape[1] // 2
    for slot in range(2):
        to = slice(slot * channels, (slot + 1) * channels)
        source = slice((1 - slot) * channels, (2 - slot) * channels)
        first_ref[:, to] = handed_ref[:CTX, source]
        enter_ref[0, :, to] = join_three(handed_ref, CTX, source)
        enter_ref[1, :, to] = join_three(handed_ref, CTX + 3 * STATES, source)
    rate = rate_ref[...]
    decay = jnp.exp(-rate)
    coef = coef_ref[...]

    def step(eight, state):
        rows = []
        for k in range(8):
            rows.append(jnp.sum(coef * state, axis=0, keepdims=True))
            state = decay * state
        acc[aligned(eight * 8, 8), :] = jnp.concatenate(rows, axis=0)
        return state

    lax.fori_loop(0, 16, step, enter_ref[0] * jnp.exp(-129.0 * rate))
    second_ref[...] = (local_ref[...] + acc[...]).astype(bf16)


def ssm_signal_grad(
    flag_ref, near_ref, returned_ref, rate_ref, coef_ref, skip_ref, dqkv_ref, near_weight_ref,
    far_weight_ref, own_ref, send_ref, last_ref, rows_out, total,
):
    channels = rate_ref.shape[1] // 2
    adjoints = []
    for slot in range(2):
        to = slice(slot * channels, (slot + 1) * channels)
        source = slice((1 - slot) * channels, (2 - slot) * channels)
        last_ref[:, to] = returned_ref[:CTX, source].astype(f32)
        adjoints.append(join_three(returned_ref, CTX, source))
    decay = jnp.exp(-rate_ref[...])
    coef = coef_ref[...]
    skip = skip_ref[...]

    def step(j, adjoint, chunk):
        eight = 15 - j
        at = aligned(eight * 8, 8)
        if chunk % 2:
            g8 = (near_ref, last_ref)[chunk // 2][at, :]
        rows = [None] * 8
        for k in range(7, -1, -1):
            adjoint = decay * adjoint
            if chunk % 2:
                adjoint = adjoint + g8[k : k + 1]
            rows[k] = jnp.sum(coef * adjoint, axis=0, keepdims=True)
        y8 = jnp.concatenate(rows, axis=0)
        if chunk % 2:
            y8 = y8 + skip * g8
        rows_out[aligned((chunk * 16 + eight) * 8, 8), :] = y8
        return adjoint

    adjoint = jnp.concatenate(adjoints, axis=1)
    for chunk in (3, 2, 1, 0):
        adjoint = lax.fori_loop(0, 16, partial(step, chunk=chunk), adjoint)
    split = near_weight_ref.shape[1]
    for half in (1, 0):
        total[...] = mm(dqkv_ref[half, :, :split], near_weight_ref[...], NT) + mm(
            dqkv_ref[half, :, split:], far_weight_ref[...], NT
        )
        source = aligned(jnp.bitwise_xor(flag_ref[ODD], half) * HALF, HALF)
        for slot, name in enumerate((NEAR, FAR)):
            total[:, aligned(flag_ref[name] * channels, channels)] += rows_out[
                source, slot * channels : (slot + 1) * channels
            ]
        if half:
            send_ref[...] = total[...].astype(bf16)
        else:
            own_ref[...] = total[...]


def ssm_param_grad(
    flag_ref, tile_ref, near_ref, last_ref, enter_ref, rate_ref, coef_ref, out_ref, xs
):
    load_signal(flag_ref, tile_ref, xs)
    decay = jnp.exp(-rate_ref[...])
    zero = jnp.zeros_like(decay)

    def step(eight, carry, chunk):
        state, slope, for_coef, for_rate = carry
        x8 = xs[aligned((chunk * 16 + eight) * 8, 8), :]
        if chunk % 2:
            g8 = (near_ref, last_ref)[chunk // 2][aligned(eight * 8, 8), :]
        for k in range(8):
            slope = decay * (slope + state)
            state = decay * state + x8[k : k + 1]
            if chunk % 2:
                for_coef = for_coef + state * g8[k : k + 1]
                for_rate = for_rate + slope * g8[k : k + 1]
        return state, slope, for_coef, for_rate

    carry = (enter_ref[0], enter_ref[1], zero, zero)
    for chunk in range(4):
        carry = lax.fori_loop(0, 16, partial(step, chunk=chunk), carry)
    out_ref[:STATES, :] = -coef_ref[...] * carry[3]
    out_ref[STATES : 2 * STATES, :] = carry[2]
    skip = jnp.sum(xs[CTX : 2 * CTX] * near_ref[...], axis=0, keepdims=True) + jnp.sum(
        xs[3 * CTX :] * last_ref[...], axis=0, keepdims=True
    )
    out_ref[2 * STATES :, :] = jnp.concatenate(
        [skip, jnp.zeros((out_ref.shape[0] - 2 * STATES - 1, skip.shape[1]), f32)], axis=0
    )


def causal(scores):
    rows = lax.broadcasted_iota(jnp.int32, scores.shape, 0)
    cols = lax.broadcasted_iota(jnp.int32, scores.shape, 1)
    return jnp.where(cols <= rows, scores, masked_score)


def softmax_parts(parts):
    top = parts[0].max(axis=-1, keepdims=True)
    for part in parts[1:]:
        top = jnp.maximum(top, part.max(axis=-1, keepdims=True))
    weights = [jnp.exp(part - top) for part in parts]
    total = weights[0].sum(axis=-1, keepdims=True)
    for weight in weights[1:]:
        total = total + weight.sum(axis=-1, keepdims=True)
    return [weight / total for weight in weights]


def block_probs(q0, q1, k0, k1, first, second, whole, late):
    has_first = late > 0
    is_whole = whole > 0
    chosen = jnp.where(is_whole, first, second)
    chosen_ok = jnp.logical_or(jnp.logical_not(is_whole), has_first)
    s00 = causal(mm(q0, k0, NT) * score_scale)
    s0c = jnp.where(has_first, mm(q0, first, NT) * score_scale, masked_score)
    s11 = causal(mm(q1, k1, NT) * score_scale)
    s10 = jnp.where(is_whole, mm(q1, k0, NT) * score_scale, masked_score)
    s1c = jnp.where(chosen_ok, mm(q1, chosen, NT) * score_scale, masked_score)
    return softmax_parts([s00, s0c]), softmax_parts([s11, s10, s1c]), chosen


def head_parts(qkv_ref, head, half):
    channels = qkv_ref.shape[2] // 3
    return [
        qkv_ref[half, :, part * channels + head * HD : part * channels + (head + 1) * HD]
        for part in range(3)
    ]


def attention_forward(
    flag_ref, near_ref, far_ref, first_ref, second_ref, out_near_ref, out_far_ref, att_ref, own_ref,
    send_ref,
):
    half0 = flag_ref[ODD]
    half1 = 1 - half0
    heads = near_ref.shape[2] // (3 * HD)
    for index in range(2 * heads):
        qkv_ref = (near_ref, far_ref)[index // heads]
        q0, k0, v0 = head_parts(qkv_ref, index % heads, half0)
        q1, k1, v1 = head_parts(qkv_ref, index % heads, half1)
        at = slice(index * HD, (index + 1) * HD)
        first = first_ref[:, at]
        second = second_ref[:, at]
        (p00, p0c), (p11, p10, p1c), chosen = block_probs(
            q0, q1, k0, k1, first, second, flag_ref[WHOLE], flag_ref[LATE]
        )
        att_ref[half0, :, at] = (mm(p00.astype(bf16), v0) + mm(p0c.astype(bf16), first)).astype(
            bf16
        )
        att_ref[half1, :, at] = (
            mm(p11.astype(bf16), v1) + mm(p10.astype(bf16), v0) + mm(p1c.astype(bf16), chosen)
        ).astype(bf16)
    split = heads * HD

    def projected(half):
        return mm(att_ref[half, :, :split], out_near_ref[...]) + mm(
            att_ref[half, :, split:], out_far_ref[...], NT
        )

    send_ref[...] = projected(1).astype(bf16)
    own_ref[...] = projected(0)


def attended_grads(flag_ref, own_ref, other_ref, out_near_ref, out_far_ref, grad_ref, sent_ref):
    split = out_near_ref.shape[0]
    for half, ref in enumerate((own_ref, other_ref)):
        grad_ref[half, :, :split] = mm(ref[...], out_near_ref[...], NT).astype(bf16)
        grad_ref[half, :, split:] = mm(ref[...], out_far_ref[...]).astype(bf16)
        in_sent_order(flag_ref, ref, sent_ref.at[half])


def attention_backward(
    flag_ref, near_ref, far_ref, first_ref, second_ref, grad_ref, rate_ref, out_ref, second_out_ref,
    returned_ref,
):
    half0 = flag_ref[ODD]
    half1 = 1 - half0
    is_whole = flag_ref[WHOLE] > 0
    heads = near_ref.shape[2] // (3 * HD)
    for index in range(2 * heads):
        slot, head = index // heads, index % heads
        qkv_ref = (near_ref, far_ref)[slot]
        q0, k0, v0 = head_parts(qkv_ref, head, half0)
        q1, k1, v1 = head_parts(qkv_ref, head, half1)
        at = slice(index * HD, (index + 1) * HD)
        g0 = grad_ref[half0, :, at]
        g1 = grad_ref[half1, :, at]
        first = first_ref[:, at]
        second = second_ref[:, at]
        early, later, chosen = block_probs(
            q0, q1, k0, k1, first, second, flag_ref[WHOLE], flag_ref[LATE]
        )

        def score_grads(probs, rows, values):
            prob_grads = [mm(rows, v, NT) for v in values]
            centre = sum((p * d).sum(axis=-1, keepdims=True) for p, d in zip(probs, prob_grads))
            return [(p * (d - centre)).astype(bf16) for p, d in zip(probs, prob_grads)]

        d00, d0c = score_grads(early, g0, (v0, first))
        d11, d10, d1c = score_grads(later, g1, (v1, v0, chosen))
        p00, p0c = [p.astype(bf16) for p in early]
        p11, p10, p1c = [p.astype(bf16) for p in later]
        base = slot * 3 * heads * HD + head * HD
        for_q, for_k, for_v = [
            slice(base + part * heads * HD, base + part * heads * HD + HD) for part in range(3)
        ]
        out_ref[half0, :, for_q] = ((mm(d00, k0) + mm(d0c, first)) * score_scale).astype(bf16)
        out_ref[half1, :, for_q] = (
            (mm(d11, k1) + mm(d10, k0) + mm(d1c, chosen)) * score_scale
        ).astype(bf16)
        out_ref[half0, :, for_k] = ((mm(d00, q0, TN) + mm(d10, q1, TN)) * score_scale).astype(bf16)
        out_ref[half1, :, for_k] = (mm(d11, q1, TN) * score_scale).astype(bf16)
        out_ref[half0, :, for_v] = (mm(p00, g0, TN) + mm(p10, g1, TN)).astype(bf16)
        out_ref[half1, :, for_v] = mm(p11, g1, TN).astype(bf16)
        from_early = mm(d0c, q0, TN) * score_scale + mm(p0c, g0, TN)
        from_later = mm(d1c, q1, TN) * score_scale + mm(p1c, g1, TN)
        returned_ref[:CTX, at] = (from_early + jnp.where(is_whole, from_later, 0.0)).astype(bf16)
        second_out_ref[:, at] = jnp.where(is_whole, 0.0, from_later)

    rate = rate_ref[...]
    decay = jnp.exp(-rate)

    def step(j, adjoint):
        g8 = second_out_ref[aligned((15 - j) * 8, 8), :]
        for k in range(7, -1, -1):
            adjoint = decay * adjoint + g8[k : k + 1]
        return adjoint

    adjoint = lax.fori_loop(0, 16, step, jnp.zeros_like(rate)) * jnp.exp(-float(CTX) * rate)
    for k, part in enumerate(split_three(adjoint)):
        returned_ref[CTX + k * STATES : CTX + (k + 1) * STATES, :] = part


def flat(ref):
    if len(ref.shape) == 2:
        return ref[...]
    part = ref[:, 0]
    return part.reshape(part.shape[0] * part.shape[1], part.shape[2])


def feed_forward(
    flag_ref, n_ref, c_ref, up0_ref, down0_ref, up1_ref, down1_ref, act_ref, gate_ref, sent_ref,
    down_out_ref, back_out_ref, acc_down, acc_back,
):
    step = pl.program_id(0)
    steps = pl.num_programs(0)
    per = steps // 2

    @pl.when(step == 0)
    def _():
        acc_down[...] = jnp.zeros_like(acc_down)
        acc_back[...] = jnp.zeros_like(acc_back)
        in_sent_order(flag_ref, n_ref, sent_ref)

    def body(up, down, slot):
        gate = mm(n_ref[...], up)
        cdf = 0.5 * (1.0 + lax.erf(gate * (1.0 / math.sqrt(2.0))))
        act = (gate * cdf).astype(bf16)
        slope = cdf + gate * jnp.exp(-0.5 * gate * gate) * (1.0 / math.sqrt(2.0 * math.pi))
        grad = (mm(c_ref[...], down, NT) * slope).astype(bf16)
        gate_ref[...] = grad
        hidden = act_ref.shape[1] // 2
        width = hidden // GROUP
        count = act.shape[1] // width
        for k in range(count):
            mask = jnp.bitwise_xor(flag_ref[PLACE], (step - slot * per) * count + k)
            to = (1 - mask % 2) * 4 + (mask // 2 % 2) * 2 + mask // 4
            act_ref[:, aligned(slot * hidden + to * width, width)] = act[
                :, k * width : (k + 1) * width
            ]
        acc_down[...] += mm(act, down)
        acc_back[...] += mm(grad, up, NT)

    @pl.when(step < per)
    def _():
        body(up0_ref[...], down0_ref[...], 0)

    @pl.when(step >= per)
    def _():
        body(flat(up1_ref), flat(down1_ref), 1)

    @pl.when(step == steps - 1)
    def _():
        down_out_ref[...] = acc_down[...].astype(down_out_ref.dtype)
        back_out_ref[...] = acc_back[...].astype(back_out_ref.dtype)


def run_feed_forward(flags, rows, cot, up, down, far, kind):
    tokens, width = rows.shape
    block = 512
    hidden = up.shape[1]
    per = hidden // block
    slices, slice_rows = far.shape[0], far.shape[2]

    def near_at(j):
        return jnp.minimum(j, per - 1)

    def far_at(j):
        return jnp.maximum(j - per, 0)

    whole = pl.BlockSpec((tokens, width), lambda j: (0, 0))
    return pl.pallas_call(
        feed_forward,
        grid=(2 * per,),
        out_shape=(
            shape((tokens, 2 * hidden), bf16),
            shape((tokens, 2 * hidden), bf16),
            shape((tokens, width), bf16),
            shape((tokens, width), kind),
            shape((tokens, width), kind),
        ),
        in_specs=[
            pl.BlockSpec(memory_space=pltpu.SMEM),
            whole,
            whole,
            pl.BlockSpec((width, block), lambda j: (0, near_at(j))),
            pl.BlockSpec((block, width), lambda j: (near_at(j), 0)),
            pl.BlockSpec((slices, 1, slice_rows, block), lambda j: (0, 0, 0, far_at(j))),
            pl.BlockSpec((slices // per, 1, slice_rows, width), lambda j: (far_at(j), 1, 0, 0)),
        ],
        out_specs=(
            pl.BlockSpec((tokens, 2 * hidden), lambda j: (0, 0)),
            pl.BlockSpec((tokens, block), lambda j: (0, j)),
            whole,
            whole,
            whole,
        ),
        scratch_shapes=[pltpu.VMEM((tokens, width), f32), pltpu.VMEM((tokens, width), f32)],
        compiler_params=pltpu.CompilerParams(
            vmem_limit_bytes=24 * 1024 * 1024, dimension_semantics=("arbitrary",)
        ),
        cost_estimate=pl.CostEstimate(flops=0, bytes_accessed=0, transcendentals=0),
    )(flags, rows, cot, up, down, far, far)


def products(lhs_refs, rhs_refs, columns, split=None):
    total = None
    for lhs_ref, rhs_ref in zip(lhs_refs, rhs_refs):
        term = mm(lhs_ref[:, columns], rhs_ref[...], TN)
        total = term if total is None else total + term
    return total


def down_pass(flag_ref, act0, act1, cot0, cot1, out_ref):
    hidden = act0.shape[1] // 2
    part = hidden // 4
    for slot in range(2):
        value = products(
            (act0, act1), (cot0, cot1), slice(slot * hidden, slot * hidden + hidden // 2)
        ).astype(bf16)
        out_ref[slot * part : (slot + 1) * part, :] = value[part:]
        out_ref[(2 + slot) * part : (3 + slot) * part, :] = value[:part]


def down_keep(flag_ref, act0, act1, cot0, cot1, core_ref, send_ref, left_ref):
    hidden = act0.shape[1] // 2
    part = hidden // 4
    for slot in range(2):
        value = products(
            (act0, act1), (cot0, cot1), slice(slot * hidden + hidden // 2, (slot + 1) * hidden)
        )
        to = slice(slot * part, (slot + 1) * part)
        send_ref[to, :] = (value[part:] + core_ref[to, :].astype(f32)).astype(bf16)
        left_ref[to, :] = value[:part] + core_ref[2 * part + to.start : 2 * part + to.stop, :].astype(
            f32
        )


def down_step(flag_ref, left_ref, received_ref, own_ref, send_ref):
    rows = own_ref.shape[0] // 2
    for slot in range(2):
        to = slice(slot * rows, (slot + 1) * rows)
        own = slice(2 * slot * rows, (2 * slot + 1) * rows)
        send = slice((2 * slot + 1) * rows, (2 * slot + 2) * rows)
        own_ref[to, :] = left_ref[own, :] + received_ref[own, :].astype(f32)
        send_ref[to, :] = (left_ref[send, :] + received_ref[send, :].astype(f32)).astype(bf16)


def y_first(value, rows):
    parts = [value[k * rows : (k + 1) * rows] for k in (1, 3, 0, 2)]
    return jnp.concatenate(parts[:2], 0), jnp.concatenate(parts[2:], 0)


def rows_pass(flag_ref, lhs0, lhs1, rhs0, rhs1, out_ref):
    half = lhs0.shape[1] // 2
    value = products((lhs0, lhs1), (rhs0, rhs1), slice(0, half)).astype(bf16)
    send, left = y_first(value, half // 4)
    out_ref[: half // 2, :] = send
    out_ref[half // 2 :, :] = left


def rows_keep(flag_ref, lhs0, lhs1, rhs0, rhs1, core_ref, send_ref, left_ref):
    half = lhs0.shape[1] // 2
    value = products((lhs0, lhs1), (rhs0, rhs1), slice(half, 2 * half))
    send, left = y_first(value, half // 4)
    send_ref[...] = (send + core_ref[: half // 2, :].astype(f32)).astype(bf16)
    left_ref[...] = left + core_ref[half // 2 :, :].astype(f32)


def rows_step(
    flag_ref, up_left, out_left, up_received, out_received, up_own, out_own, send_ref
):
    rows = up_own.shape[0]
    at = 0
    for left, received, own in ((up_left, up_received, up_own), (out_left, out_received, out_own)):
        own[...] = left[:rows, :] + received[:rows, :].astype(f32)
        width = own.shape[1]
        send_ref[:, at : at + width] = (left[rows:, :] + received[rows:, :].astype(f32)).astype(bf16)
        at += width


def own_slices(
    flag_ref, down_own, down_received, up_own, out_own, rows_received, near_ref, far_ref
):
    rows, hidden, channels = up_own.shape[0], up_own.shape[1] // 2, out_own.shape[1] // 2
    down = down_own[...] + down_received[...].astype(f32)
    up = up_own[...] + rows_received[:, : 2 * hidden].astype(f32)
    out = out_own[...] + rows_received[:, 2 * hidden :].astype(f32)
    width = down.shape[1]
    for slot, ref in enumerate((near_ref, far_ref)):
        ref[:, :width] = down[slot * rows : (slot + 1) * rows].astype(ref.dtype)
        ref[:, width : width + hidden] = up[:, slot * hidden : (slot + 1) * hidden].astype(ref.dtype)
        ref[:, width + hidden :] = out[:, slot * channels : (slot + 1) * channels].astype(ref.dtype)


def attn_pass(flag_ref, lhs0, lhs1, rhs0, rhs1, out_ref):
    half = lhs0.shape[1] // 2
    out_ref[...] = products((lhs0, lhs1), (rhs0, rhs1), slice(0, half)).astype(bf16)


def attn_keep(flag_ref, lhs0, lhs1, rhs0, rhs1, core_ref, own_ref, *send_refs):
    half = lhs0.shape[1] // 2
    rows = half // 4
    value = products((lhs0, lhs1), (rhs0, rhs1), slice(half, 2 * half)) + core_ref[...].astype(f32)
    own_ref[...] = value[:rows]
    for k, ref in enumerate(send_refs):
        ref[...] = value[(k + 1) * rows : (k + 2) * rows].astype(bf16)


def attn_own(flag_ref, own_ref, r1_ref, r2_ref, r3_ref, near_ref, far_ref):
    total = own_ref[...] + (
        r1_ref[...].astype(f32) + r2_ref[...].astype(f32) + r3_ref[...].astype(f32)
    )
    width = near_ref.shape[1]
    near_ref[...] = total[:, :width]
    far_ref[...] = total[:, width:].astype(bf16)


def add_two(flag_ref, a_ref, b_ref, out_ref):
    out_ref[...] = (a_ref[...].astype(f32) + b_ref[...].astype(f32)).astype(out_ref.dtype)


def add_three(flag_ref, a_ref, b_ref, c_ref, out_ref):
    out_ref[...] = (a_ref[...] + b_ref[...] + c_ref[...].astype(f32)).astype(out_ref.dtype)


def pack_small(flag_ref, param_ref, gains_ref, received_ref, near_ref, far_ref):
    gains = gains_ref[...] + received_ref[...]
    width = gains.shape[1]
    rows = param_ref.shape[0]
    for slot, ref in enumerate((near_ref, far_ref)):
        ref[:rows, :] = param_ref[:, slot * width : (slot + 1) * width]
        ref[rows:, :] = gains


def widen(flag_ref, all_ref, down_ref, up_ref, out_ref):
    down, up = down_ref.shape[1], up_ref.shape[1]
    down_ref[...] = all_ref[:, :down].astype(f32)
    up_ref[...] = all_ref[:, down : down + up].astype(f32)
    out_ref[...] = all_ref[:, down + up :].astype(f32).T


def sources(flag_ref, even_ref, odd_ref):
    for pair in range(GROUP // 2):
        for side, ref in enumerate((even_ref, odd_ref)):
            source = jnp.bitwise_xor(flag_ref[PLACE], 2 * pair + side)
            yield ref, pair, aligned(source * even_ref.shape[1], even_ref.shape[1])


def assemble_weight(flag_ref, even_ref, odd_ref, tile_ref, weight_ref, out_ref, qkv_ref):
    split = weight_ref.shape[1]
    for ref, pair, at in sources(flag_ref, even_ref, odd_ref):
        weight_ref[at, :] = ref[pair, :, :split]
        out_ref[at, :] = ref[pair, :, split:]
    project(flag_ref, tile_ref, weight_ref, qkv_ref)


def assemble_grad(flag_ref, even_ref, odd_ref, qkv_ref):
    channels = qkv_ref.shape[2]
    for ref, pair, at in sources(flag_ref, even_ref, odd_ref):
        for part in range(3):
            qkv_ref[part, at, :] = ref[pair, :, part * channels : (part + 1) * channels].astype(f32)


class Order:
    def __init__(self):
        self.last = ()

    def __call__(self, *values):
        tied = lax.optimization_barrier((values, self.last))[0]
        return tied[0] if len(tied) == 1 else tied

    def done(self, result):
        self.last = result
        return result


def per_device(
    inputs,
    block_size,
    gain_attn,
    qkv_weight,
    ssm_rate,
    ssm_coef,
    ssm_skip,
    out_weight,
    gain_mlp,
    up_weight,
    down_weight,
    cotangent,
    dp_size,
):
    z = lax.axis_index("mp")
    place = jnp.bitwise_and(lax.axis_index("dp"), GROUP - 1)
    groups = [[g * GROUP + k for k in range(GROUP)] for g in range(dp_size // GROUP)]
    groups = groups if len(groups) > 1 else None

    def swap_mp(value, mask):
        return lax.ppermute(value, "mp", [(k, k ^ mask) for k in range(4)])

    def swap_dp(value, mask):
        return lax.ppermute(value, "dp", [(k, k ^ mask) for k in range(dp_size)])

    def gather(value):
        return lax.all_gather(value, "dp", axis=0, tiled=True, axis_index_groups=groups)

    def gather_by_xor(piece):
        return [piece] + [swap_dp(piece, 2 * k) for k in range(1, GROUP // 2)]

    def over_groups(own):
        mask = GROUP
        while mask < dp_size:
            own = own + swap_dp(own.astype(bf16), mask).astype(f32)
            mask *= 2
        return own.astype(bf16)

    model_dim = inputs.shape[2]
    channels = qkv_weight.shape[2]
    hidden = up_weight.shape[1]
    wide = 2 * channels
    rows = model_dim // GROUP
    row = inputs[0]
    cot = cotangent[0]
    z_far = jnp.bitwise_xor(z, 2)
    whole = (block_size[0] > HALF).astype(jnp.int32)
    flags = jnp.stack(
        [whole, jnp.right_shift(z, 1), jnp.bitwise_and(z, 1), z, z_far, place]
    ).astype(jnp.int32)
    gain_one = gain_attn[None]
    gain_two = gain_mlp[None]
    order = Order()
    half = shape((HALF, model_dim))
    half_low = shape((HALF, model_dim), bf16)

    normed_one = order.done(call(norm_one, half_low)(flags, row, gain_one))
    paired_one = swap_mp(normed_one, 1)
    qkv_parts = jnp.transpose(qkv_weight, (1, 0, 2))
    attn_slice, mlp_slice = order.done(
        run_cut_slices(flags, order(qkv_parts), out_weight, up_weight, down_weight)
    )
    attn_across = swap_mp(attn_slice, 2)
    ssm_pack = jnp.concatenate(
        [ssm_rate.T, ssm_coef.T, ssm_skip[None], jnp.zeros((7, channels), f32)], 0
    )
    ssm_both = jnp.concatenate([ssm_pack, swap_mp(ssm_pack, 2)], 1)
    rate_t, coef_t, skip_t = ssm_both[:16], ssm_both[16:32], ssm_both[32:33]
    near_qkv = order.done(jnp.concatenate(list(order(*[qkv_parts[k] for k in range(3)])), 1))

    paired_one, attn_across = order.done(order(paired_one, attn_across))
    attn_pieces = gather_by_xor(attn_across)
    mlp_across = swap_mp(order(mlp_slice), 2)
    tile_one, one_sent, second_local, handed = order.done(
        call(
            ssm_forward,
            (
                shape((2, HALF, model_dim), bf16),
                shape((2, HALF, model_dim), bf16),
                shape((CTX, wide)),
                shape((CTX + 6 * STATES, wide), bf16),
            ),
            scratch=[pltpu.VMEM((2 * HALF, wide), f32)],
        )(flags, normed_one, order(paired_one), rate_t, coef_t, skip_t)
    )
    handed = lax.ppermute(handed, "mp", [(0, 2), (1, 3)])

    qkv_shape = shape((2, HALF, 3 * channels), bf16)
    qkv_near = order.done(call(project, qkv_shape)(flags, order(tile_one), near_qkv))
    even = order.done(jnp.stack(list(order(*attn_pieces))))
    odd_part = swap_dp(even, 1)
    far_qkv, far_out, qkv_far = order.done(
        call(
            assemble_weight,
            (
                shape((model_dim, 3 * channels), bf16),
                shape((model_dim, channels), bf16),
                qkv_shape,
            ),
        )(flags, even, order(odd_part), tile_one)
    )
    ctx_first, ctx_second, enter_state = order.done(
        call(
            ssm_carry_in,
            (shape((CTX, wide), bf16), shape((CTX, wide), bf16), shape((2, STATES, wide))),
            scratch=[pltpu.VMEM((CTX, wide), f32)],
        )(flags, second_local, order(handed), rate_t, coef_t)
    )
    mlp_far = gather(order(mlp_across)).reshape(GROUP, 2, rows, model_dim)
    paired_cot = swap_mp(order(cot), 1)
    attended, out_own, out_send = order.done(
        call(attention_forward, (shape((2, HALF, wide), bf16), half, half_low))(
            flags, order(qkv_near), qkv_far, ctx_first, ctx_second, out_weight, far_out
        )
    )
    out_received = swap_mp(out_send, 1)
    paired_cot = order.done(order(paired_cot))
    middle, normed_two = order.done(
        call(norm_two, (half, half_low))(flags, row, out_own, order(out_received), gain_two)
    )

    paired_two = swap_mp(normed_two, 1)
    mlp = (up_weight, down_weight, mlp_far)
    act_own, gate_own, two_own, down_own, back_own = order.done(
        run_feed_forward(flags, order(normed_two), cot, *mlp, f32)
    )
    act_other, gate_other, two_other, down_send, back_send = order.done(
        run_feed_forward(flags, order(paired_two), paired_cot, *mlp, bf16)
    )
    back_received = swap_mp(back_send, 1)

    def low(*dims):
        return shape(dims, bf16)

    side = model_dim // 2
    acts = (act_own, act_other, cot, paired_cot)
    passed = order.done(call(down_pass, low(hidden, model_dim))(flags, order(act_own), *acts[1:]))
    down_core = swap_dp(passed, 1)
    middle_grad, attn_grad, gain_mlp_grad = order.done(
        call(norm_two_back, (half, half_low, shape((1, model_dim))))(
            flags, middle, back_own, order(back_received), cot, gain_two
        )
    )
    paired_back = swap_mp(attn_grad, 1)
    passed = order.done(
        call(rows_pass, low(side, 2 * hidden))(
            flags, order(two_own), two_other, gate_own, gate_other
        )
    )
    up_core = swap_dp(passed, 1)
    down_send_x, down_left = order.done(
        call(down_keep, (low(side, model_dim), shape((side, model_dim))))(
            flags, *acts, order(down_core)
        )
    )
    down_x = swap_dp(down_send_x, 2)
    up_send_y, up_left = order.done(
        call(rows_keep, (low(side // 2, 2 * hidden), shape((side // 2, 2 * hidden))))(
            flags, two_own, two_other, gate_own, gate_other, order(up_core)
        )
    )
    up_y = swap_dp(up_send_y, 4)

    att_grad, back_sent = order.done(
        call(
            attended_grads,
            (shape((2, HALF, wide), bf16), shape((2, HALF, model_dim), bf16)),
        )(flags, attn_grad, order(paired_back), out_weight, far_out)
    )
    down_received = swap_mp(order(down_send), 1)
    outs = (back_sent[0], back_sent[1], attended[0], attended[1])
    passed = order.done(call(rows_pass, low(side, wide))(flags, *outs))
    out_core = swap_dp(passed, 1)
    dqkv, second_grad, returned = order.done(
        call(
            attention_backward,
            (
                shape((2, HALF, 6 * channels), bf16),
                shape((CTX, wide)),
                shape((CTX + 3 * STATES, wide), bf16),
            ),
        )(flags, qkv_near, qkv_far, ctx_first, ctx_second, order(att_grad), rate_t)
    )
    returned = lax.ppermute(returned, "mp", [(2, 0), (3, 1)])
    out_send_y, out_left = order.done(
        call(rows_keep, (low(side // 2, wide), shape((side // 2, wide))))(
            flags, *outs, order(out_core)
        )
    )
    out_y = swap_dp(out_send_y, 4)
    ones = (one_sent[0], one_sent[1], dqkv[0], dqkv[1])
    passed = order.done(call(attn_pass, low(side, 6 * channels))(flags, order(ones[0]), *ones[1:]))
    attn_core = swap_dp(passed, 1)
    down_mine, down_send_y = order.done(
        call(down_step, (shape((2 * rows, model_dim)), low(2 * rows, model_dim)))(
            flags, down_left, order(down_x)
        )
    )
    down_y = swap_dp(down_send_y, 4)
    one_own, one_send, last_grad = order.done(
        call(
            ssm_signal_grad,
            (half, half_low, shape((CTX, wide))),
            scratch=[pltpu.VMEM((2 * HALF, wide), f32), pltpu.VMEM((HALF, model_dim), f32)],
        )(
            flags, second_grad, order(returned), rate_t, coef_t, skip_t, dqkv, near_qkv, far_qkv
        )
    )
    one_received = swap_mp(one_send, 1)
    up_mine, out_mine, rows_send_x = order.done(
        call(
            rows_step,
            (shape((rows, 2 * hidden)), shape((rows, wide)), low(rows, 2 * hidden + wide)),
        )(flags, up_left, out_left, *order(up_y, out_y))
    )
    rows_x = swap_dp(rows_send_x, 2)
    attn_mine, *attn_sends = order.done(
        call(attn_keep, (shape((rows, 6 * channels)),) + (low(rows, 6 * channels),) * 3)(
            flags, *ones, order(attn_core)
        )
    )
    attn_sent = [swap_dp(part, SENT[5 + k]) for k, part in enumerate(attn_sends)]
    param_grad = order.done(
        call(
            ssm_param_grad,
            shape((40, wide)),
            scratch=[pltpu.VMEM((2 * HALF, wide), f32)],
        )(flags, order(tile_one), second_grad, last_grad, enter_state, rate_t, coef_t)
    )
    input_grad, gains = order.done(
        call(norm_one_back, (half, shape((2 * model_dim // channels, channels))))(
            flags, row, one_own, order(one_received), middle_grad, gain_one, gain_mlp_grad
        )
    )
    mlp_width = model_dim + hidden + channels
    mlp_near, mlp_send = order.done(
        call(own_slices, (shape((rows, mlp_width)), low(rows, mlp_width)))(
            flags, down_mine, order(down_y), up_mine, out_mine, order(rows_x)
        )
    )
    mlp_received = swap_mp(mlp_send, 2)
    attn_near, attn_send = order.done(
        call(attn_own, (shape((rows, 3 * channels)), low(rows, 3 * channels)))(
            flags, attn_mine, *order(*attn_sent)
        )
    )
    attn_received = swap_mp(attn_send, 2)
    gains_received = swap_mp(order(gains), 1)
    output = order.done(
        call(add_three, half_low)(flags, middle, down_own, order(down_received))
    )
    attn_slice_grad = order.done(
        call(add_two, low(rows, 3 * channels))(flags, attn_near, order(attn_received))
    )
    attn_pieces = gather_by_xor(over_groups(attn_slice_grad))
    mlp_slice_grad = order.done(
        call(add_two, low(rows, mlp_width))(flags, mlp_near, order(mlp_received))
    )
    mlp_full = gather(over_groups(mlp_slice_grad))
    small = shape((48, channels))
    packed, packed_far = order.done(
        call(pack_small, (small, small))(flags, param_grad, gains, order(gains_received))
    )
    packed = order.done(call(add_two, small)(flags, packed, order(swap_mp(packed_far, 2))))
    packed = order.done(call(add_two, small)(flags, packed, order(swap_dp(packed, 1))))
    even = order.done(jnp.stack(list(order(*attn_pieces))))
    odd_part = swap_dp(even, 1)
    mask = 2
    while mask < dp_size:
        packed = order.done(call(add_two, small)(flags, packed, order(swap_dp(packed, mask))))
        mask *= 2
    qkv_grad = order.done(
        call(assemble_grad, shape((3, model_dim, channels)))(flags, even, order(odd_part))
    )
    down_grad, up_grad, out_grad = call(
        widen, (shape(down_weight.shape), shape(up_weight.shape), shape(out_weight.shape))
    )(flags, order(mlp_full))
    gains = packed[40:].reshape(2, model_dim)
    return (
        output[None],
        input_grad[None],
        gains[0],
        jnp.transpose(qkv_grad, (1, 0, 2)),
        packed[:16].T,
        packed[16:32].T,
        packed[32],
        out_grad,
        gains[1],
        up_grad,
        down_grad,
    )


def solution(mesh):
    return jax.shard_map(
        partial(per_device, dp_size=mesh.shape["dp"]),
        mesh=mesh,
        in_specs=(
            P("dp", "mp", None),
            P("dp"),
            P(),
            P(None, None, "mp"),
            P("mp", None),
            P("mp", None),
            P("mp"),
            P("mp", None),
            P(),
            P(None, "mp"),
            P("mp", None),
            P("dp", "mp", None),
        ),
        out_specs=(
            P("dp", "mp", None),
            P("dp", "mp", None),
            P(),
            P(None, None, "mp"),
            P("mp", None),
            P("mp", None),
            P("mp"),
            P("mp", None),
            P(),
            P(None, "mp"),
            P("mp", None),
        ),
        check_vma=False,
    )
```

```python
from functools import partial
import math

import jax
import jax.numpy as jnp
from jax import lax
from jax.experimental import pallas as pl
from jax.experimental.pallas import tpu as pltpu
from jax.sharding import PartitionSpec as P

HD = 128
CTX = 128
HALF = 256
STATES = 16
GROUP = 8

f32 = jnp.float32
bf16 = jnp.bfloat16
epsilon = 1e-05
masked_score = -1e30
score_scale = 1.0 / math.sqrt(HD)
VMEM_LIMIT = 16 * 1024 * 1024

NT = (((1,), (1,)), ((), ()))
TN = (((0,), (0,)), ((), ()))
NN = (((1,), (0,)), ((), ()))

WHOLE, LATE, ODD, NEAR, FAR, PLACE = range(6)


def mm(a, b, dims=NN):
    return lax.dot_general(a, b, dims, preferred_element_type=f32)


def shape(dims, dtype=f32):
    return jax.ShapeDtypeStruct(dims, dtype)


def length(micros):
    return pl.CostEstimate(flops=int(micros * 1e9), bytes_accessed=0, transcendentals=0)


def call(kernel, out_shape, scratch=(), micros=0):
    def run(flags, *args):
        vmem = pl.BlockSpec(memory_space=pltpu.VMEM)
        return pl.pallas_call(
            kernel,
            out_shape=out_shape,
            in_specs=[pl.BlockSpec(memory_space=pltpu.SMEM)] + [vmem] * len(args),
            out_specs=jax.tree.map(lambda _: vmem, out_shape),
            scratch_shapes=scratch,
            compiler_params=pltpu.CompilerParams(vmem_limit_bytes=VMEM_LIMIT),
            cost_estimate=length(micros),
        )(flags, *args)

    return run


SENT = (1, 5, 3, 7, 0, 4, 2, 6)


def in_sent_order(flag_ref, value_ref, out_ref, masks=SENT):
    width = value_ref.shape[1] // GROUP
    for k, mask in enumerate(masks):
        source = jnp.bitwise_xor(flag_ref[PLACE], mask)
        out_ref[:, k * width : (k + 1) * width] = value_ref[:, aligned(source * width, width)]


def aligned(start, size):
    return pl.ds(pl.multiple_of(start, size), size)


def cut_slices(
    flag_ref, qkv_ref, out_ref, up_ref, down_ref, ssm_ref, attn_ref, mlp_ref, out_slice, *sems
):
    rows = mlp_ref.shape[0] // 2
    channels = out_slice.shape[0]
    count = ssm_ref.shape[0]
    for k, part in enumerate(split_three(ssm_ref[...])):
        attn_ref[rows : rows + count, k * channels : (k + 1) * channels] = part
    attn_ref[rows : rows + count, 3 * channels :] = jnp.zeros((count, channels), bf16)
    at = aligned(flag_ref[PLACE] * rows, rows)
    copies = [
        pltpu.make_async_copy(
            qkv_ref.at[part, at, :],
            attn_ref.at[:rows, part * channels : (part + 1) * channels],
            sems[part],
        )
        for part in range(3)
    ] + [
        pltpu.make_async_copy(out_ref.at[:, at], out_slice, sems[3]),
        pltpu.make_async_copy(up_ref.at[at, :], mlp_ref.at[:rows, :], sems[4]),
        pltpu.make_async_copy(down_ref.at[at, :], mlp_ref.at[rows:, :], sems[5]),
    ]
    for copy in copies:
        copy.start()
    for copy in copies:
        copy.wait()
    attn_ref[:rows, 3 * channels :] = out_slice[...].T


def join_ssm(flag_ref, own_ref, across_ref, out_ref):
    channels = own_ref.shape[1]
    start = across_ref.shape[0] - own_ref.shape[0]
    out_ref[:, :channels] = own_ref[...]
    parts = [across_ref[start:, k * channels : (k + 1) * channels].astype(f32) for k in range(3)]
    out_ref[:, channels:] = (parts[0] + parts[1]) + parts[2]


def run_cut_slices(flags, qkv_parts, out_weight, up_weight, down_weight, ssm_pack):
    channels = qkv_parts.shape[2]
    width = out_weight.shape[1]
    rows = width // GROUP
    vmem = pl.BlockSpec(memory_space=pltpu.VMEM)
    return pl.pallas_call(
        cut_slices,
        in_specs=[pl.BlockSpec(memory_space=pltpu.SMEM)]
        + [pl.BlockSpec(memory_space=pltpu.HBM)] * 4
        + [vmem],
        out_specs=(vmem, vmem),
        out_shape=(
            shape((rows + ssm_pack.shape[0], 4 * channels), bf16),
            shape((2 * rows, width), bf16),
        ),
        scratch_shapes=[pltpu.VMEM((channels, rows), bf16)] + [pltpu.SemaphoreType.DMA] * 6,
        compiler_params=pltpu.CompilerParams(vmem_limit_bytes=56 * 1024 * 1024),
        cost_estimate=length(0),
    )(flags, qkv_parts, out_weight, up_weight, down_weight, ssm_pack)


def normalise(values):
    mean = jnp.mean(values, axis=-1, keepdims=True)
    centred = values - mean
    spread = jnp.mean(centred * centred, axis=-1, keepdims=True)
    inverse = lax.rsqrt(spread + epsilon)
    return centred * inverse, inverse


def normalise_back(grad, gain, hat, inverse):
    inner = grad * gain
    return (
        inner
        - jnp.mean(inner, axis=-1, keepdims=True)
        - hat * jnp.mean(inner * hat, axis=-1, keepdims=True)
    ) * inverse


def by_rows(body, rows, block=64):
    for k in range(rows // block):
        body(slice(k * block, (k + 1) * block))


def norm_one(flag_ref, x_ref, gain_ref, out_ref):
    def body(at):
        hat, _ = normalise(x_ref[at, :].astype(f32))
        out_ref[at, :] = (hat * gain_ref[...]).astype(bf16)

    by_rows(body, x_ref.shape[0])


def touch(flag_ref, up_ref, down_ref, cot_ref, paired_ref, out_ref):
    out_ref[...] = (
        up_ref[:8, :128] + down_ref[:8, :128] + (cot_ref[:8, :128] + paired_ref[:8, :128])
    )


def norm_two(flag_ref, x_ref, own_ref, received_ref, gain_ref, middle_ref, out_ref):
    def body(at):
        middle = x_ref[at, :].astype(f32) + own_ref[at, :] + received_ref[at, :].astype(f32)
        middle_ref[at, :] = middle
        hat, _ = normalise(middle)
        out_ref[at, :] = (hat * gain_ref[...]).astype(bf16)

    by_rows(body, x_ref.shape[0])


def norm_two_back(
    flag_ref, middle_ref, own_ref, received_ref, cot_ref, gain_ref, warm_ref, grad_ref, low_ref,
    gain_out_ref,
):
    sums = []

    def body(at):
        hat, inverse = normalise(middle_ref[at, :])
        grad = own_ref[at, :] + received_ref[at, :].astype(f32)
        sums.append(jnp.sum(grad * hat, axis=0, keepdims=True))
        total = cot_ref[at, :].astype(f32) + normalise_back(grad, gain_ref[...], hat, inverse)
        grad_ref[at, :] = total
        low_ref[at, :] = total.astype(bf16)

    by_rows(body, middle_ref.shape[0])
    gain_out_ref[...] = sum(sums)


def norm_one_back(
    flag_ref, x_ref, own_ref, received_ref, middle_ref, gain_ref, gain_two_grad_ref, grad_ref,
    gain_out_ref,
):
    sums = []

    def body(at):
        hat, inverse = normalise(x_ref[at, :].astype(f32))
        grad = own_ref[at, :] + received_ref[at, :].astype(f32)
        sums.append(jnp.sum(grad * hat, axis=0, keepdims=True))
        grad_ref[at, :] = middle_ref[at, :] + normalise_back(grad, gain_ref[...], hat, inverse)

    by_rows(body, x_ref.shape[0])
    width = gain_out_ref.shape[1]
    pieces = x_ref.shape[1] // width
    for which, value in enumerate((sum(sums), gain_two_grad_ref[...])):
        for k in range(pieces):
            row = which * pieces + k
            gain_out_ref[row : row + 1, :] = value[:, k * width : (k + 1) * width]


def split_three(value):
    high = value.astype(bf16)
    rest = value - high.astype(f32)
    middle = rest.astype(bf16)
    return [high, middle, (rest - middle.astype(f32)).astype(bf16)]


def join_three(ref, start, lanes):
    parts = [ref[start + k * STATES : start + (k + 1) * STATES, lanes] for k in range(3)]
    return (parts[0].astype(f32) + parts[1].astype(f32)) + parts[2].astype(f32)


def load_signal(flag_ref, tile_ref, xs):
    channels = xs.shape[1] // 2
    for half in range(2):
        source = jnp.bitwise_xor(flag_ref[ODD], half)
        for slot, name in enumerate((NEAR, FAR)):
            xs[half * HALF : (half + 1) * HALF, slot * channels : (slot + 1) * channels] = tile_ref[
                source, :, aligned(flag_ref[name] * channels, channels)
            ].astype(f32)


def ssm_forward(
    flag_ref, own_ref, other_ref, rate_ref, coef_ref, skip_ref, tile_ref, sent_ref,
    second_ref, handed_ref, xs,
):
    tile_ref[0] = own_ref[...]
    tile_ref[1] = other_ref[...]
    in_sent_order(flag_ref, own_ref, sent_ref.at[0])
    in_sent_order(flag_ref, other_ref, sent_ref.at[1])
    load_signal(flag_ref, tile_ref, xs)
    decay = jnp.exp(-rate_ref[...])
    coef = coef_ref[...]
    skip = skip_ref[...]
    zero = jnp.zeros_like(decay)

    def step(eight, carry, chunk):
        state, slope = carry
        x8 = xs[aligned((chunk * 16 + eight) * 8, 8), :]
        rows = []
        for k in range(8):
            slope = decay * (slope + state)
            state = decay * state + x8[k : k + 1]
            if chunk % 2:
                rows.append(jnp.sum(coef * state, axis=0, keepdims=True))
        if chunk % 2:
            y8 = jnp.concatenate(rows, axis=0) + skip * x8
            at = aligned(eight * 8, 8)
            if chunk == 1:
                second_ref[at, :] = y8
            else:
                xs[at, :] = y8
        return state, slope

    carry = (zero, zero)
    for chunk in range(4):
        carry = lax.fori_loop(0, 16, partial(step, chunk=chunk), carry)
    handed_ref[:CTX, :] = xs[:CTX, :].astype(bf16)
    for k, part in enumerate(split_three(carry[0]) + split_three(carry[1])):
        handed_ref[CTX + k * STATES : CTX + (k + 1) * STATES, :] = part


def project(flag_ref, tile_ref, weight_ref, qkv_ref):
    for half in range(2):
        qkv_ref[half] = mm(tile_ref[half], weight_ref[...]).astype(bf16)


def ssm_carry_in(
    flag_ref, local_ref, handed_ref, rate_ref, coef_ref, first_ref, second_ref, enter_ref, acc
):
    channels = rate_ref.shape[1] // 2
    for slot in range(2):
        to = slice(slot * channels, (slot + 1) * channels)
        source = slice((1 - slot) * channels, (2 - slot) * channels)
        first_ref[:, to] = handed_ref[:CTX, source]
        enter_ref[0, :, to] = join_three(handed_ref, CTX, source)
        enter_ref[1, :, to] = join_three(handed_ref, CTX + 3 * STATES, source)
    rate = rate_ref[...]
    decay = jnp.exp(-rate)
    coef = coef_ref[...]

    def step(eight, state):
        rows = []
        for k in range(8):
            rows.append(jnp.sum(coef * state, axis=0, keepdims=True))
            state = decay * state
        acc[aligned(eight * 8, 8), :] = jnp.concatenate(rows, axis=0)
        return state

    lax.fori_loop(0, 16, step, enter_ref[0] * jnp.exp(-129.0 * rate))
    second_ref[...] = (local_ref[...] + acc[...]).astype(bf16)


def qkv_back(flag_ref, dqkv_ref, near_weight_ref, far_weight_ref, out_ref):
    split = near_weight_ref.shape[1]
    for half in range(2):
        out_ref[half] = mm(dqkv_ref[half, :, :split], near_weight_ref[...], NT) + mm(
            dqkv_ref[half, :, split:], far_weight_ref[...], NT
        )


def ssm_signal_grad(
    flag_ref, near_ref, returned_ref, rate_ref, coef_ref, skip_ref, total_ref, own_ref, send_ref,
    last_ref, rows_out, total,
):
    channels = rate_ref.shape[1] // 2
    adjoints = []
    for slot in range(2):
        to = slice(slot * channels, (slot + 1) * channels)
        source = slice((1 - slot) * channels, (2 - slot) * channels)
        last_ref[:, to] = returned_ref[:CTX, source].astype(f32)
        adjoints.append(join_three(returned_ref, CTX, source))
    decay = jnp.exp(-rate_ref[...])
    coef = coef_ref[...]
    skip = skip_ref[...]

    def step(j, adjoint, chunk):
        eight = 15 - j
        at = aligned(eight * 8, 8)
        if chunk % 2:
            g8 = (near_ref, last_ref)[chunk // 2][at, :]
        rows = [None] * 8
        for k in range(7, -1, -1):
            adjoint = decay * adjoint
            if chunk % 2:
                adjoint = adjoint + g8[k : k + 1]
            rows[k] = jnp.sum(coef * adjoint, axis=0, keepdims=True)
        y8 = jnp.concatenate(rows, axis=0)
        if chunk % 2:
            y8 = y8 + skip * g8
        rows_out[aligned((chunk * 16 + eight) * 8, 8), :] = y8
        return adjoint

    adjoint = jnp.concatenate(adjoints, axis=1)
    for chunk in (3, 2, 1, 0):
        adjoint = lax.fori_loop(0, 16, partial(step, chunk=chunk), adjoint)
    for half in (1, 0):
        total[...] = total_ref[half]
        source = aligned(jnp.bitwise_xor(flag_ref[ODD], half) * HALF, HALF)
        for slot, name in enumerate((NEAR, FAR)):
            total[:, aligned(flag_ref[name] * channels, channels)] += rows_out[
                source, slot * channels : (slot + 1) * channels
            ]
        if half:
            send_ref[...] = total[...].astype(bf16)
        else:
            own_ref[...] = total[...]


def ssm_param_grad(
    flag_ref, tile_ref, near_ref, last_ref, enter_ref, rate_ref, coef_ref, out_ref, xs
):
    load_signal(flag_ref, tile_ref, xs)
    decay = jnp.exp(-rate_ref[...])
    zero = jnp.zeros_like(decay)

    def step(eight, carry, chunk):
        state, slope, for_coef, for_rate = carry
        x8 = xs[aligned((chunk * 16 + eight) * 8, 8), :]
        if chunk % 2:
            g8 = (near_ref, last_ref)[chunk // 2][aligned(eight * 8, 8), :]
        for k in range(8):
            slope = decay * (slope + state)
            state = decay * state + x8[k : k + 1]
            if chunk % 2:
                for_coef = for_coef + state * g8[k : k + 1]
                for_rate = for_rate + slope * g8[k : k + 1]
        return state, slope, for_coef, for_rate

    carry = (enter_ref[0], enter_ref[1], zero, zero)
    for chunk in range(4):
        carry = lax.fori_loop(0, 16, partial(step, chunk=chunk), carry)
    out_ref[:STATES, :] = -coef_ref[...] * carry[3]
    out_ref[STATES : 2 * STATES, :] = carry[2]
    skip = jnp.sum(xs[CTX : 2 * CTX] * near_ref[...], axis=0, keepdims=True) + jnp.sum(
        xs[3 * CTX :] * last_ref[...], axis=0, keepdims=True
    )
    out_ref[2 * STATES :, :] = jnp.concatenate(
        [skip, jnp.zeros((out_ref.shape[0] - 2 * STATES - 1, skip.shape[1]), f32)], axis=0
    )


def causal(scores):
    rows = lax.broadcasted_iota(jnp.int32, scores.shape, 0)
    cols = lax.broadcasted_iota(jnp.int32, scores.shape, 1)
    return jnp.where(cols <= rows, scores, masked_score)


def softmax_parts(parts):
    top = parts[0].max(axis=-1, keepdims=True)
    for part in parts[1:]:
        top = jnp.maximum(top, part.max(axis=-1, keepdims=True))
    weights = [jnp.exp(part - top) for part in parts]
    total = weights[0].sum(axis=-1, keepdims=True)
    for weight in weights[1:]:
        total = total + weight.sum(axis=-1, keepdims=True)
    return [weight / total for weight in weights]


def block_probs(q0, q1, k0, k1, first, second, whole, late):
    has_first = late > 0
    is_whole = whole > 0
    chosen = jnp.where(is_whole, first, second)
    chosen_ok = jnp.logical_or(jnp.logical_not(is_whole), has_first)
    s00 = causal(mm(q0, k0, NT) * score_scale)
    s0c = jnp.where(has_first, mm(q0, first, NT) * score_scale, masked_score)
    s11 = causal(mm(q1, k1, NT) * score_scale)
    s10 = jnp.where(is_whole, mm(q1, k0, NT) * score_scale, masked_score)
    s1c = jnp.where(chosen_ok, mm(q1, chosen, NT) * score_scale, masked_score)
    return softmax_parts([s00, s0c]), softmax_parts([s11, s10, s1c]), chosen


def head_parts(qkv_ref, head, half):
    channels = qkv_ref.shape[2] // 3
    return [
        qkv_ref[half, :, part * channels + head * HD : part * channels + (head + 1) * HD]
        for part in range(3)
    ]


def attend(flag_ref, qkv_ref, first_ref, second_ref, att_ref, slot):
    half0 = flag_ref[ODD]
    half1 = 1 - half0
    heads = qkv_ref.shape[2] // (3 * HD)
    for head in range(heads):
        q0, k0, v0 = head_parts(qkv_ref, head, half0)
        q1, k1, v1 = head_parts(qkv_ref, head, half1)
        at = slice((slot * heads + head) * HD, (slot * heads + head + 1) * HD)
        first = first_ref[:, at]
        second = second_ref[:, at]
        (p00, p0c), (p11, p10, p1c), chosen = block_probs(
            q0, q1, k0, k1, first, second, flag_ref[WHOLE], flag_ref[LATE]
        )
        to = slice(head * HD, (head + 1) * HD)
        att_ref[half0, :, to] = (mm(p00.astype(bf16), v0) + mm(p0c.astype(bf16), first)).astype(
            bf16
        )
        att_ref[half1, :, to] = (
            mm(p11.astype(bf16), v1) + mm(p10.astype(bf16), v0) + mm(p1c.astype(bf16), chosen)
        ).astype(bf16)


def attention_near(flag_ref, qkv_ref, first_ref, second_ref, att_ref):
    attend(flag_ref, qkv_ref, first_ref, second_ref, att_ref, 0)


def attention_far(
    flag_ref, qkv_ref, first_ref, second_ref, near_ref, out_near_ref, out_far_ref, att_ref, own_ref,
    send_ref,
):
    attend(flag_ref, qkv_ref, first_ref, second_ref, att_ref, 1)

    def projected(half):
        return mm(near_ref[half], out_near_ref[...]) + mm(att_ref[half], out_far_ref[...], NT)

    send_ref[...] = projected(1).astype(bf16)
    own_ref[...] = projected(0)


def attended_grads(flag_ref, own_ref, other_ref, out_near_ref, out_far_ref, grad_ref, sent_ref):
    split = out_near_ref.shape[0]
    for half, ref in enumerate((own_ref, other_ref)):
        grad_ref[half, :, :split] = mm(ref[...], out_near_ref[...], NT).astype(bf16)
        grad_ref[half, :, split:] = mm(ref[...], out_far_ref[...]).astype(bf16)
        in_sent_order(flag_ref, ref, sent_ref.at[half])


def attention_backward(
    flag_ref, near_ref, far_ref, first_ref, second_ref, grad_ref, rate_ref, out_ref, second_out_ref,
    returned_ref,
):
    half0 = flag_ref[ODD]
    half1 = 1 - half0
    is_whole = flag_ref[WHOLE] > 0
    heads = near_ref.shape[2] // (3 * HD)
    for index in range(2 * heads):
        slot, head = index // heads, index % heads
        qkv_ref = (near_ref, far_ref)[slot]
        q0, k0, v0 = head_parts(qkv_ref, head, half0)
        q1, k1, v1 = head_parts(qkv_ref, head, half1)
        at = slice(index * HD, (index + 1) * HD)
        g0 = grad_ref[half0, :, at]
        g1 = grad_ref[half1, :, at]
        first = first_ref[:, at]
        second = second_ref[:, at]
        early, later, chosen = block_probs(
            q0, q1, k0, k1, first, second, flag_ref[WHOLE], flag_ref[LATE]
        )

        def score_grads(probs, rows, values):
            prob_grads = [mm(rows, v, NT) for v in values]
            centre = sum((p * d).sum(axis=-1, keepdims=True) for p, d in zip(probs, prob_grads))
            return [(p * (d - centre)).astype(bf16) for p, d in zip(probs, prob_grads)]

        d00, d0c = score_grads(early, g0, (v0, first))
        d11, d10, d1c = score_grads(later, g1, (v1, v0, chosen))
        p00, p0c = [p.astype(bf16) for p in early]
        p11, p10, p1c = [p.astype(bf16) for p in later]
        base = slot * 3 * heads * HD + head * HD
        for_q, for_k, for_v = [
            slice(base + part * heads * HD, base + part * heads * HD + HD) for part in range(3)
        ]
        out_ref[half0, :, for_q] = ((mm(d00, k0) + mm(d0c, first)) * score_scale).astype(bf16)
        out_ref[half1, :, for_q] = (
            (mm(d11, k1) + mm(d10, k0) + mm(d1c, chosen)) * score_scale
        ).astype(bf16)
        out_ref[half0, :, for_k] = ((mm(d00, q0, TN) + mm(d10, q1, TN)) * score_scale).astype(bf16)
        out_ref[half1, :, for_k] = (mm(d11, q1, TN) * score_scale).astype(bf16)
        out_ref[half0, :, for_v] = (mm(p00, g0, TN) + mm(p10, g1, TN)).astype(bf16)
        out_ref[half1, :, for_v] = mm(p11, g1, TN).astype(bf16)
        from_early = mm(d0c, q0, TN) * score_scale + mm(p0c, g0, TN)
        from_later = mm(d1c, q1, TN) * score_scale + mm(p1c, g1, TN)
        returned_ref[:CTX, at] = (from_early + jnp.where(is_whole, from_later, 0.0)).astype(bf16)
        second_out_ref[:, at] = jnp.where(is_whole, 0.0, from_later)

    rate = rate_ref[...]
    decay = jnp.exp(-rate)

    def step(j, adjoint):
        g8 = second_out_ref[aligned((15 - j) * 8, 8), :]
        for k in range(7, -1, -1):
            adjoint = decay * adjoint + g8[k : k + 1]
        return adjoint

    adjoint = lax.fori_loop(0, 16, step, jnp.zeros_like(rate)) * jnp.exp(-float(CTX) * rate)
    for k, part in enumerate(split_three(adjoint)):
        returned_ref[CTX + k * STATES : CTX + (k + 1) * STATES, :] = part


def flat(ref):
    if len(ref.shape) == 2:
        return ref[...]
    part = ref[:, 0]
    return part.reshape(part.shape[0] * part.shape[1], part.shape[2])


def feed_forward(
    flag_ref, n_ref, c_ref, up0_ref, down0_ref, up1_ref, down1_ref, act_ref, gate_ref, sent_ref,
    down_out_ref, back_out_ref, acc_down, acc_back,
):
    step = pl.program_id(0)
    steps = pl.num_programs(0)
    per = steps // 2

    @pl.when(step == 0)
    def _():
        acc_down[...] = jnp.zeros_like(acc_down)
        acc_back[...] = jnp.zeros_like(acc_back)
        in_sent_order(flag_ref, n_ref, sent_ref)

    def body(up, down, slot):
        gate = mm(n_ref[...], up)
        cdf = 0.5 * (1.0 + lax.erf(gate * (1.0 / math.sqrt(2.0))))
        act = (gate * cdf).astype(bf16)
        slope = cdf + gate * jnp.exp(-0.5 * gate * gate) * (1.0 / math.sqrt(2.0 * math.pi))
        grad = (mm(c_ref[...], down, NT) * slope).astype(bf16)
        gate_ref[...] = grad
        hidden = act_ref.shape[1] // 2
        width = hidden // GROUP
        count = act.shape[1] // width
        for k in range(count):
            mask = jnp.bitwise_xor(flag_ref[PLACE], (step - slot * per) * count + k)
            to = (1 - mask % 2) * 4 + (mask // 2 % 2) * 2 + mask // 4
            act_ref[:, aligned(slot * hidden + to * width, width)] = act[
                :, k * width : (k + 1) * width
            ]
        acc_down[...] += mm(act, down)
        acc_back[...] += mm(grad, up, NT)

    @pl.when(step < per)
    def _():
        body(up0_ref[...], down0_ref[...], 0)

    @pl.when(step >= per)
    def _():
        body(flat(up1_ref), flat(down1_ref), 1)

    @pl.when(step == steps - 1)
    def _():
        down_out_ref[...] = acc_down[...].astype(down_out_ref.dtype)
        back_out_ref[...] = acc_back[...].astype(back_out_ref.dtype)


def run_feed_forward(flags, rows, cot, up, down, far, kind):
    tokens, width = rows.shape
    block = 512
    hidden = up.shape[1]
    per = hidden // block
    slices, slice_rows = far.shape[0], far.shape[2]

    def near_at(j):
        return jnp.minimum(j, per - 1)

    def far_at(j):
        return jnp.maximum(j - per, 0)

    whole = pl.BlockSpec((tokens, width), lambda j: (0, 0))
    return pl.pallas_call(
        feed_forward,
        grid=(2 * per,),
        out_shape=(
            shape((tokens, 2 * hidden), bf16),
            shape((tokens, 2 * hidden), bf16),
            shape((tokens, width), bf16),
            shape((tokens, width), kind),
            shape((tokens, width), kind),
        ),
        in_specs=[
            pl.BlockSpec(memory_space=pltpu.SMEM),
            whole,
            whole,
            pl.BlockSpec((width, block), lambda j: (0, near_at(j))),
            pl.BlockSpec((block, width), lambda j: (near_at(j), 0)),
            pl.BlockSpec((slices, 1, slice_rows, block), lambda j: (0, 0, 0, far_at(j))),
            pl.BlockSpec((slices // per, 1, slice_rows, width), lambda j: (far_at(j), 1, 0, 0)),
        ],
        out_specs=(
            pl.BlockSpec((tokens, 2 * hidden), lambda j: (0, 0)),
            pl.BlockSpec((tokens, block), lambda j: (0, j)),
            whole,
            whole,
            whole,
        ),
        scratch_shapes=[pltpu.VMEM((tokens, width), f32), pltpu.VMEM((tokens, width), f32)],
        compiler_params=pltpu.CompilerParams(
            vmem_limit_bytes=24 * 1024 * 1024, dimension_semantics=("arbitrary",)
        ),
        cost_estimate=length(0),
    )(flags, rows, cot, up, down, far, far)


def products(lhs_refs, rhs_refs, columns, split=None):
    total = None
    for lhs_ref, rhs_ref in zip(lhs_refs, rhs_refs):
        term = mm(lhs_ref[:, columns], rhs_ref[...], TN)
        total = term if total is None else total + term
    return total


def down_pass(flag_ref, act0, act1, cot0, cot1, out_ref):
    hidden = act0.shape[1] // 2
    part = hidden // 4
    for slot in range(2):
        value = products(
            (act0, act1), (cot0, cot1), slice(slot * hidden, slot * hidden + hidden // 2)
        ).astype(bf16)
        out_ref[slot * part : (slot + 1) * part, :] = value[part:]
        out_ref[(2 + slot) * part : (3 + slot) * part, :] = value[:part]


def down_keep(flag_ref, act0, act1, cot0, cot1, core_ref, send_ref, left_ref):
    hidden = act0.shape[1] // 2
    part = hidden // 4
    for slot in range(2):
        value = products(
            (act0, act1), (cot0, cot1), slice(slot * hidden + hidden // 2, (slot + 1) * hidden)
        )
        to = slice(slot * part, (slot + 1) * part)
        send_ref[to, :] = (value[part:] + core_ref[to, :].astype(f32)).astype(bf16)
        left_ref[to, :] = value[:part] + core_ref[2 * part + to.start : 2 * part + to.stop, :].astype(
            f32
        )


def down_step(flag_ref, left_ref, received_ref, own_ref, send_ref):
    rows = own_ref.shape[0] // 2
    for slot in range(2):
        to = slice(slot * rows, (slot + 1) * rows)
        own = slice(2 * slot * rows, (2 * slot + 1) * rows)
        send = slice((2 * slot + 1) * rows, (2 * slot + 2) * rows)
        own_ref[to, :] = left_ref[own, :] + received_ref[own, :].astype(f32)
        send_ref[to, :] = (left_ref[send, :] + received_ref[send, :].astype(f32)).astype(bf16)


def y_first(value, rows):
    parts = [value[k * rows : (k + 1) * rows] for k in (1, 3, 0, 2)]
    return jnp.concatenate(parts[:2], 0), jnp.concatenate(parts[2:], 0)


def rows_pass(flag_ref, lhs0, lhs1, rhs0, rhs1, out_ref):
    half = lhs0.shape[1] // 2
    value = products((lhs0, lhs1), (rhs0, rhs1), slice(0, half)).astype(bf16)
    send, left = y_first(value, half // 4)
    out_ref[: half // 2, :] = send
    out_ref[half // 2 :, :] = left


def rows_keep(flag_ref, lhs0, lhs1, rhs0, rhs1, core_ref, send_ref, left_ref):
    half = lhs0.shape[1] // 2
    value = products((lhs0, lhs1), (rhs0, rhs1), slice(half, 2 * half))
    send, left = y_first(value, half // 4)
    send_ref[...] = (send + core_ref[: half // 2, :].astype(f32)).astype(bf16)
    left_ref[...] = left + core_ref[half // 2 :, :].astype(f32)


def up_step(flag_ref, left_ref, received_ref, own_ref, send_ref):
    rows = own_ref.shape[0]
    own_ref[...] = left_ref[:rows, :] + received_ref[:rows, :].astype(f32)
    send_ref[...] = (left_ref[rows:, :] + received_ref[rows:, :].astype(f32)).astype(bf16)


def own_slices(flag_ref, down_own, down_received, up_own, up_received, near_ref, far_ref):
    rows, hidden = up_own.shape[0], up_own.shape[1] // 2
    down = down_own[...] + down_received[...].astype(f32)
    up = up_own[...] + up_received[...].astype(f32)
    width = down.shape[1]
    for slot, ref in enumerate((near_ref, far_ref)):
        ref[:, :width] = down[slot * rows : (slot + 1) * rows].astype(ref.dtype)
        ref[:, width:] = up[:, slot * hidden : (slot + 1) * hidden].astype(ref.dtype)


def attn_pass(flag_ref, one0, one1, dqkv0, dqkv1, back0, back1, att0, att1, att2, att3, out_ref):
    half = one0.shape[1] // 2
    width = dqkv0.shape[1]
    channels = att0.shape[1]
    columns = slice(0, half)
    out_ref[:, :width] = products((one0, one1), (dqkv0, dqkv1), columns).astype(bf16)
    for slot, pair in enumerate(((att0, att1), (att2, att3))):
        at = width + slot * channels
        out_ref[:, at : at + channels] = products((back0, back1), pair, columns).astype(bf16)


def attn_keep(
    flag_ref, one0, one1, dqkv0, dqkv1, back0, back1, att0, att1, att2, att3, core_ref, own_ref,
    *send_refs,
):
    half = one0.shape[1] // 2
    rows = half // 4
    width = dqkv0.shape[1]
    channels = att0.shape[1]
    columns = slice(half, 2 * half)
    blocks = [(0, products((one0, one1), (dqkv0, dqkv1), columns))]
    for slot, pair in enumerate(((att0, att1), (att2, att3))):
        blocks.append((width + slot * channels, products((back0, back1), pair, columns)))
    for at, block in blocks:
        to = slice(at, at + block.shape[1])
        block = block + core_ref[:, to].astype(f32)
        own_ref[:, to] = block[:rows]
        for k, ref in enumerate(send_refs):
            ref[:, to] = block[(k + 1) * rows : (k + 2) * rows].astype(bf16)


def attn_own(
    flag_ref, own_ref, r1_ref, r2_ref, r3_ref, param_ref, gains_ref, gains_received, near_ref,
    far_ref,
):
    rows = own_ref.shape[0]
    total = own_ref[...] + (
        r1_ref[...].astype(f32) + r2_ref[...].astype(f32) + r3_ref[...].astype(f32)
    )
    channels = total.shape[1] // 8
    gains = gains_ref[...] + gains_received[...]
    for slot, ref in enumerate((near_ref, far_ref)):
        ref[:rows, : 3 * channels] = total[:, slot * 3 * channels : (slot + 1) * 3 * channels].astype(
            ref.dtype
        )
        ref[:rows, 3 * channels :] = total[
            :, (6 + slot) * channels : (7 + slot) * channels
        ].astype(ref.dtype)
        small = jnp.concatenate(
            [param_ref[:, slot * channels : (slot + 1) * channels], gains], axis=0
        ).astype(ref.dtype)
        count = small.shape[0] // 4
        for quarter in range(4):
            ref[rows : rows + count, quarter * channels : (quarter + 1) * channels] = small[
                quarter * count : (quarter + 1) * count
            ]
        ref[rows + count :, :] = jnp.zeros((ref.shape[0] - rows - count, 4 * channels), ref.dtype)


def add_two(flag_ref, a_ref, b_ref, out_ref):
    out_ref[...] = (a_ref[...].astype(f32) + b_ref[...].astype(f32)).astype(out_ref.dtype)


def add_three(flag_ref, a_ref, b_ref, c_ref, out_ref):
    out_ref[...] = (a_ref[...] + b_ref[...] + c_ref[...].astype(f32)).astype(out_ref.dtype)


def widen(all_ref, down_ref, up_ref):
    down = down_ref.shape[1]
    down_ref[...] = all_ref[:, :down].astype(f32)
    up_ref[...] = all_ref[:, down:].astype(f32)


def run_widen(value, down_width, up_width):
    rows = value.shape[0] // 4
    return pl.pallas_call(
        widen,
        grid=(4,),
        in_specs=[pl.BlockSpec((rows, value.shape[1]), lambda j: (j, 0))],
        out_specs=(
            pl.BlockSpec((rows, down_width), lambda j: (j, 0)),
            pl.BlockSpec((rows, up_width), lambda j: (j, 0)),
        ),
        out_shape=(shape((value.shape[0], down_width)), shape((value.shape[0], up_width))),
        compiler_params=pltpu.CompilerParams(vmem_limit_bytes=56 * 1024 * 1024),
        cost_estimate=length(0),
    )(value)


def sources(flag_ref, even_ref, odd_ref, rows):
    for pair in range(GROUP // 2):
        for side, ref in enumerate((even_ref, odd_ref)):
            source = jnp.bitwise_xor(flag_ref[PLACE], 2 * pair + side)
            yield ref, pair, aligned(source * rows, rows)


def assemble_weight(flag_ref, even_ref, odd_ref, tile_ref, weight_ref, out_ref, qkv_ref):
    split = weight_ref.shape[1]
    for ref, pair, at in sources(flag_ref, even_ref, odd_ref, even_ref.shape[1]):
        weight_ref[at, :] = ref[pair, :, :split]
        out_ref[at, :] = ref[pair, :, split:]
    project(flag_ref, tile_ref, weight_ref, qkv_ref)


def assemble_grad(flag_ref, even_ref, odd_ref, qkv_ref, out_ref, small_ref):
    channels = qkv_ref.shape[2]
    rows = qkv_ref.shape[1] // GROUP
    count = small_ref.shape[0] // 4
    total = None
    for ref, pair, at in sources(flag_ref, even_ref, odd_ref, rows):
        for part in range(3):
            qkv_ref[part, at, :] = ref[
                pair, :rows, part * channels : (part + 1) * channels
            ].astype(f32)
        out_ref[:, at] = ref[pair, :rows, 3 * channels :].astype(f32).T
        term = ref[pair, rows:, :].astype(f32)
        total = term if total is None else total + term
    for quarter in range(4):
        small_ref[quarter * count : (quarter + 1) * count, :] = total[
            :count, quarter * channels : (quarter + 1) * channels
        ]


class Order:
    def __init__(self):
        self.last = ()

    def __call__(self, *values):
        tied = lax.optimization_barrier((values, self.last))[0]
        return tied[0] if len(tied) == 1 else tied

    def done(self, result):
        self.last = result
        return result


def per_device(
    inputs,
    block_size,
    gain_attn,
    qkv_weight,
    ssm_rate,
    ssm_coef,
    ssm_skip,
    out_weight,
    gain_mlp,
    up_weight,
    down_weight,
    cotangent,
    dp_size,
):
    z = lax.axis_index("mp")
    place = jnp.bitwise_and(lax.axis_index("dp"), GROUP - 1)
    groups = [[g * GROUP + k for k in range(GROUP)] for g in range(dp_size // GROUP)]
    groups = groups if len(groups) > 1 else None

    def swap_mp(value, mask):
        return lax.ppermute(value, "mp", [(k, k ^ mask) for k in range(4)])

    def swap_dp(value, mask):
        return lax.ppermute(value, "dp", [(k, k ^ mask) for k in range(dp_size)])

    def gather(value):
        return lax.all_gather(value, "dp", axis=0, tiled=True, axis_index_groups=groups)

    def gather_by_xor(piece):
        return [piece] + [swap_dp(piece, 2 * k) for k in range(1, GROUP // 2)]

    def over_groups(own):
        mask = GROUP
        while mask < dp_size:
            own = own + swap_dp(own.astype(bf16), mask).astype(f32)
            mask *= 2
        return own.astype(bf16)

    model_dim = inputs.shape[2]
    channels = qkv_weight.shape[2]
    hidden = up_weight.shape[1]
    wide = 2 * channels
    rows = model_dim // GROUP
    row = inputs[0]
    cot = cotangent[0]
    z_far = jnp.bitwise_xor(z, 2)
    whole = (block_size[0] > HALF).astype(jnp.int32)
    flags = jnp.stack(
        [whole, jnp.right_shift(z, 1), jnp.bitwise_and(z, 1), z, z_far, place]
    ).astype(jnp.int32)
    gain_one = gain_attn[None]
    gain_two = gain_mlp[None]
    order = Order()
    half = shape((HALF, model_dim))
    half_low = shape((HALF, model_dim), bf16)

    normed_one = order.done(call(norm_one, half_low)(flags, row, gain_one))
    paired_one = swap_mp(normed_one, 1)
    qkv_parts = jnp.transpose(qkv_weight, (1, 0, 2))
    ssm_pack = jnp.concatenate(
        [ssm_rate.T, ssm_coef.T, ssm_skip[None], jnp.zeros((15, channels), f32)], 0
    )
    attn_slice, mlp_slice = order.done(
        run_cut_slices(flags, order(qkv_parts), out_weight, up_weight, down_weight, ssm_pack)
    )
    attn_across = swap_mp(attn_slice, 2)
    near_qkv = order.done(jnp.concatenate(list(order(*[qkv_parts[k] for k in range(3)])), 1))

    paired_one, attn_across = order.done(order(paired_one, attn_across))
    attn_mine = attn_across[:rows]
    attn_x = swap_dp(attn_mine, 2)
    mlp_across = swap_mp(order(mlp_slice), 2)
    paired_cot = swap_mp(order(cot), 1)
    ssm_both = call(join_ssm, shape((48, wide)))(flags, ssm_pack, attn_across)
    rate_t, coef_t, skip_t = ssm_both[:16], ssm_both[16:32], ssm_both[32:33]
    tile_one, one_sent, second_local, handed = order.done(
        call(
            ssm_forward,
            (
                shape((2, HALF, model_dim), bf16),
                shape((2, HALF, model_dim), bf16),
                shape((CTX, wide)),
                shape((CTX + 6 * STATES, wide), bf16),
            ),
            scratch=[pltpu.VMEM((2 * HALF, wide), f32)],
        )(flags, normed_one, order(paired_one), rate_t, coef_t, skip_t)
    )
    handed = lax.ppermute(handed, "mp", [(0, 2), (1, 3)])

    qkv_shape = shape((2, HALF, 3 * channels), bf16)
    att_shape = shape((2, HALF, channels), bf16)
    attn_two = order.done(jnp.stack([attn_mine, order(attn_x)]))
    attn_y = swap_dp(attn_two, 4)
    paired_cot = order.done(order(paired_cot))
    mlp_across = order.done(order(mlp_across))
    qkv_near = order.done(
        call(project, qkv_shape, micros=4)(flags, order(tile_one), near_qkv)
    )
    attn_y = order.done(order(attn_y))
    ctx_first, ctx_second, enter_state = order.done(
        call(
            ssm_carry_in,
            (shape((CTX, wide), bf16), shape((CTX, wide), bf16), shape((2, STATES, wide))),
            scratch=[pltpu.VMEM((CTX, wide), f32)],
        )(flags, second_local, order(handed), rate_t, coef_t)
    )
    mlp_far = gather(order(mlp_across)).reshape(GROUP, 2, rows, model_dim)
    even = order.done(jnp.concatenate(list(order(attn_two, attn_y)), 0))
    odd_part = swap_dp(even, 1)
    att_near = order.done(
        call(attention_near, att_shape)(flags, order(qkv_near), ctx_first, ctx_second)
    )
    far_qkv, far_out, qkv_far = order.done(
        call(
            assemble_weight,
            (
                shape((model_dim, 3 * channels), bf16),
                shape((model_dim, channels), bf16),
                qkv_shape,
            ),
        )(flags, even, order(odd_part), tile_one)
    )
    att_far, out_own, out_send = order.done(
        call(attention_far, (att_shape, half, half_low))(
            flags, order(qkv_far), ctx_first, ctx_second, att_near, out_weight, far_out
        )
    )
    out_received = swap_mp(out_send, 1)
    middle, normed_two = order.done(
        call(norm_two, (half, half_low))(
            flags, row, out_own, order(out_received), gain_two
        )
    )

    paired_two = swap_mp(normed_two, 1)
    warm = order.done(
        call(touch, shape((8, 128), bf16))(flags, order(up_weight), down_weight, cot, paired_cot)
    )
    mlp = (up_weight, down_weight, mlp_far)
    act_other, gate_other, two_other, down_send, back_send = order.done(
        run_feed_forward(flags, order(paired_two), paired_cot, *mlp, bf16)
    )
    back_received = swap_mp(back_send, 1)
    act_own, gate_own, two_own, down_own, back_own = order.done(
        run_feed_forward(flags, order(normed_two), cot, *mlp, f32)
    )

    def low(*dims):
        return shape(dims, bf16)

    side = model_dim // 2
    acts = (act_own, act_other, cot, paired_cot)
    passed = order.done(call(down_pass, low(hidden, model_dim))(flags, order(act_own), *acts[1:]))
    down_core = swap_dp(passed, 1)
    ups = (two_own, two_other, gate_own, gate_other)
    passed = order.done(call(rows_pass, low(side, 2 * hidden))(flags, order(two_own), *ups[1:]))
    up_core = swap_dp(passed, 1)
    middle_grad, attn_grad, gain_mlp_grad = order.done(
        call(norm_two_back, (half, half_low, shape((1, model_dim))), micros=12)(
            flags, middle, back_own, order(back_received), cot, gain_two, warm
        )
    )
    paired_back = swap_mp(attn_grad, 1)
    down_send_x, down_left = order.done(
        call(down_keep, (low(side, model_dim), shape((side, model_dim))))(
            flags, *acts, order(down_core)
        )
    )
    down_x = swap_dp(down_send_x, 2)
    up_send_y, up_left = order.done(
        call(rows_keep, (low(side // 2, 2 * hidden), shape((side // 2, 2 * hidden))))(
            flags, *ups, order(up_core)
        )
    )
    up_y = swap_dp(up_send_y, 4)

    att_grad, back_sent = order.done(
        call(
            attended_grads,
            (shape((2, HALF, wide), bf16), shape((2, HALF, model_dim), bf16)),
            micros=4,
        )(flags, attn_grad, order(paired_back), out_weight, far_out)
    )
    dqkv, second_grad, returned = order.done(
        call(
            attention_backward,
            (
                shape((2, HALF, 6 * channels), bf16),
                shape((CTX, wide)),
                shape((CTX + 3 * STATES, wide), bf16),
            ),
        )(flags, qkv_near, qkv_far, ctx_first, ctx_second, order(att_grad), rate_t)
    )
    returned = lax.ppermute(returned, "mp", [(2, 0), (3, 1)])
    one_total = order.done(
        call(qkv_back, shape((2, HALF, model_dim)))(flags, order(dqkv), near_qkv, far_qkv)
    )
    attns = (
        one_sent[0], one_sent[1], dqkv[0], dqkv[1], back_sent[0], back_sent[1],
        att_near[0], att_near[1], att_far[0], att_far[1],
    )
    passed = order.done(
        call(attn_pass, low(side, 8 * channels))(flags, order(attns[0]), *attns[1:])
    )
    attn_core = swap_dp(passed, 1)
    down_mine, down_send_y = order.done(
        call(down_step, (shape((2 * rows, model_dim)), low(2 * rows, model_dim)))(
            flags, down_left, order(down_x)
        )
    )
    down_y = swap_dp(down_send_y, 4)
    up_mine, up_send_x = order.done(
        call(up_step, (shape((rows, 2 * hidden)), low(rows, 2 * hidden)))(
            flags, up_left, order(up_y)
        )
    )
    up_x = swap_dp(up_send_x, 2)
    one_own, one_send, last_grad = order.done(
        call(
            ssm_signal_grad,
            (half, half_low, shape((CTX, wide))),
            scratch=[pltpu.VMEM((2 * HALF, wide), f32), pltpu.VMEM((HALF, model_dim), f32)],
            micros=30,
        )(flags, second_grad, order(returned), rate_t, coef_t, skip_t, one_total)
    )
    one_received = swap_mp(one_send, 1)
    attn_mine, *attn_sends = order.done(
        call(attn_keep, (shape((rows, 8 * channels)),) + (low(rows, 8 * channels),) * 3)(
            flags, *attns, order(attn_core)
        )
    )
    attn_sent = [swap_dp(part, SENT[5 + k]) for k, part in enumerate(attn_sends)]
    mlp_width = model_dim + hidden
    mlp_near, mlp_send = order.done(
        call(own_slices, (shape((rows, mlp_width)), low(rows, mlp_width)))(
            flags, down_mine, order(down_y), up_mine, order(up_x)
        )
    )
    mlp_received = swap_mp(mlp_send, 2)
    param_grad = order.done(
        call(
            ssm_param_grad,
            shape((40, wide)),
            scratch=[pltpu.VMEM((2 * HALF, wide), f32)],
            micros=3,
        )(flags, order(tile_one), second_grad, last_grad, enter_state, rate_t, coef_t)
    )
    input_grad, gains = order.done(
        call(norm_one_back, (half, shape((2 * model_dim // channels, channels))))(
            flags, row, one_own, order(one_received), middle_grad, gain_one, gain_mlp_grad
        )
    )
    gains_received = swap_mp(gains, 1)
    slice_rows = rows + 16
    *attn_sent, gains_received = order(*attn_sent, gains_received)
    attn_near, attn_send = order.done(
        call(attn_own, (shape((slice_rows, 4 * channels)), low(slice_rows, 4 * channels)))(
            flags, attn_mine, *attn_sent, param_grad, gains, gains_received
        )
    )
    attn_received = swap_mp(attn_send, 2)
    mlp_slice_grad = order.done(
        call(add_two, low(rows, mlp_width))(flags, mlp_near, order(mlp_received))
    )
    mlp_full = gather(over_groups(mlp_slice_grad))
    down_received = swap_mp(order(down_send), 1)
    attn_slice_grad = order.done(
        call(add_two, low(slice_rows, 4 * channels))(flags, attn_near, order(attn_received))
    )
    attn_pieces = gather_by_xor(over_groups(attn_slice_grad))
    output = order.done(
        call(add_three, half_low)(flags, middle, down_own, order(down_received))
    )
    even = order.done(jnp.stack(list(order(*attn_pieces))))
    odd_part = swap_dp(even, 1)
    qkv_grad, out_grad, small = order.done(
        call(
            assemble_grad,
            (
                shape((3, model_dim, channels)),
                shape(out_weight.shape),
                shape((48, channels)),
            ),
        )(flags, even, order(odd_part))
    )
    down_grad, up_grad = run_widen(order(mlp_full), model_dim, hidden)
    gains = small[40:].reshape(2, model_dim)
    return (
        output[None],
        input_grad[None],
        gains[0],
        jnp.transpose(qkv_grad, (1, 0, 2)),
        small[:16].T,
        small[16:32].T,
        small[32],
        out_grad,
        gains[1],
        up_grad,
        down_grad,
    )


def solution(mesh):
    return jax.shard_map(
        partial(per_device, dp_size=mesh.shape["dp"]),
        mesh=mesh,
        in_specs=(
            P("dp", "mp", None),
            P("dp"),
            P(),
            P(None, None, "mp"),
            P("mp", None),
            P("mp", None),
            P("mp"),
            P("mp", None),
            P(),
            P(None, "mp"),
            P("mp", None),
            P("dp", "mp", None),
        ),
        out_specs=(
            P("dp", "mp", None),
            P("dp", "mp", None),
            P(),
            P(None, None, "mp"),
            P("mp", None),
            P("mp", None),
            P("mp"),
            P("mp", None),
            P(),
            P(None, "mp"),
            P("mp", None),
        ),
        check_vma=False,
    )
```

```python
from functools import partial
import math

import jax
import jax.numpy as jnp
from jax import lax
from jax.experimental import pallas as pl
from jax.experimental.pallas import tpu as pltpu
from jax.sharding import PartitionSpec as P

HD = 128
CTX = 128
HALF = 256
STATES = 16
GROUP = 8

f32 = jnp.float32
bf16 = jnp.bfloat16
epsilon = 1e-05
masked_score = -1e30
score_scale = 1.0 / math.sqrt(HD)
VMEM_LIMIT = 16 * 1024 * 1024

NT = (((1,), (1,)), ((), ()))
TN = (((0,), (0,)), ((), ()))
NN = (((1,), (0,)), ((), ()))

WHOLE, LATE, ODD, NEAR, FAR, PLACE = range(6)


def mm(a, b, dims=NN):
    return lax.dot_general(a, b, dims, preferred_element_type=f32)


def shape(dims, dtype=f32):
    return jax.ShapeDtypeStruct(dims, dtype)


def length(micros):
    return pl.CostEstimate(flops=int(micros * 1e9), bytes_accessed=0, transcendentals=0)


def call(kernel, out_shape, scratch=(), micros=0):
    def run(flags, *args):
        vmem = pl.BlockSpec(memory_space=pltpu.VMEM)
        return pl.pallas_call(
            kernel,
            out_shape=out_shape,
            in_specs=[pl.BlockSpec(memory_space=pltpu.SMEM)] + [vmem] * len(args),
            out_specs=jax.tree.map(lambda _: vmem, out_shape),
            scratch_shapes=scratch,
            compiler_params=pltpu.CompilerParams(vmem_limit_bytes=VMEM_LIMIT),
            cost_estimate=length(micros),
        )(flags, *args)

    return run


SENT = (1, 5, 3, 7, 0, 4, 2, 6)


def in_sent_order(flag_ref, value_ref, out_ref, masks=SENT):
    width = value_ref.shape[1] // GROUP
    for k, mask in enumerate(masks):
        source = jnp.bitwise_xor(flag_ref[PLACE], mask)
        out_ref[:, k * width : (k + 1) * width] = value_ref[:, aligned(source * width, width)]


def aligned(start, size):
    return pl.ds(pl.multiple_of(start, size), size)


def cut_slices(
    flag_ref, qkv_ref, out_ref, up_ref, down_ref, ssm_ref, attn_ref, mlp_ref, out_slice, *sems
):
    rows = mlp_ref.shape[0] // 2
    channels = out_slice.shape[0]
    count = ssm_ref.shape[0]
    for k, part in enumerate(split_three(ssm_ref[...])):
        attn_ref[rows : rows + count, k * channels : (k + 1) * channels] = part
    attn_ref[rows : rows + count, 3 * channels :] = jnp.zeros((count, channels), bf16)
    at = aligned(flag_ref[PLACE] * rows, rows)
    copies = [
        pltpu.make_async_copy(
            qkv_ref.at[part, at, :],
            attn_ref.at[:rows, part * channels : (part + 1) * channels],
            sems[part],
        )
        for part in range(3)
    ] + [
        pltpu.make_async_copy(out_ref.at[:, at], out_slice, sems[3]),
        pltpu.make_async_copy(up_ref.at[at, :], mlp_ref.at[:rows, :], sems[4]),
        pltpu.make_async_copy(down_ref.at[at, :], mlp_ref.at[rows:, :], sems[5]),
    ]
    for copy in copies:
        copy.start()
    for copy in copies:
        copy.wait()
    attn_ref[:rows, 3 * channels :] = out_slice[...].T


def join_ssm(flag_ref, own_ref, across_ref, out_ref):
    channels = own_ref.shape[1]
    start = across_ref.shape[0] - own_ref.shape[0]
    out_ref[:, :channels] = own_ref[...]
    parts = [across_ref[start:, k * channels : (k + 1) * channels].astype(f32) for k in range(3)]
    out_ref[:, channels:] = (parts[0] + parts[1]) + parts[2]


def run_cut_slices(flags, qkv_parts, out_weight, up_weight, down_weight, ssm_pack):
    channels = qkv_parts.shape[2]
    width = out_weight.shape[1]
    rows = width // GROUP
    vmem = pl.BlockSpec(memory_space=pltpu.VMEM)
    return pl.pallas_call(
        cut_slices,
        in_specs=[pl.BlockSpec(memory_space=pltpu.SMEM)]
        + [pl.BlockSpec(memory_space=pltpu.HBM)] * 4
        + [vmem],
        out_specs=(vmem, vmem),
        out_shape=(
            shape((rows + ssm_pack.shape[0], 4 * channels), bf16),
            shape((2 * rows, width), bf16),
        ),
        scratch_shapes=[pltpu.VMEM((channels, rows), bf16)] + [pltpu.SemaphoreType.DMA] * 6,
        compiler_params=pltpu.CompilerParams(vmem_limit_bytes=56 * 1024 * 1024),
        cost_estimate=length(0),
    )(flags, qkv_parts, out_weight, up_weight, down_weight, ssm_pack)


def normalise(values):
    mean = jnp.mean(values, axis=-1, keepdims=True)
    centred = values - mean
    spread = jnp.mean(centred * centred, axis=-1, keepdims=True)
    inverse = lax.rsqrt(spread + epsilon)
    return centred * inverse, inverse


def normalise_back(grad, gain, hat, inverse):
    inner = grad * gain
    return (
        inner
        - jnp.mean(inner, axis=-1, keepdims=True)
        - hat * jnp.mean(inner * hat, axis=-1, keepdims=True)
    ) * inverse


def by_rows(body, rows, block=64):
    for k in range(rows // block):
        body(slice(k * block, (k + 1) * block))


def norm_one(flag_ref, x_ref, gain_ref, out_ref):
    def body(at):
        hat, _ = normalise(x_ref[at, :].astype(f32))
        out_ref[at, :] = (hat * gain_ref[...]).astype(bf16)

    by_rows(body, x_ref.shape[0])


def touch(flag_ref, up_ref, down_ref, cot_ref, paired_ref, rows_ref, out_ref):
    out_ref[...] = (
        (up_ref[:8, :128] + down_ref[:8, :128])
        + (cot_ref[:8, :128] + paired_ref[:8, :128])
        + rows_ref[:8, :128]
    )


def norm_two(flag_ref, x_ref, own_ref, received_ref, gain_ref, middle_ref, out_ref):
    def body(at):
        middle = x_ref[at, :].astype(f32) + own_ref[at, :] + received_ref[at, :].astype(f32)
        middle_ref[at, :] = middle
        hat, _ = normalise(middle)
        out_ref[at, :] = (hat * gain_ref[...]).astype(bf16)

    by_rows(body, x_ref.shape[0])


def norm_two_back(
    flag_ref, middle_ref, own_ref, received_ref, cot_ref, gain_ref, warm_ref, grad_ref, low_ref,
    gain_out_ref,
):
    sums = []

    def body(at):
        hat, inverse = normalise(middle_ref[at, :])
        grad = own_ref[at, :] + received_ref[at, :].astype(f32)
        sums.append(jnp.sum(grad * hat, axis=0, keepdims=True))
        total = cot_ref[at, :].astype(f32) + normalise_back(grad, gain_ref[...], hat, inverse)
        grad_ref[at, :] = total
        low_ref[at, :] = total.astype(bf16)

    by_rows(body, middle_ref.shape[0])
    gain_out_ref[...] = sum(sums)


def norm_one_back(
    flag_ref, x_ref, own_ref, received_ref, middle_ref, gain_ref, gain_two_grad_ref, grad_ref,
    gain_out_ref,
):
    sums = []

    def body(at):
        hat, inverse = normalise(x_ref[at, :].astype(f32))
        grad = own_ref[at, :] + received_ref[at, :].astype(f32)
        sums.append(jnp.sum(grad * hat, axis=0, keepdims=True))
        grad_ref[at, :] = middle_ref[at, :] + normalise_back(grad, gain_ref[...], hat, inverse)

    by_rows(body, x_ref.shape[0])
    width = gain_out_ref.shape[1]
    pieces = x_ref.shape[1] // width
    for which, value in enumerate((sum(sums), gain_two_grad_ref[...])):
        for k in range(pieces):
            row = which * pieces + k
            gain_out_ref[row : row + 1, :] = value[:, k * width : (k + 1) * width]


def split_three(value):
    high = value.astype(bf16)
    rest = value - high.astype(f32)
    middle = rest.astype(bf16)
    return [high, middle, (rest - middle.astype(f32)).astype(bf16)]


def join_three(ref, start, lanes):
    parts = [ref[start + k * STATES : start + (k + 1) * STATES, lanes] for k in range(3)]
    return (parts[0].astype(f32) + parts[1].astype(f32)) + parts[2].astype(f32)


def load_signal(flag_ref, tile_ref, xs):
    channels = xs.shape[1] // 2
    for half in range(2):
        source = jnp.bitwise_xor(flag_ref[ODD], half)
        for slot, name in enumerate((NEAR, FAR)):
            xs[half * HALF : (half + 1) * HALF, slot * channels : (slot + 1) * channels] = tile_ref[
                source, :, aligned(flag_ref[name] * channels, channels)
            ].astype(f32)


def ssm_forward(
    flag_ref, own_ref, other_ref, rate_ref, coef_ref, skip_ref, tile_ref, sent_ref,
    second_ref, handed_ref, xs,
):
    tile_ref[0] = own_ref[...]
    tile_ref[1] = other_ref[...]
    in_sent_order(flag_ref, own_ref, sent_ref.at[0])
    in_sent_order(flag_ref, other_ref, sent_ref.at[1])
    load_signal(flag_ref, tile_ref, xs)
    decay = jnp.exp(-rate_ref[...])
    coef = coef_ref[...]
    skip = skip_ref[...]
    zero = jnp.zeros_like(decay)

    def step(eight, carry, chunk):
        state, slope = carry
        x8 = xs[aligned((chunk * 16 + eight) * 8, 8), :]
        rows = []
        for k in range(8):
            slope = decay * (slope + state)
            state = decay * state + x8[k : k + 1]
            if chunk % 2:
                rows.append(jnp.sum(coef * state, axis=0, keepdims=True))
        if chunk % 2:
            y8 = jnp.concatenate(rows, axis=0) + skip * x8
            at = aligned(eight * 8, 8)
            if chunk == 1:
                second_ref[at, :] = y8
            else:
                xs[at, :] = y8
        return state, slope

    carry = (zero, zero)
    for chunk in range(4):
        carry = lax.fori_loop(0, 16, partial(step, chunk=chunk), carry)
    handed_ref[:CTX, :] = xs[:CTX, :].astype(bf16)
    for k, part in enumerate(split_three(carry[0]) + split_three(carry[1])):
        handed_ref[CTX + k * STATES : CTX + (k + 1) * STATES, :] = part


def project(flag_ref, tile_ref, weight_ref, qkv_ref):
    for half in range(2):
        qkv_ref[half] = mm(tile_ref[half], weight_ref[...]).astype(bf16)


def ssm_carry_in(
    flag_ref, local_ref, handed_ref, rate_ref, coef_ref, first_ref, second_ref, enter_ref, acc
):
    channels = rate_ref.shape[1] // 2
    for slot in range(2):
        to = slice(slot * channels, (slot + 1) * channels)
        source = slice((1 - slot) * channels, (2 - slot) * channels)
        first_ref[:, to] = handed_ref[:CTX, source]
        enter_ref[0, :, to] = join_three(handed_ref, CTX, source)
        enter_ref[1, :, to] = join_three(handed_ref, CTX + 3 * STATES, source)
    rate = rate_ref[...]
    decay = jnp.exp(-rate)
    coef = coef_ref[...]

    def step(eight, state):
        rows = []
        for k in range(8):
            rows.append(jnp.sum(coef * state, axis=0, keepdims=True))
            state = decay * state
        acc[aligned(eight * 8, 8), :] = jnp.concatenate(rows, axis=0)
        return state

    lax.fori_loop(0, 16, step, enter_ref[0] * jnp.exp(-129.0 * rate))
    second_ref[...] = (local_ref[...] + acc[...]).astype(bf16)


def qkv_back(flag_ref, dqkv_ref, near_weight_ref, far_weight_ref, out_ref):
    split = near_weight_ref.shape[1]
    for half in range(2):
        out_ref[half] = mm(dqkv_ref[half, :, :split], near_weight_ref[...], NT) + mm(
            dqkv_ref[half, :, split:], far_weight_ref[...], NT
        )


def ssm_signal_grad(
    flag_ref, near_ref, returned_ref, rate_ref, coef_ref, skip_ref, total_ref, own_ref, send_ref,
    last_ref, rows_out, total,
):
    channels = rate_ref.shape[1] // 2
    adjoints = []
    for slot in range(2):
        to = slice(slot * channels, (slot + 1) * channels)
        source = slice((1 - slot) * channels, (2 - slot) * channels)
        last_ref[:, to] = returned_ref[:CTX, source].astype(f32)
        adjoints.append(join_three(returned_ref, CTX, source))
    decay = jnp.exp(-rate_ref[...])
    coef = coef_ref[...]
    skip = skip_ref[...]

    def step(j, adjoint, chunk):
        eight = 15 - j
        at = aligned(eight * 8, 8)
        if chunk % 2:
            g8 = (near_ref, last_ref)[chunk // 2][at, :]
        rows = [None] * 8
        for k in range(7, -1, -1):
            adjoint = decay * adjoint
            if chunk % 2:
                adjoint = adjoint + g8[k : k + 1]
            rows[k] = jnp.sum(coef * adjoint, axis=0, keepdims=True)
        y8 = jnp.concatenate(rows, axis=0)
        if chunk % 2:
            y8 = y8 + skip * g8
        rows_out[aligned((chunk * 16 + eight) * 8, 8), :] = y8
        return adjoint

    adjoint = jnp.concatenate(adjoints, axis=1)
    for chunk in (3, 2, 1, 0):
        adjoint = lax.fori_loop(0, 16, partial(step, chunk=chunk), adjoint)
    for half in (1, 0):
        total[...] = total_ref[half]
        source = aligned(jnp.bitwise_xor(flag_ref[ODD], half) * HALF, HALF)
        for slot, name in enumerate((NEAR, FAR)):
            total[:, aligned(flag_ref[name] * channels, channels)] += rows_out[
                source, slot * channels : (slot + 1) * channels
            ]
        if half:
            send_ref[...] = total[...].astype(bf16)
        else:
            own_ref[...] = total[...]


def ssm_param_grad(
    flag_ref, tile_ref, near_ref, last_ref, enter_ref, rate_ref, coef_ref, out_ref, xs
):
    load_signal(flag_ref, tile_ref, xs)
    decay = jnp.exp(-rate_ref[...])
    zero = jnp.zeros_like(decay)

    def step(eight, carry, chunk):
        state, slope, for_coef, for_rate = carry
        x8 = xs[aligned((chunk * 16 + eight) * 8, 8), :]
        if chunk % 2:
            g8 = (near_ref, last_ref)[chunk // 2][aligned(eight * 8, 8), :]
        for k in range(8):
            slope = decay * (slope + state)
            state = decay * state + x8[k : k + 1]
            if chunk % 2:
                for_coef = for_coef + state * g8[k : k + 1]
                for_rate = for_rate + slope * g8[k : k + 1]
        return state, slope, for_coef, for_rate

    carry = (enter_ref[0], enter_ref[1], zero, zero)
    for chunk in range(4):
        carry = lax.fori_loop(0, 16, partial(step, chunk=chunk), carry)
    out_ref[:STATES, :] = -coef_ref[...] * carry[3]
    out_ref[STATES : 2 * STATES, :] = carry[2]
    skip = jnp.sum(xs[CTX : 2 * CTX] * near_ref[...], axis=0, keepdims=True) + jnp.sum(
        xs[3 * CTX :] * last_ref[...], axis=0, keepdims=True
    )
    out_ref[2 * STATES :, :] = jnp.concatenate(
        [skip, jnp.zeros((out_ref.shape[0] - 2 * STATES - 1, skip.shape[1]), f32)], axis=0
    )


def causal(scores):
    rows = lax.broadcasted_iota(jnp.int32, scores.shape, 0)
    cols = lax.broadcasted_iota(jnp.int32, scores.shape, 1)
    return jnp.where(cols <= rows, scores, masked_score)


def softmax_parts(parts):
    top = parts[0].max(axis=-1, keepdims=True)
    for part in parts[1:]:
        top = jnp.maximum(top, part.max(axis=-1, keepdims=True))
    weights = [jnp.exp(part - top) for part in parts]
    total = weights[0].sum(axis=-1, keepdims=True)
    for weight in weights[1:]:
        total = total + weight.sum(axis=-1, keepdims=True)
    return [weight / total for weight in weights]


def block_probs(q0, q1, k0, k1, first, second, whole, late):
    has_first = late > 0
    is_whole = whole > 0
    chosen = jnp.where(is_whole, first, second)
    chosen_ok = jnp.logical_or(jnp.logical_not(is_whole), has_first)
    s00 = causal(mm(q0, k0, NT) * score_scale)
    s0c = jnp.where(has_first, mm(q0, first, NT) * score_scale, masked_score)
    s11 = causal(mm(q1, k1, NT) * score_scale)
    s10 = jnp.where(is_whole, mm(q1, k0, NT) * score_scale, masked_score)
    s1c = jnp.where(chosen_ok, mm(q1, chosen, NT) * score_scale, masked_score)
    return softmax_parts([s00, s0c]), softmax_parts([s11, s10, s1c]), chosen


def head_parts(qkv_ref, head, half):
    channels = qkv_ref.shape[2] // 3
    return [
        qkv_ref[half, :, part * channels + head * HD : part * channels + (head + 1) * HD]
        for part in range(3)
    ]


def attend(flag_ref, qkv_ref, first_ref, second_ref, att_ref, slot):
    half0 = flag_ref[ODD]
    half1 = 1 - half0
    heads = qkv_ref.shape[2] // (3 * HD)
    for head in range(heads):
        q0, k0, v0 = head_parts(qkv_ref, head, half0)
        q1, k1, v1 = head_parts(qkv_ref, head, half1)
        at = slice((slot * heads + head) * HD, (slot * heads + head + 1) * HD)
        first = first_ref[:, at]
        second = second_ref[:, at]
        (p00, p0c), (p11, p10, p1c), chosen = block_probs(
            q0, q1, k0, k1, first, second, flag_ref[WHOLE], flag_ref[LATE]
        )
        to = slice(head * HD, (head + 1) * HD)
        att_ref[half0, :, to] = (mm(p00.astype(bf16), v0) + mm(p0c.astype(bf16), first)).astype(
            bf16
        )
        att_ref[half1, :, to] = (
            mm(p11.astype(bf16), v1) + mm(p10.astype(bf16), v0) + mm(p1c.astype(bf16), chosen)
        ).astype(bf16)


def attention_near(flag_ref, qkv_ref, first_ref, second_ref, att_ref):
    attend(flag_ref, qkv_ref, first_ref, second_ref, att_ref, 0)


def attention_far(
    flag_ref, qkv_ref, first_ref, second_ref, near_ref, out_near_ref, out_far_ref, att_ref, own_ref,
    send_ref,
):
    attend(flag_ref, qkv_ref, first_ref, second_ref, att_ref, 1)

    def projected(half):
        return mm(near_ref[half], out_near_ref[...]) + mm(att_ref[half], out_far_ref[...], NT)

    send_ref[...] = projected(1).astype(bf16)
    own_ref[...] = projected(0)


def attended_grads(flag_ref, own_ref, other_ref, out_near_ref, out_far_ref, grad_ref, sent_ref):
    split = out_near_ref.shape[0]
    for half, ref in enumerate((own_ref, other_ref)):
        grad_ref[half, :, :split] = mm(ref[...], out_near_ref[...], NT).astype(bf16)
        grad_ref[half, :, split:] = mm(ref[...], out_far_ref[...]).astype(bf16)
        in_sent_order(flag_ref, ref, sent_ref.at[half])


def attention_backward(
    flag_ref, near_ref, far_ref, first_ref, second_ref, grad_ref, rate_ref, out_ref, second_out_ref,
    returned_ref,
):
    half0 = flag_ref[ODD]
    half1 = 1 - half0
    is_whole = flag_ref[WHOLE] > 0
    heads = near_ref.shape[2] // (3 * HD)
    for index in range(2 * heads):
        slot, head = index // heads, index % heads
        qkv_ref = (near_ref, far_ref)[slot]
        q0, k0, v0 = head_parts(qkv_ref, head, half0)
        q1, k1, v1 = head_parts(qkv_ref, head, half1)
        at = slice(index * HD, (index + 1) * HD)
        g0 = grad_ref[half0, :, at]
        g1 = grad_ref[half1, :, at]
        first = first_ref[:, at]
        second = second_ref[:, at]
        early, later, chosen = block_probs(
            q0, q1, k0, k1, first, second, flag_ref[WHOLE], flag_ref[LATE]
        )

        def score_grads(probs, rows, values):
            prob_grads = [mm(rows, v, NT) for v in values]
            centre = sum((p * d).sum(axis=-1, keepdims=True) for p, d in zip(probs, prob_grads))
            return [(p * (d - centre)).astype(bf16) for p, d in zip(probs, prob_grads)]

        d00, d0c = score_grads(early, g0, (v0, first))
        d11, d10, d1c = score_grads(later, g1, (v1, v0, chosen))
        p00, p0c = [p.astype(bf16) for p in early]
        p11, p10, p1c = [p.astype(bf16) for p in later]
        base = slot * 3 * heads * HD + head * HD
        for_q, for_k, for_v = [
            slice(base + part * heads * HD, base + part * heads * HD + HD) for part in range(3)
        ]
        out_ref[half0, :, for_q] = ((mm(d00, k0) + mm(d0c, first)) * score_scale).astype(bf16)
        out_ref[half1, :, for_q] = (
            (mm(d11, k1) + mm(d10, k0) + mm(d1c, chosen)) * score_scale
        ).astype(bf16)
        out_ref[half0, :, for_k] = ((mm(d00, q0, TN) + mm(d10, q1, TN)) * score_scale).astype(bf16)
        out_ref[half1, :, for_k] = (mm(d11, q1, TN) * score_scale).astype(bf16)
        out_ref[half0, :, for_v] = (mm(p00, g0, TN) + mm(p10, g1, TN)).astype(bf16)
        out_ref[half1, :, for_v] = mm(p11, g1, TN).astype(bf16)
        from_early = mm(d0c, q0, TN) * score_scale + mm(p0c, g0, TN)
        from_later = mm(d1c, q1, TN) * score_scale + mm(p1c, g1, TN)
        returned_ref[:CTX, at] = (from_early + jnp.where(is_whole, from_later, 0.0)).astype(bf16)
        second_out_ref[:, at] = jnp.where(is_whole, 0.0, from_later)

    rate = rate_ref[...]
    decay = jnp.exp(-rate)

    def step(j, adjoint):
        g8 = second_out_ref[aligned((15 - j) * 8, 8), :]
        for k in range(7, -1, -1):
            adjoint = decay * adjoint + g8[k : k + 1]
        return adjoint

    adjoint = lax.fori_loop(0, 16, step, jnp.zeros_like(rate)) * jnp.exp(-float(CTX) * rate)
    for k, part in enumerate(split_three(adjoint)):
        returned_ref[CTX + k * STATES : CTX + (k + 1) * STATES, :] = part


def feed_forward(
    flag_ref, n_ref, c_ref, up0_ref, down0_ref, up1_ref, down1_ref, act_ref, gate_ref, sent_ref,
    down_out_ref, back_out_ref, acc_down, acc_back,
):
    step = pl.program_id(0)
    steps = pl.num_programs(0)
    per = steps // 2

    @pl.when(step == 0)
    def _():
        acc_down[...] = jnp.zeros_like(acc_down)
        acc_back[...] = jnp.zeros_like(acc_back)
        in_sent_order(flag_ref, n_ref, sent_ref)

    def body(up, down, slot):
        gate = mm(n_ref[...], up)
        cdf = 0.5 * (1.0 + lax.erf(gate * (1.0 / math.sqrt(2.0))))
        act = (gate * cdf).astype(bf16)
        slope = cdf + gate * jnp.exp(-0.5 * gate * gate) * (1.0 / math.sqrt(2.0 * math.pi))
        grad = (mm(c_ref[...], down, NT) * slope).astype(bf16)
        gate_ref[...] = grad
        hidden = act_ref.shape[1] // 2
        width = hidden // GROUP
        count = act.shape[1] // width
        for k in range(count):
            mask = jnp.bitwise_xor(flag_ref[PLACE], (step - slot * per) * count + k)
            to = (1 - mask % 2) * 4 + (mask // 2 % 2) * 2 + mask // 4
            act_ref[:, aligned(slot * hidden + to * width, width)] = act[
                :, k * width : (k + 1) * width
            ]
        acc_down[...] += mm(act, down)
        acc_back[...] += mm(grad, up, NT)

    @pl.when(step < per)
    def _():
        body(up0_ref[...], down0_ref[...], 0)

    @pl.when(step >= per)
    def _():
        body(up1_ref[...], down1_ref[...], 1)

    @pl.when(step == steps - 1)
    def _():
        down_out_ref[...] = acc_down[...].astype(down_out_ref.dtype)
        back_out_ref[...] = acc_back[...].astype(back_out_ref.dtype)


def run_feed_forward(flags, rows, cot, up, down, up_far, down_far, kind):
    tokens, width = rows.shape
    block = 512
    hidden = up.shape[1]
    per = hidden // block

    def near_at(j):
        return jnp.minimum(j, per - 1)

    def far_at(j):
        return jnp.maximum(j - per, 0)

    whole = pl.BlockSpec((tokens, width), lambda j: (0, 0))
    return pl.pallas_call(
        feed_forward,
        grid=(2 * per,),
        out_shape=(
            shape((tokens, 2 * hidden), bf16),
            shape((tokens, 2 * hidden), bf16),
            shape((tokens, width), bf16),
            shape((tokens, width), kind),
            shape((tokens, width), kind),
        ),
        in_specs=[
            pl.BlockSpec(memory_space=pltpu.SMEM),
            whole,
            whole,
            pl.BlockSpec((width, block), lambda j: (0, near_at(j))),
            pl.BlockSpec((block, width), lambda j: (near_at(j), 0)),
            pl.BlockSpec((width, block), lambda j: (0, far_at(j))),
            pl.BlockSpec((block, width), lambda j: (far_at(j), 0)),
        ],
        out_specs=(
            pl.BlockSpec((tokens, 2 * hidden), lambda j: (0, 0)),
            pl.BlockSpec((tokens, block), lambda j: (0, j)),
            whole,
            whole,
            whole,
        ),
        scratch_shapes=[pltpu.VMEM((tokens, width), f32), pltpu.VMEM((tokens, width), f32)],
        compiler_params=pltpu.CompilerParams(
            vmem_limit_bytes=24 * 1024 * 1024, dimension_semantics=("arbitrary",)
        ),
        cost_estimate=length(0),
    )(flags, rows, cot, up, down, up_far, down_far)


def products(lhs_refs, rhs_refs, columns, split=None):
    total = None
    for lhs_ref, rhs_ref in zip(lhs_refs, rhs_refs):
        term = mm(lhs_ref[:, columns], rhs_ref[...], TN)
        total = term if total is None else total + term
    return total


def down_pass(flag_ref, act0, act1, cot0, cot1, out_ref):
    hidden = act0.shape[1] // 2
    part = hidden // 4
    for slot in range(2):
        value = products(
            (act0, act1), (cot0, cot1), slice(slot * hidden, slot * hidden + hidden // 2)
        ).astype(bf16)
        out_ref[slot * part : (slot + 1) * part, :] = value[part:]
        out_ref[(2 + slot) * part : (3 + slot) * part, :] = value[:part]


def down_keep(flag_ref, act0, act1, cot0, cot1, core_ref, send_ref, left_ref):
    hidden = act0.shape[1] // 2
    part = hidden // 4
    for slot in range(2):
        value = products(
            (act0, act1), (cot0, cot1), slice(slot * hidden + hidden // 2, (slot + 1) * hidden)
        )
        to = slice(slot * part, (slot + 1) * part)
        send_ref[to, :] = (value[part:] + core_ref[to, :].astype(f32)).astype(bf16)
        left_ref[to, :] = value[:part] + core_ref[2 * part + to.start : 2 * part + to.stop, :].astype(
            f32
        )


def down_step(flag_ref, left_ref, received_ref, own_ref, send_ref):
    rows = own_ref.shape[0] // 2
    for slot in range(2):
        to = slice(slot * rows, (slot + 1) * rows)
        own = slice(2 * slot * rows, (2 * slot + 1) * rows)
        send = slice((2 * slot + 1) * rows, (2 * slot + 2) * rows)
        own_ref[to, :] = left_ref[own, :] + received_ref[own, :].astype(f32)
        send_ref[to, :] = (left_ref[send, :] + received_ref[send, :].astype(f32)).astype(bf16)


def y_first(value, rows):
    parts = [value[k * rows : (k + 1) * rows] for k in (1, 3, 0, 2)]
    return jnp.concatenate(parts[:2], 0), jnp.concatenate(parts[2:], 0)


def rows_pass(flag_ref, lhs0, lhs1, rhs0, rhs1, out_ref):
    half = lhs0.shape[1] // 2
    value = products((lhs0, lhs1), (rhs0, rhs1), slice(0, half)).astype(bf16)
    send, left = y_first(value, half // 4)
    out_ref[: half // 2, :] = send
    out_ref[half // 2 :, :] = left


def rows_keep(flag_ref, lhs0, lhs1, rhs0, rhs1, core_ref, send_ref, left_ref):
    half = lhs0.shape[1] // 2
    value = products((lhs0, lhs1), (rhs0, rhs1), slice(half, 2 * half))
    send, left = y_first(value, half // 4)
    send_ref[...] = (send + core_ref[: half // 2, :].astype(f32)).astype(bf16)
    left_ref[...] = left + core_ref[half // 2 :, :].astype(f32)


def up_step(flag_ref, left_ref, received_ref, own_ref, send_ref):
    rows = own_ref.shape[0]
    own_ref[...] = left_ref[:rows, :] + received_ref[:rows, :].astype(f32)
    send_ref[...] = (left_ref[rows:, :] + received_ref[rows:, :].astype(f32)).astype(bf16)


def own_slices(flag_ref, down_own, down_received, up_own, up_received, near_ref, far_ref):
    rows, hidden = up_own.shape[0], up_own.shape[1] // 2
    down = down_own[...] + down_received[...].astype(f32)
    up = up_own[...] + up_received[...].astype(f32)
    width = down.shape[1]
    for slot, ref in enumerate((near_ref, far_ref)):
        ref[:, :width] = down[slot * rows : (slot + 1) * rows].astype(ref.dtype)
        ref[:, width:] = up[:, slot * hidden : (slot + 1) * hidden].astype(ref.dtype)


def attn_pass(flag_ref, one0, one1, dqkv0, dqkv1, back0, back1, att0, att1, att2, att3, out_ref):
    half = one0.shape[1] // 2
    width = dqkv0.shape[1]
    channels = att0.shape[1]
    columns = slice(0, half)
    out_ref[:, :width] = products((one0, one1), (dqkv0, dqkv1), columns).astype(bf16)
    for slot, pair in enumerate(((att0, att1), (att2, att3))):
        at = width + slot * channels
        out_ref[:, at : at + channels] = products((back0, back1), pair, columns).astype(bf16)


def attn_keep(
    flag_ref, one0, one1, dqkv0, dqkv1, back0, back1, att0, att1, att2, att3, core_ref, own_ref,
    *send_refs,
):
    half = one0.shape[1] // 2
    rows = half // 4
    width = dqkv0.shape[1]
    channels = att0.shape[1]
    columns = slice(half, 2 * half)
    blocks = [(0, products((one0, one1), (dqkv0, dqkv1), columns))]
    for slot, pair in enumerate(((att0, att1), (att2, att3))):
        blocks.append((width + slot * channels, products((back0, back1), pair, columns)))
    for at, block in blocks:
        to = slice(at, at + block.shape[1])
        block = block + core_ref[:, to].astype(f32)
        own_ref[:, to] = block[:rows]
        for k, ref in enumerate(send_refs):
            ref[:, to] = block[(k + 1) * rows : (k + 2) * rows].astype(bf16)


def attn_own(
    flag_ref, own_ref, r1_ref, r2_ref, r3_ref, param_ref, gains_ref, gains_received, near_ref,
    far_ref,
):
    rows = own_ref.shape[0]
    total = own_ref[...] + (
        r1_ref[...].astype(f32) + r2_ref[...].astype(f32) + r3_ref[...].astype(f32)
    )
    channels = total.shape[1] // 8
    gains = gains_ref[...] + gains_received[...]
    for slot, ref in enumerate((near_ref, far_ref)):
        ref[:rows, : 3 * channels] = total[:, slot * 3 * channels : (slot + 1) * 3 * channels].astype(
            ref.dtype
        )
        ref[:rows, 3 * channels :] = total[
            :, (6 + slot) * channels : (7 + slot) * channels
        ].astype(ref.dtype)
        small = jnp.concatenate(
            [param_ref[:, slot * channels : (slot + 1) * channels], gains], axis=0
        ).astype(ref.dtype)
        count = small.shape[0] // 4
        for quarter in range(4):
            ref[rows : rows + count, quarter * channels : (quarter + 1) * channels] = small[
                quarter * count : (quarter + 1) * count
            ]
        ref[rows + count :, :] = jnp.zeros((ref.shape[0] - rows - count, 4 * channels), ref.dtype)


def add_two(flag_ref, a_ref, b_ref, out_ref):
    out_ref[...] = (a_ref[...].astype(f32) + b_ref[...].astype(f32)).astype(out_ref.dtype)


def add_halves(flag_ref, a_ref, b_ref, left_ref, right_ref):
    width = left_ref.shape[1]
    total = a_ref[...] + b_ref[...].astype(f32)
    left_ref[...] = total[:, :width].astype(bf16)
    right_ref[...] = total[:, width:].astype(bf16)


def split_rows(flag_ref, value_ref, top_ref, bottom_ref):
    rows = top_ref.shape[0]
    top_ref[...] = value_ref[:rows, :]
    bottom_ref[...] = value_ref[rows:, :]


def add_three(flag_ref, a_ref, b_ref, c_ref, out_ref):
    out_ref[...] = (a_ref[...] + b_ref[...] + c_ref[...].astype(f32)).astype(out_ref.dtype)


def sources(flag_ref, even_ref, odd_ref, rows):
    for pair in range(GROUP // 2):
        for side, ref in enumerate((even_ref, odd_ref)):
            source = jnp.bitwise_xor(flag_ref[PLACE], 2 * pair + side)
            yield ref, pair, aligned(source * rows, rows)


def assemble_weight(flag_ref, even_ref, odd_ref, tile_ref, weight_ref, out_ref, qkv_ref):
    split = weight_ref.shape[1]
    for ref, pair, at in sources(flag_ref, even_ref, odd_ref, even_ref.shape[1]):
        weight_ref[at, :] = ref[pair, :, :split]
        out_ref[at, :] = ref[pair, :, split:]
    project(flag_ref, tile_ref, weight_ref, qkv_ref)


def assemble_grad(flag_ref, even_ref, odd_ref, qkv_ref, out_ref, small_ref):
    channels = qkv_ref.shape[2]
    rows = qkv_ref.shape[1] // GROUP
    count = small_ref.shape[0] // 4
    total = None
    for ref, pair, at in sources(flag_ref, even_ref, odd_ref, rows):
        for part in range(3):
            qkv_ref[part, at, :] = ref[
                pair, :rows, part * channels : (part + 1) * channels
            ].astype(f32)
        out_ref[:, at] = ref[pair, :rows, 3 * channels :].astype(f32).T
        term = ref[pair, rows:, :].astype(f32)
        total = term if total is None else total + term
    for quarter in range(4):
        small_ref[quarter * count : (quarter + 1) * count, :] = total[
            :count, quarter * channels : (quarter + 1) * channels
        ]


def stack_two(flag_ref, a_ref, ax_ref, b_ref, by_ref, a_out, b_out):
    a_out[0], a_out[1] = a_ref[...], ax_ref[...]
    b_out[0], b_out[1] = b_ref[...], by_ref[...]


def stack_four(flag_ref, a_ref, b_ref, c_ref, d_ref, out_ref):
    for k, ref in enumerate((a_ref, b_ref, c_ref, d_ref)):
        out_ref[k] = ref[...]


def stack_eight(flag_ref, a_ref, ay_ref, b_ref, bx_ref, out_ref):
    out_ref[0, 0], out_ref[1, 0] = a_ref[0], a_ref[1]
    out_ref[2, 0], out_ref[3, 0] = ay_ref[0], ay_ref[1]
    out_ref[0, 1], out_ref[2, 1] = b_ref[0], b_ref[1]
    out_ref[1, 1], out_ref[3, 1] = bx_ref[0], bx_ref[1]


def place_two(flag_ref, even_ref, odd_ref, a_out, b_out):
    for ref, pair, at in sources(flag_ref, even_ref, odd_ref, even_ref.shape[2]):
        a_out[at, :] = ref[pair, 0].astype(a_out.dtype)
        b_out[at, :] = ref[pair, 1].astype(b_out.dtype)


def place_wide(flag_ref, even_ref, odd_ref, a_out, b_out):
    @pl.when(pl.program_id(0) % 2 == 0)
    def _():
        a_out[...] = even_ref[0, 0].astype(f32)
        b_out[...] = even_ref[0, 1].astype(f32)

    @pl.when(pl.program_id(0) % 2 == 1)
    def _():
        a_out[...] = odd_ref[0, 0].astype(f32)
        b_out[...] = odd_ref[0, 1].astype(f32)


def run_place_wide(flags, even, odd):
    rows, width = even.shape[2:]
    piece = pl.BlockSpec((1, 2, rows, width), lambda j, flag_ref: (j // 2, 0, 0, 0))
    place = pl.BlockSpec(
        (rows, width), lambda j, flag_ref: (jnp.bitwise_xor(flag_ref[PLACE], j), 0)
    )
    out = shape((GROUP * rows, width))
    return pl.pallas_call(
        place_wide,
        grid_spec=pltpu.PrefetchScalarGridSpec(
            num_scalar_prefetch=1,
            grid=(GROUP,),
            in_specs=[piece, piece],
            out_specs=(place, place),
        ),
        out_shape=(out, out),
        compiler_params=pltpu.CompilerParams(vmem_limit_bytes=VMEM_LIMIT),
        cost_estimate=length(0),
    )(flags, even, odd)


class Order:
    def __init__(self):
        self.last = ()

    def __call__(self, *values):
        tied = lax.optimization_barrier((values, self.last))[0]
        return tied[0] if len(tied) == 1 else tied

    def done(self, result):
        self.last = result
        return result


def per_device(
    inputs,
    block_size,
    gain_attn,
    qkv_weight,
    ssm_rate,
    ssm_coef,
    ssm_skip,
    out_weight,
    gain_mlp,
    up_weight,
    down_weight,
    cotangent,
    dp_size,
):
    z = lax.axis_index("mp")
    place = jnp.bitwise_and(lax.axis_index("dp"), GROUP - 1)

    def swap_mp(value, mask):
        return lax.ppermute(value, "mp", [(k, k ^ mask) for k in range(4)])

    def swap_dp(value, mask):
        return lax.ppermute(value, "dp", [(k, k ^ mask) for k in range(dp_size)])

    def gather_by_xor(piece):
        return [piece] + [swap_dp(piece, 2 * k) for k in range(1, GROUP // 2)]

    def low(*dims):
        return shape(dims, bf16)

    def over_groups(own):
        mask = GROUP
        while mask < dp_size:
            own = own + swap_dp(own.astype(bf16), mask).astype(f32)
            mask *= 2
        return own.astype(bf16)

    model_dim = inputs.shape[2]
    channels = qkv_weight.shape[2]
    hidden = up_weight.shape[1]
    wide = 2 * channels
    rows = model_dim // GROUP
    row = inputs[0]
    cot = cotangent[0]
    z_far = jnp.bitwise_xor(z, 2)
    whole = (block_size[0] > HALF).astype(jnp.int32)
    flags = jnp.stack(
        [whole, jnp.right_shift(z, 1), jnp.bitwise_and(z, 1), z, z_far, place]
    ).astype(jnp.int32)
    gain_one = gain_attn[None]
    gain_two = gain_mlp[None]
    order = Order()
    half = shape((HALF, model_dim))
    half_low = shape((HALF, model_dim), bf16)

    normed_one = order.done(call(norm_one, half_low)(flags, row, gain_one))
    paired_one = swap_mp(normed_one, 1)
    qkv_parts = jnp.transpose(qkv_weight, (1, 0, 2))
    ssm_pack = jnp.concatenate(
        [ssm_rate.T, ssm_coef.T, ssm_skip[None], jnp.zeros((15, channels), f32)], 0
    )
    attn_slice, mlp_slice = order.done(
        run_cut_slices(flags, order(qkv_parts), out_weight, up_weight, down_weight, ssm_pack)
    )
    attn_across = swap_mp(attn_slice, 2)
    near_qkv = order.done(jnp.concatenate(list(order(*[qkv_parts[k] for k in range(3)])), 1))

    paired_one, attn_across = order.done(order(paired_one, attn_across))
    attn_own_slice = attn_across[:rows]
    attn_x = swap_dp(attn_own_slice, 2)
    attn_y = swap_dp(attn_own_slice, 4)
    mlp_across = swap_mp(order(mlp_slice), 2)
    paired_cot = swap_mp(order(cot), 1)
    ssm_both = call(join_ssm, shape((48, wide)))(flags, ssm_pack, attn_across)
    rate_t, coef_t, skip_t = ssm_both[:16], ssm_both[16:32], ssm_both[32:33]
    tile_one, one_sent, second_local, handed = order.done(
        call(
            ssm_forward,
            (
                shape((2, HALF, model_dim), bf16),
                shape((2, HALF, model_dim), bf16),
                shape((CTX, wide)),
                shape((CTX + 6 * STATES, wide), bf16),
            ),
            scratch=[pltpu.VMEM((2 * HALF, wide), f32)],
        )(flags, normed_one, order(paired_one), rate_t, coef_t, skip_t)
    )
    handed = lax.ppermute(handed, "mp", [(0, 2), (1, 3)])

    qkv_shape = shape((2, HALF, 3 * channels), bf16)
    att_shape = shape((2, HALF, channels), bf16)
    attn_x = order.done(order(attn_x))
    attn_xy = swap_dp(attn_x, 4)
    qkv_near = order.done(call(project, qkv_shape)(flags, order(tile_one), near_qkv))
    attn_y, paired_cot = order.done(order(attn_y, paired_cot))
    even = order.done(
        call(stack_four, shape((4,) + attn_x.shape, bf16))(
            flags, attn_own_slice, attn_x, attn_y, order(attn_xy)
        )
    )
    odd_part = swap_dp(even, 1)
    slice_shape = low(rows, model_dim)
    mlp_up, mlp_down = order.done(
        call(split_rows, (slice_shape, slice_shape))(flags, order(mlp_across))
    )
    mlp_up_x = swap_dp(mlp_up, 2)
    mlp_down_y = swap_dp(mlp_down, 4)
    ctx_first, ctx_second, enter_state = order.done(
        call(
            ssm_carry_in,
            (shape((CTX, wide), bf16), shape((CTX, wide), bf16), shape((2, STATES, wide))),
            scratch=[pltpu.VMEM((CTX, wide), f32)],
            micros=6,
        )(flags, second_local, order(handed), rate_t, coef_t)
    )
    att_near = order.done(
        call(attention_near, att_shape)(flags, order(qkv_near), ctx_first, ctx_second)
    )
    far_qkv, far_out, qkv_far = order.done(
        call(
            assemble_weight,
            (
                shape((model_dim, 3 * channels), bf16),
                shape((model_dim, channels), bf16),
                qkv_shape,
            ),
        )(flags, even, order(odd_part), tile_one)
    )
    att_far, out_own, out_send = order.done(
        call(attention_far, (att_shape, half, half_low))(
            flags, order(qkv_far), ctx_first, ctx_second, att_near, out_weight, far_out
        )
    )
    out_received = swap_mp(out_send, 1)
    pair_shape = low(2, rows, model_dim)
    mlp_up_two, mlp_down_two = order.done(
        call(stack_two, (pair_shape, pair_shape), micros=3)(
            flags, mlp_up, order(mlp_up_x), mlp_down, order(mlp_down_y)
        )
    )
    mlp_up_y = swap_dp(mlp_up_two, 4)
    mlp_down_x = swap_dp(mlp_down_two, 2)
    middle, normed_two = order.done(
        call(norm_two, (half, half_low), micros=3)(
            flags, row, out_own, order(out_received), gain_two
        )
    )

    paired_two = swap_mp(normed_two, 1)
    eight_shape = low(GROUP // 2, 2, rows, model_dim)
    mlp_even = order.done(
        call(stack_eight, eight_shape, micros=1)(
            flags, mlp_up_two, order(mlp_up_y), mlp_down_two, order(mlp_down_x)
        )
    )
    mlp_odd = swap_dp(mlp_even, 1)
    paired_two = order(paired_two)
    warm = order.done(
        call(touch, shape((8, 128), bf16), micros=12)(
            flags, up_weight, down_weight, cot, paired_cot, paired_two
        )
    )
    up_far, down_far = order.done(
        call(place_two, (low(model_dim, hidden), low(hidden, model_dim)))(
            flags, mlp_even, order(mlp_odd)
        )
    )
    mlp = (up_weight, down_weight, up_far, down_far)
    act_other, gate_other, two_other, down_send, back_send = order.done(
        run_feed_forward(flags, order(paired_two), paired_cot, *mlp, bf16)
    )
    back_received = swap_mp(back_send, 1)
    act_own, gate_own, two_own, down_own, back_own = order.done(
        run_feed_forward(flags, order(normed_two), cot, *mlp, f32)
    )

    side = model_dim // 2
    acts = (act_own, act_other, cot, paired_cot)
    passed = order.done(call(down_pass, low(hidden, model_dim))(flags, order(act_own), *acts[1:]))
    down_core = swap_dp(passed, 1)
    ups = (two_own, two_other, gate_own, gate_other)
    passed = order.done(call(rows_pass, low(side, 2 * hidden))(flags, order(two_own), *ups[1:]))
    up_core = swap_dp(passed, 1)
    middle_grad, attn_grad, gain_mlp_grad = order.done(
        call(norm_two_back, (half, half_low, shape((1, model_dim))), micros=12)(
            flags, middle, back_own, order(back_received), cot, gain_two, warm
        )
    )
    paired_back = swap_mp(attn_grad, 1)
    down_send_x, down_left = order.done(
        call(down_keep, (low(side, model_dim), shape((side, model_dim))))(
            flags, *acts, order(down_core)
        )
    )
    down_x = swap_dp(down_send_x, 2)
    up_send_y, up_left = order.done(
        call(rows_keep, (low(side // 2, 2 * hidden), shape((side // 2, 2 * hidden))))(
            flags, *ups, order(up_core)
        )
    )
    up_y = swap_dp(up_send_y, 4)

    att_grad, back_sent = order.done(
        call(
            attended_grads,
            (shape((2, HALF, wide), bf16), shape((2, HALF, model_dim), bf16)),
            micros=4,
        )(flags, attn_grad, order(paired_back), out_weight, far_out)
    )
    down_received = swap_mp(order(down_send), 1)
    dqkv, second_grad, returned = order.done(
        call(
            attention_backward,
            (
                shape((2, HALF, 6 * channels), bf16),
                shape((CTX, wide)),
                shape((CTX + 3 * STATES, wide), bf16),
            ),
        )(flags, qkv_near, qkv_far, ctx_first, ctx_second, order(att_grad), rate_t)
    )
    returned = lax.ppermute(returned, "mp", [(2, 0), (3, 1)])
    one_total = order.done(
        call(qkv_back, shape((2, HALF, model_dim)))(flags, order(dqkv), near_qkv, far_qkv)
    )
    attns = (
        one_sent[0], one_sent[1], dqkv[0], dqkv[1], back_sent[0], back_sent[1],
        att_near[0], att_near[1], att_far[0], att_far[1],
    )
    passed = order.done(
        call(attn_pass, low(side, 8 * channels))(flags, order(attns[0]), *attns[1:])
    )
    attn_core = swap_dp(passed, 1)
    down_mine, down_send_y = order.done(
        call(down_step, (shape((2 * rows, model_dim)), low(2 * rows, model_dim)))(
            flags, down_left, order(down_x)
        )
    )
    down_y = swap_dp(down_send_y, 4)
    up_mine, up_send_x = order.done(
        call(up_step, (shape((rows, 2 * hidden)), low(rows, 2 * hidden)))(
            flags, up_left, order(up_y)
        )
    )
    up_x = swap_dp(up_send_x, 2)
    one_own, one_send, last_grad = order.done(
        call(
            ssm_signal_grad,
            (half, half_low, shape((CTX, wide))),
            scratch=[pltpu.VMEM((2 * HALF, wide), f32), pltpu.VMEM((HALF, model_dim), f32)],
            micros=30,
        )(flags, second_grad, order(returned), rate_t, coef_t, skip_t, one_total)
    )
    one_received = swap_mp(one_send, 1)
    output = order.done(
        call(add_three, half_low)(flags, middle, down_own, order(down_received))
    )
    attn_mine, *attn_sends = order.done(
        call(attn_keep, (shape((rows, 8 * channels)),) + (low(rows, 8 * channels),) * 3)(
            flags, *attns, order(attn_core)
        )
    )
    attn_sent = [swap_dp(part, SENT[5 + k]) for k, part in enumerate(attn_sends)]
    mlp_width = model_dim + hidden
    mlp_near, mlp_send = order.done(
        call(own_slices, (shape((rows, mlp_width)), low(rows, mlp_width)))(
            flags, down_mine, order(down_y), up_mine, order(up_x)
        )
    )
    mlp_received = swap_mp(mlp_send, 2)
    param_grad = order.done(
        call(
            ssm_param_grad,
            shape((40, wide)),
            scratch=[pltpu.VMEM((2 * HALF, wide), f32)],
            micros=3,
        )(flags, order(tile_one), second_grad, last_grad, enter_state, rate_t, coef_t)
    )
    input_grad, gains = order.done(
        call(norm_one_back, (half, shape((2 * model_dim // channels, channels))))(
            flags, row, one_own, order(one_received), middle_grad, gain_one, gain_mlp_grad
        )
    )
    gains_received = swap_mp(gains, 1)
    down_mine, up_mine = order.done(
        call(add_halves, (slice_shape, slice_shape))(flags, mlp_near, order(mlp_received))
    )
    down_mine, up_mine = over_groups(down_mine), over_groups(up_mine)
    down_x = swap_dp(down_mine, 2)
    up_y = swap_dp(up_mine, 4)
    slice_rows = rows + 16
    *attn_sent, gains_received = order(*attn_sent, gains_received)
    attn_near, attn_send = order.done(
        call(attn_own, (shape((slice_rows, 4 * channels)), low(slice_rows, 4 * channels)))(
            flags, attn_mine, *attn_sent, param_grad, gains, gains_received
        )
    )
    attn_received = swap_mp(attn_send, 2)
    down_two, up_two = order.done(
        call(stack_two, (pair_shape, pair_shape), micros=3)(
            flags, down_mine, order(down_x), up_mine, order(up_y)
        )
    )
    down_y = swap_dp(down_two, 4)
    up_x = swap_dp(up_two, 2)
    attn_slice_grad = order.done(
        call(add_two, low(slice_rows, 4 * channels), micros=3)(
            flags, attn_near, order(attn_received)
        )
    )
    attn_slice_grad = over_groups(attn_slice_grad)
    attn_sent = [swap_dp(attn_slice_grad, 2 * k) for k in range(1, GROUP // 2)]
    even = order.done(
        call(stack_four, low(4, slice_rows, 4 * channels))(
            flags, attn_slice_grad, *order(*attn_sent)
        )
    )
    odd_part = swap_dp(even, 1)
    mlp_even = order.done(
        call(stack_eight, eight_shape, micros=5)(
            flags, down_two, order(down_y), up_two, order(up_x)
        )
    )
    mlp_odd = swap_dp(mlp_even, 1)
    qkv_grad, out_grad, small = order.done(
        call(
            assemble_grad,
            (
                shape((3, model_dim, channels)),
                shape(out_weight.shape),
                shape((48, channels)),
            ),
            micros=6,
        )(flags, even, order(odd_part))
    )
    down_grad, up_grad = run_place_wide(flags, mlp_even, order(mlp_odd))
    gains = small[40:].reshape(2, model_dim)
    return (
        output[None],
        input_grad[None],
        gains[0],
        jnp.transpose(qkv_grad, (1, 0, 2)),
        small[:16].T,
        small[16:32].T,
        small[32],
        out_grad,
        gains[1],
        up_grad,
        down_grad,
    )


def solution(mesh):
    return jax.shard_map(
        partial(per_device, dp_size=mesh.shape["dp"]),
        mesh=mesh,
        in_specs=(
            P("dp", "mp", None),
            P("dp"),
            P(),
            P(None, None, "mp"),
            P("mp", None),
            P("mp", None),
            P("mp"),
            P("mp", None),
            P(),
            P(None, "mp"),
            P("mp", None),
            P("dp", "mp", None),
        ),
        out_specs=(
            P("dp", "mp", None),
            P("dp", "mp", None),
            P(),
            P(None, None, "mp"),
            P("mp", None),
            P("mp", None),
            P("mp"),
            P("mp", None),
            P(),
            P(None, "mp"),
            P("mp", None),
        ),
        check_vma=False,
    )
```

```python
from functools import partial
import math

import jax
import jax.numpy as jnp
from jax import lax
from jax.experimental import pallas as pl
from jax.experimental.pallas import tpu as pltpu
from jax.sharding import PartitionSpec as P

HD = 128
CTX = 128
HALF = 256
STATES = 16
GROUP = 8

f32 = jnp.float32
bf16 = jnp.bfloat16
epsilon = 1e-05
masked_score = -1e30
score_scale = 1.0 / math.sqrt(HD)
VMEM_LIMIT = 16 * 1024 * 1024

NT = (((1,), (1,)), ((), ()))
TN = (((0,), (0,)), ((), ()))
NN = (((1,), (0,)), ((), ()))

WHOLE, LATE, ODD, NEAR, FAR, PLACE = range(6)


def mm(a, b, dims=NN):
    return lax.dot_general(a, b, dims, preferred_element_type=f32)


def shape(dims, dtype=f32):
    return jax.ShapeDtypeStruct(dims, dtype)


def length(micros):
    return pl.CostEstimate(flops=int(micros * 1e9), bytes_accessed=0, transcendentals=0)


def call(kernel, out_shape, scratch=(), micros=0):
    def run(flags, *args):
        vmem = pl.BlockSpec(memory_space=pltpu.VMEM)
        return pl.pallas_call(
            kernel,
            out_shape=out_shape,
            in_specs=[pl.BlockSpec(memory_space=pltpu.SMEM)] + [vmem] * len(args),
            out_specs=jax.tree.map(lambda _: vmem, out_shape),
            scratch_shapes=scratch,
            compiler_params=pltpu.CompilerParams(vmem_limit_bytes=VMEM_LIMIT),
            cost_estimate=length(micros),
        )(flags, *args)

    return run


SENT = (1, 5, 3, 7, 0, 4, 2, 6)


def in_sent_order(flag_ref, value_ref, out_ref, masks=SENT):
    width = value_ref.shape[1] // GROUP
    for k, mask in enumerate(masks):
        source = jnp.bitwise_xor(flag_ref[PLACE], mask)
        out_ref[:, k * width : (k + 1) * width] = value_ref[:, aligned(source * width, width)]


def aligned(start, size):
    return pl.ds(pl.multiple_of(start, size), size)


def cut_slices(
    flag_ref, qkv_ref, out_ref, up_ref, down_ref, rate_ref, coef_ref, skip_ref, attn_ref, up_slice,
    down_slice, ssm_ref, out_slice, *sems,
):
    rows = up_slice.shape[0]
    channels = out_slice.shape[0]
    count = ssm_ref.shape[0]
    ssm_ref[:STATES, :] = rate_ref[...]
    ssm_ref[STATES : 2 * STATES, :] = coef_ref[...]
    ssm_ref[2 * STATES :, :] = jnp.zeros((count - 2 * STATES, channels), f32)
    ssm_ref[2 * STATES : 2 * STATES + 1, :] = skip_ref[...]
    for k, part in enumerate(split_three(ssm_ref[...])):
        attn_ref[rows : rows + count, k * channels : (k + 1) * channels] = part
    attn_ref[rows : rows + count, 3 * channels :] = jnp.zeros((count, channels), bf16)
    at = aligned(flag_ref[PLACE] * rows, rows)
    copies = [
        pltpu.make_async_copy(
            qkv_ref.at[part, at, :],
            attn_ref.at[:rows, part * channels : (part + 1) * channels],
            sems[part],
        )
        for part in range(3)
    ] + [
        pltpu.make_async_copy(out_ref.at[:, at], out_slice, sems[3]),
        pltpu.make_async_copy(up_ref.at[at, :], up_slice, sems[4]),
        pltpu.make_async_copy(down_ref.at[at, :], down_slice, sems[5]),
    ]
    for copy in copies:
        copy.start()
    for copy in copies:
        copy.wait()
    attn_ref[:rows, 3 * channels :] = out_slice[...].T


def join_ssm(flag_ref, own_ref, across_ref, out_ref):
    channels = own_ref.shape[1]
    start = across_ref.shape[0] - own_ref.shape[0]
    out_ref[:, :channels] = own_ref[...]
    parts = [across_ref[start:, k * channels : (k + 1) * channels].astype(f32) for k in range(3)]
    out_ref[:, channels:] = (parts[0] + parts[1]) + parts[2]


def run_cut_slices(flags, qkv_parts, out_weight, up_weight, down_weight, *ssm_parts):
    channels = qkv_parts.shape[2]
    width = out_weight.shape[1]
    rows = width // GROUP
    vmem = pl.BlockSpec(memory_space=pltpu.VMEM)
    return pl.pallas_call(
        cut_slices,
        in_specs=[pl.BlockSpec(memory_space=pltpu.SMEM)]
        + [pl.BlockSpec(memory_space=pltpu.HBM)] * 4
        + [vmem] * 3,
        out_specs=(vmem,) * 4,
        out_shape=(
            shape((rows + 48, 4 * channels), bf16),
            shape((rows, width), bf16),
            shape((rows, width), bf16),
            shape((48, channels)),
        ),
        scratch_shapes=[pltpu.VMEM((channels, rows), bf16)] + [pltpu.SemaphoreType.DMA] * 6,
        compiler_params=pltpu.CompilerParams(vmem_limit_bytes=56 * 1024 * 1024),
        cost_estimate=length(0),
    )(flags, qkv_parts, out_weight, up_weight, down_weight, *ssm_parts)


def normalise(values):
    mean = jnp.mean(values, axis=-1, keepdims=True)
    centred = values - mean
    spread = jnp.mean(centred * centred, axis=-1, keepdims=True)
    inverse = lax.rsqrt(spread + epsilon)
    return centred * inverse, inverse


def normalise_back(grad, gain, hat, inverse):
    inner = grad * gain
    return (
        inner
        - jnp.mean(inner, axis=-1, keepdims=True)
        - hat * jnp.mean(inner * hat, axis=-1, keepdims=True)
    ) * inverse


def by_rows(body, rows, block=64):
    for k in range(rows // block):
        body(slice(k * block, (k + 1) * block))


def norm_one(flag_ref, x_ref, gain_ref, out_ref):
    def body(at):
        hat, _ = normalise(x_ref[at, :].astype(f32))
        out_ref[at, :] = (hat * gain_ref[...]).astype(bf16)

    by_rows(body, x_ref.shape[0])


def touch(flag_ref, up_ref, down_ref, cot_ref, paired_ref, rows_ref, out_ref):
    out_ref[...] = (
        (up_ref[:8, :128] + down_ref[:8, :128])
        + (cot_ref[:8, :128] + paired_ref[:8, :128])
        + rows_ref[:8, :128]
    )


def norm_two(flag_ref, x_ref, own_ref, received_ref, gain_ref, middle_ref, out_ref):
    def body(at):
        middle = x_ref[at, :].astype(f32) + own_ref[at, :] + received_ref[at, :].astype(f32)
        middle_ref[at, :] = middle
        hat, _ = normalise(middle)
        out_ref[at, :] = (hat * gain_ref[...]).astype(bf16)

    by_rows(body, x_ref.shape[0])


def norm_two_back(
    flag_ref, middle_ref, own_ref, received_ref, cot_ref, gain_ref, warm_ref, grad_ref, low_ref,
    gain_out_ref,
):
    sums = []

    def body(at):
        hat, inverse = normalise(middle_ref[at, :])
        grad = own_ref[at, :] + received_ref[at, :].astype(f32)
        sums.append(jnp.sum(grad * hat, axis=0, keepdims=True))
        total = cot_ref[at, :].astype(f32) + normalise_back(grad, gain_ref[...], hat, inverse)
        grad_ref[at, :] = total
        low_ref[at, :] = total.astype(bf16)

    by_rows(body, middle_ref.shape[0])
    gain_out_ref[...] = sum(sums)


def norm_one_back(
    flag_ref, x_ref, own_ref, received_ref, middle_ref, gain_ref, gain_two_grad_ref, grad_ref,
    gain_out_ref,
):
    sums = []

    def body(at):
        hat, inverse = normalise(x_ref[at, :].astype(f32))
        grad = own_ref[at, :] + received_ref[at, :].astype(f32)
        sums.append(jnp.sum(grad * hat, axis=0, keepdims=True))
        grad_ref[at, :] = middle_ref[at, :] + normalise_back(grad, gain_ref[...], hat, inverse)

    by_rows(body, x_ref.shape[0])
    width = gain_out_ref.shape[1]
    pieces = x_ref.shape[1] // width
    for which, value in enumerate((sum(sums), gain_two_grad_ref[...])):
        for k in range(pieces):
            row = which * pieces + k
            gain_out_ref[row : row + 1, :] = value[:, k * width : (k + 1) * width]


def split_three(value):
    high = value.astype(bf16)
    rest = value - high.astype(f32)
    middle = rest.astype(bf16)
    return [high, middle, (rest - middle.astype(f32)).astype(bf16)]


def join_three(ref, start, lanes):
    parts = [ref[start + k * STATES : start + (k + 1) * STATES, lanes] for k in range(3)]
    return (parts[0].astype(f32) + parts[1].astype(f32)) + parts[2].astype(f32)


def load_signal(flag_ref, tile_ref, xs):
    channels = xs.shape[1] // 2
    for half in range(2):
        source = jnp.bitwise_xor(flag_ref[ODD], half)
        for slot, name in enumerate((NEAR, FAR)):
            xs[half * HALF : (half + 1) * HALF, slot * channels : (slot + 1) * channels] = tile_ref[
                source, :, aligned(flag_ref[name] * channels, channels)
            ].astype(f32)


def ssm_forward(
    flag_ref, own_ref, other_ref, rate_ref, coef_ref, skip_ref, tile_ref, sent_ref,
    second_ref, handed_ref, xs,
):
    tile_ref[0] = own_ref[...]
    tile_ref[1] = other_ref[...]
    in_sent_order(flag_ref, own_ref, sent_ref.at[0])
    in_sent_order(flag_ref, other_ref, sent_ref.at[1])
    load_signal(flag_ref, tile_ref, xs)
    decay = jnp.exp(-rate_ref[...])
    coef = coef_ref[...]
    skip = skip_ref[...]

    def step(eight, state, chunk):
        x8 = xs[aligned((chunk * 16 + eight) * 8, 8), :]
        rows = []
        for k in range(8):
            state = decay * state + x8[k : k + 1]
            if chunk % 2:
                rows.append(jnp.sum(coef * state, axis=0, keepdims=True))
        if chunk % 2:
            y8 = jnp.concatenate(rows, axis=0) + skip * x8
            at = aligned(eight * 8, 8)
            if chunk == 1:
                second_ref[at, :] = y8
            else:
                xs[at, :] = y8
        return state

    state = jnp.zeros_like(decay)
    for chunk in range(4):
        state = lax.fori_loop(0, 16, partial(step, chunk=chunk), state)
    handed_ref[:CTX, :] = xs[:CTX, :].astype(bf16)
    for k, part in enumerate(split_three(state)):
        handed_ref[CTX + k * STATES : CTX + (k + 1) * STATES, :] = part


def project(flag_ref, tile_ref, weight_ref, qkv_ref):
    for half in range(2):
        qkv_ref[half] = mm(tile_ref[half], weight_ref[...]).astype(bf16)


def ssm_carry_in(
    flag_ref, local_ref, handed_ref, rate_ref, coef_ref, first_ref, second_ref, enter_ref, acc
):
    channels = rate_ref.shape[1] // 2
    for slot in range(2):
        to = slice(slot * channels, (slot + 1) * channels)
        source = slice((1 - slot) * channels, (2 - slot) * channels)
        first_ref[:, to] = handed_ref[:CTX, source]
        enter_ref[:, to] = join_three(handed_ref, CTX, source)
    rate = rate_ref[...]
    decay = jnp.exp(-rate)
    coef = coef_ref[...]

    def step(eight, state):
        rows = []
        for k in range(8):
            rows.append(jnp.sum(coef * state, axis=0, keepdims=True))
            state = decay * state
        acc[aligned(eight * 8, 8), :] = jnp.concatenate(rows, axis=0)
        return state

    lax.fori_loop(0, 16, step, enter_ref[...] * jnp.exp(-129.0 * rate))
    second_ref[...] = (local_ref[...] + acc[...]).astype(bf16)


def qkv_back(flag_ref, dqkv_ref, near_weight_ref, far_weight_ref, out_ref):
    split = near_weight_ref.shape[1]
    for half in range(2):
        out_ref[half] = mm(dqkv_ref[half, :, :split], near_weight_ref[...], NT) + mm(
            dqkv_ref[half, :, split:], far_weight_ref[...], NT
        )


def ssm_signal_grad(
    flag_ref, near_ref, returned_ref, rate_ref, coef_ref, skip_ref, total_ref, own_ref, send_ref,
    last_ref, adjoint_ref, rows_out, total,
):
    channels = rate_ref.shape[1] // 2
    adjoints = []
    for slot in range(2):
        to = slice(slot * channels, (slot + 1) * channels)
        source = slice((1 - slot) * channels, (2 - slot) * channels)
        last_ref[:, to] = returned_ref[:CTX, source].astype(f32)
        adjoints.append(join_three(returned_ref, CTX, source))
    decay = jnp.exp(-rate_ref[...])
    coef = coef_ref[...]
    skip = skip_ref[...]

    def step(j, adjoint, chunk):
        eight = 15 - j
        at = aligned(eight * 8, 8)
        if chunk % 2:
            g8 = (near_ref, last_ref)[chunk // 2][at, :]
        rows = [None] * 8
        for k in range(7, -1, -1):
            adjoint = decay * adjoint
            if chunk % 2:
                adjoint = adjoint + g8[k : k + 1]
            rows[k] = jnp.sum(coef * adjoint, axis=0, keepdims=True)
        y8 = jnp.concatenate(rows, axis=0)
        if chunk % 2:
            y8 = y8 + skip * g8
        rows_out[aligned((chunk * 16 + eight) * 8, 8), :] = y8
        return adjoint

    adjoint = jnp.concatenate(adjoints, axis=1)
    adjoint_ref[...] = adjoint
    for chunk in (3, 2, 1, 0):
        adjoint = lax.fori_loop(0, 16, partial(step, chunk=chunk), adjoint)
    for half in (1, 0):
        total[...] = total_ref[half]
        source = aligned(jnp.bitwise_xor(flag_ref[ODD], half) * HALF, HALF)
        for slot, name in enumerate((NEAR, FAR)):
            total[:, aligned(flag_ref[name] * channels, channels)] += rows_out[
                source, slot * channels : (slot + 1) * channels
            ]
        if half:
            send_ref[...] = total[...].astype(bf16)
        else:
            own_ref[...] = total[...]


def ssm_param_grad(
    flag_ref, tile_ref, near_ref, last_ref, enter_ref, adjoint_ref, rate_ref, coef_ref, out_ref, xs
):
    load_signal(flag_ref, tile_ref, xs)
    decay = jnp.exp(-rate_ref[...])
    zero = jnp.zeros_like(decay)

    def step(eight, carry, chunk):
        state, slope, for_coef, for_rate = carry
        x8 = xs[aligned((chunk * 16 + eight) * 8, 8), :]
        if chunk % 2:
            g8 = (near_ref, last_ref)[chunk // 2][aligned(eight * 8, 8), :]
        for k in range(8):
            slope = decay * (slope + state)
            state = decay * state + x8[k : k + 1]
            if chunk % 2:
                for_coef = for_coef + state * g8[k : k + 1]
                for_rate = for_rate + slope * g8[k : k + 1]
        return state, slope, for_coef, for_rate

    carry = (enter_ref[...], zero, zero, zero)
    for chunk in range(4):
        carry = lax.fori_loop(0, 16, partial(step, chunk=chunk), carry)
    for_rate = carry[3] + decay * adjoint_ref[...] * carry[1]
    out_ref[:STATES, :] = -coef_ref[...] * for_rate
    out_ref[STATES : 2 * STATES, :] = carry[2]
    skip = jnp.sum(xs[CTX : 2 * CTX] * near_ref[...], axis=0, keepdims=True) + jnp.sum(
        xs[3 * CTX :] * last_ref[...], axis=0, keepdims=True
    )
    out_ref[2 * STATES :, :] = jnp.concatenate(
        [skip, jnp.zeros((out_ref.shape[0] - 2 * STATES - 1, skip.shape[1]), f32)], axis=0
    )


def causal(scores):
    rows = lax.broadcasted_iota(jnp.int32, scores.shape, 0)
    cols = lax.broadcasted_iota(jnp.int32, scores.shape, 1)
    return jnp.where(cols <= rows, scores, masked_score)


def softmax_parts(parts):
    top = parts[0].max(axis=-1, keepdims=True)
    for part in parts[1:]:
        top = jnp.maximum(top, part.max(axis=-1, keepdims=True))
    weights = [jnp.exp(part - top) for part in parts]
    total = weights[0].sum(axis=-1, keepdims=True)
    for weight in weights[1:]:
        total = total + weight.sum(axis=-1, keepdims=True)
    return [weight / total for weight in weights]


def block_probs(q0, q1, k0, k1, first, second, whole, late):
    has_first = late > 0
    is_whole = whole > 0
    chosen = jnp.where(is_whole, first, second)
    chosen_ok = jnp.logical_or(jnp.logical_not(is_whole), has_first)
    s00 = causal(mm(q0, k0, NT) * score_scale)
    s0c = jnp.where(has_first, mm(q0, first, NT) * score_scale, masked_score)
    s11 = causal(mm(q1, k1, NT) * score_scale)
    s10 = jnp.where(is_whole, mm(q1, k0, NT) * score_scale, masked_score)
    s1c = jnp.where(chosen_ok, mm(q1, chosen, NT) * score_scale, masked_score)
    return softmax_parts([s00, s0c]), softmax_parts([s11, s10, s1c]), chosen


def head_parts(qkv_ref, head, half):
    channels = qkv_ref.shape[2] // 3
    return [
        qkv_ref[half, :, part * channels + head * HD : part * channels + (head + 1) * HD]
        for part in range(3)
    ]


def attend(flag_ref, qkv_ref, first_ref, second_ref, att_ref, slot):
    half0 = flag_ref[ODD]
    half1 = 1 - half0
    heads = qkv_ref.shape[2] // (3 * HD)
    for head in range(heads):
        q0, k0, v0 = head_parts(qkv_ref, head, half0)
        q1, k1, v1 = head_parts(qkv_ref, head, half1)
        at = slice((slot * heads + head) * HD, (slot * heads + head + 1) * HD)
        first = first_ref[:, at]
        second = second_ref[:, at]
        (p00, p0c), (p11, p10, p1c), chosen = block_probs(
            q0, q1, k0, k1, first, second, flag_ref[WHOLE], flag_ref[LATE]
        )
        to = slice(head * HD, (head + 1) * HD)
        att_ref[half0, :, to] = (mm(p00.astype(bf16), v0) + mm(p0c.astype(bf16), first)).astype(
            bf16
        )
        att_ref[half1, :, to] = (
            mm(p11.astype(bf16), v1) + mm(p10.astype(bf16), v0) + mm(p1c.astype(bf16), chosen)
        ).astype(bf16)


def attention_near(flag_ref, qkv_ref, first_ref, second_ref, att_ref):
    attend(flag_ref, qkv_ref, first_ref, second_ref, att_ref, 0)


def attention_far(
    flag_ref, qkv_ref, first_ref, second_ref, near_ref, out_near_ref, out_far_ref, att_ref, own_ref,
    send_ref,
):
    attend(flag_ref, qkv_ref, first_ref, second_ref, att_ref, 1)

    def projected(half):
        return mm(near_ref[half], out_near_ref[...]) + mm(att_ref[half], out_far_ref[...], NT)

    send_ref[...] = projected(1).astype(bf16)
    own_ref[...] = projected(0)


def attended_grads(flag_ref, own_ref, other_ref, out_near_ref, out_far_ref, grad_ref, sent_ref):
    split = out_near_ref.shape[0]
    for half, ref in enumerate((own_ref, other_ref)):
        grad_ref[half, :, :split] = mm(ref[...], out_near_ref[...], NT).astype(bf16)
        grad_ref[half, :, split:] = mm(ref[...], out_far_ref[...]).astype(bf16)
        in_sent_order(flag_ref, ref, sent_ref.at[half])


def attention_backward(
    flag_ref, near_ref, far_ref, first_ref, second_ref, grad_ref, rate_ref, out_ref, second_out_ref,
    returned_ref,
):
    half0 = flag_ref[ODD]
    half1 = 1 - half0
    is_whole = flag_ref[WHOLE] > 0
    heads = near_ref.shape[2] // (3 * HD)
    for index in range(2 * heads):
        slot, head = index // heads, index % heads
        qkv_ref = (near_ref, far_ref)[slot]
        q0, k0, v0 = head_parts(qkv_ref, head, half0)
        q1, k1, v1 = head_parts(qkv_ref, head, half1)
        at = slice(index * HD, (index + 1) * HD)
        g0 = grad_ref[half0, :, at]
        g1 = grad_ref[half1, :, at]
        first = first_ref[:, at]
        second = second_ref[:, at]
        early, later, chosen = block_probs(
            q0, q1, k0, k1, first, second, flag_ref[WHOLE], flag_ref[LATE]
        )

        def score_grads(probs, rows, values):
            prob_grads = [mm(rows, v, NT) for v in values]
            centre = sum((p * d).sum(axis=-1, keepdims=True) for p, d in zip(probs, prob_grads))
            return [(p * (d - centre)).astype(bf16) for p, d in zip(probs, prob_grads)]

        d00, d0c = score_grads(early, g0, (v0, first))
        d11, d10, d1c = score_grads(later, g1, (v1, v0, chosen))
        p00, p0c = [p.astype(bf16) for p in early]
        p11, p10, p1c = [p.astype(bf16) for p in later]
        base = slot * 3 * heads * HD + head * HD
        for_q, for_k, for_v = [
            slice(base + part * heads * HD, base + part * heads * HD + HD) for part in range(3)
        ]
        out_ref[half0, :, for_q] = ((mm(d00, k0) + mm(d0c, first)) * score_scale).astype(bf16)
        out_ref[half1, :, for_q] = (
            (mm(d11, k1) + mm(d10, k0) + mm(d1c, chosen)) * score_scale
        ).astype(bf16)
        out_ref[half0, :, for_k] = ((mm(d00, q0, TN) + mm(d10, q1, TN)) * score_scale).astype(bf16)
        out_ref[half1, :, for_k] = (mm(d11, q1, TN) * score_scale).astype(bf16)
        out_ref[half0, :, for_v] = (mm(p00, g0, TN) + mm(p10, g1, TN)).astype(bf16)
        out_ref[half1, :, for_v] = mm(p11, g1, TN).astype(bf16)
        from_early = mm(d0c, q0, TN) * score_scale + mm(p0c, g0, TN)
        from_later = mm(d1c, q1, TN) * score_scale + mm(p1c, g1, TN)
        returned_ref[:CTX, at] = (from_early + jnp.where(is_whole, from_later, 0.0)).astype(bf16)
        second_out_ref[:, at] = jnp.where(is_whole, 0.0, from_later)

    rate = rate_ref[...]
    decay = jnp.exp(-rate)

    def step(j, adjoint):
        g8 = second_out_ref[aligned((15 - j) * 8, 8), :]
        for k in range(7, -1, -1):
            adjoint = decay * adjoint + g8[k : k + 1]
        return adjoint

    adjoint = lax.fori_loop(0, 16, step, jnp.zeros_like(rate)) * jnp.exp(-float(CTX) * rate)
    for k, part in enumerate(split_three(adjoint)):
        returned_ref[CTX + k * STATES : CTX + (k + 1) * STATES, :] = part


def feed_forward(
    flag_ref, n_ref, c_ref, up0_ref, down0_ref, up1_ref, down1_ref, act_ref, gate_ref, sent_ref,
    down_out_ref, back_out_ref, acc_down, acc_back,
):
    step = pl.program_id(0)
    steps = pl.num_programs(0)
    per = steps // 2

    @pl.when(step == 0)
    def _():
        acc_down[...] = jnp.zeros_like(acc_down)
        acc_back[...] = jnp.zeros_like(acc_back)
        in_sent_order(flag_ref, n_ref, sent_ref)

    def body(up, down, slot):
        gate = mm(n_ref[...], up)
        cdf = 0.5 * (1.0 + lax.erf(gate * (1.0 / math.sqrt(2.0))))
        act = (gate * cdf).astype(bf16)
        slope = cdf + gate * jnp.exp(-0.5 * gate * gate) * (1.0 / math.sqrt(2.0 * math.pi))
        grad = (mm(c_ref[...], down, NT) * slope).astype(bf16)
        gate_ref[...] = grad
        hidden = act_ref.shape[1] // 2
        width = hidden // GROUP
        count = act.shape[1] // width
        for k in range(count):
            mask = jnp.bitwise_xor(flag_ref[PLACE], (step - slot * per) * count + k)
            to = (1 - mask % 2) * 4 + (mask // 2 % 2) * 2 + mask // 4
            act_ref[:, aligned(slot * hidden + to * width, width)] = act[
                :, k * width : (k + 1) * width
            ]
        acc_down[...] += mm(act, down)
        acc_back[...] += mm(grad, up, NT)

    @pl.when(step < per)
    def _():
        body(up0_ref[...], down0_ref[...], 0)

    @pl.when(step >= per)
    def _():
        body(up1_ref[...], down1_ref[...], 1)

    @pl.when(step == steps - 1)
    def _():
        down_out_ref[...] = acc_down[...].astype(down_out_ref.dtype)
        back_out_ref[...] = acc_back[...].astype(back_out_ref.dtype)


def run_feed_forward(flags, rows, cot, up, down, up_far, down_far, kind):
    tokens, width = rows.shape
    block = 512
    hidden = up.shape[1]
    per = hidden // block

    def near_at(j):
        return jnp.minimum(j, per - 1)

    def far_at(j):
        return jnp.maximum(j - per, 0)

    whole = pl.BlockSpec((tokens, width), lambda j: (0, 0))
    return pl.pallas_call(
        feed_forward,
        grid=(2 * per,),
        out_shape=(
            shape((tokens, 2 * hidden), bf16),
            shape((tokens, 2 * hidden), bf16),
            shape((tokens, width), bf16),
            shape((tokens, width), kind),
            shape((tokens, width), kind),
        ),
        in_specs=[
            pl.BlockSpec(memory_space=pltpu.SMEM),
            whole,
            whole,
            pl.BlockSpec((width, block), lambda j: (0, near_at(j))),
            pl.BlockSpec((block, width), lambda j: (near_at(j), 0)),
            pl.BlockSpec((width, block), lambda j: (0, far_at(j))),
            pl.BlockSpec((block, width), lambda j: (far_at(j), 0)),
        ],
        out_specs=(
            pl.BlockSpec((tokens, 2 * hidden), lambda j: (0, 0)),
            pl.BlockSpec((tokens, block), lambda j: (0, j)),
            whole,
            whole,
            whole,
        ),
        scratch_shapes=[pltpu.VMEM((tokens, width), f32), pltpu.VMEM((tokens, width), f32)],
        compiler_params=pltpu.CompilerParams(
            vmem_limit_bytes=24 * 1024 * 1024, dimension_semantics=("arbitrary",)
        ),
        cost_estimate=length(0),
    )(flags, rows, cot, up, down, up_far, down_far)


def products(lhs_refs, rhs_refs, columns, split=None):
    total = None
    for lhs_ref, rhs_ref in zip(lhs_refs, rhs_refs):
        term = mm(lhs_ref[:, columns], rhs_ref[...], TN)
        total = term if total is None else total + term
    return total


def down_pass(flag_ref, act0, act1, cot0, cot1, out_ref):
    hidden = act0.shape[1] // 2
    part = hidden // 4
    for slot in range(2):
        value = products(
            (act0, act1), (cot0, cot1), slice(slot * hidden, slot * hidden + hidden // 2)
        ).astype(bf16)
        out_ref[slot * part : (slot + 1) * part, :] = value[part:]
        out_ref[(2 + slot) * part : (3 + slot) * part, :] = value[:part]


def down_keep(flag_ref, act0, act1, cot0, cot1, core_ref, send_ref, left_ref):
    hidden = act0.shape[1] // 2
    part = hidden // 4
    for slot in range(2):
        value = products(
            (act0, act1), (cot0, cot1), slice(slot * hidden + hidden // 2, (slot + 1) * hidden)
        )
        to = slice(slot * part, (slot + 1) * part)
        send_ref[to, :] = (value[part:] + core_ref[to, :].astype(f32)).astype(bf16)
        left_ref[to, :] = value[:part] + core_ref[2 * part + to.start : 2 * part + to.stop, :].astype(
            f32
        )


def down_step(flag_ref, left_ref, received_ref, own_ref, send_ref):
    rows = own_ref.shape[0] // 2
    for slot in range(2):
        to = slice(slot * rows, (slot + 1) * rows)
        own = slice(2 * slot * rows, (2 * slot + 1) * rows)
        send = slice((2 * slot + 1) * rows, (2 * slot + 2) * rows)
        own_ref[to, :] = left_ref[own, :] + received_ref[own, :].astype(f32)
        send_ref[to, :] = (left_ref[send, :] + received_ref[send, :].astype(f32)).astype(bf16)


def y_first(value, rows):
    parts = [value[k * rows : (k + 1) * rows] for k in (1, 3, 0, 2)]
    return jnp.concatenate(parts[:2], 0), jnp.concatenate(parts[2:], 0)


def rows_pass(flag_ref, lhs0, lhs1, rhs0, rhs1, out_ref):
    half = lhs0.shape[1] // 2
    value = products((lhs0, lhs1), (rhs0, rhs1), slice(0, half)).astype(bf16)
    send, left = y_first(value, half // 4)
    out_ref[: half // 2, :] = send
    out_ref[half // 2 :, :] = left


def rows_keep(flag_ref, lhs0, lhs1, rhs0, rhs1, core_ref, send_ref, left_ref):
    half = lhs0.shape[1] // 2
    value = products((lhs0, lhs1), (rhs0, rhs1), slice(half, 2 * half))
    send, left = y_first(value, half // 4)
    send_ref[...] = (send + core_ref[: half // 2, :].astype(f32)).astype(bf16)
    left_ref[...] = left + core_ref[half // 2 :, :].astype(f32)


def up_step(flag_ref, left_ref, received_ref, own_ref, send_ref):
    rows = own_ref.shape[0]
    own_ref[...] = left_ref[:rows, :] + received_ref[:rows, :].astype(f32)
    send_ref[...] = (left_ref[rows:, :] + received_ref[rows:, :].astype(f32)).astype(bf16)


def own_down(flag_ref, own_ref, received_ref, near_ref, far_ref):
    rows = near_ref.shape[0]
    near_ref[...] = own_ref[:rows, :] + received_ref[:rows, :].astype(f32)
    far_ref[...] = (own_ref[rows:, :] + received_ref[rows:, :].astype(f32)).astype(bf16)


def own_up(flag_ref, own_ref, received_ref, near_ref, far_ref):
    width = near_ref.shape[1]
    near_ref[...] = own_ref[:, :width] + received_ref[:, :width].astype(f32)
    far_ref[...] = (own_ref[:, width:] + received_ref[:, width:].astype(f32)).astype(bf16)


def attn_pass(flag_ref, one0, one1, dqkv0, dqkv1, back0, back1, att0, att1, att2, att3, out_ref):
    half = one0.shape[1] // 2
    width = dqkv0.shape[1]
    channels = att0.shape[1]
    columns = slice(0, half)
    out_ref[:, :width] = products((one0, one1), (dqkv0, dqkv1), columns).astype(bf16)
    for slot, pair in enumerate(((att0, att1), (att2, att3))):
        at = width + slot * channels
        out_ref[:, at : at + channels] = products((back0, back1), pair, columns).astype(bf16)


def attn_keep(
    flag_ref, one0, one1, dqkv0, dqkv1, back0, back1, att0, att1, att2, att3, core_ref, own_ref,
    *send_refs,
):
    half = one0.shape[1] // 2
    rows = half // 4
    width = dqkv0.shape[1]
    channels = att0.shape[1]
    columns = slice(half, 2 * half)
    blocks = [(0, products((one0, one1), (dqkv0, dqkv1), columns))]
    for slot, pair in enumerate(((att0, att1), (att2, att3))):
        blocks.append((width + slot * channels, products((back0, back1), pair, columns)))
    for at, block in blocks:
        to = slice(at, at + block.shape[1])
        block = block + core_ref[:, to].astype(f32)
        own_ref[:, to] = block[:rows]
        for k, ref in enumerate(send_refs):
            ref[:, to] = block[(k + 1) * rows : (k + 2) * rows].astype(bf16)


def attn_own(
    flag_ref, own_ref, r1_ref, r2_ref, r3_ref, param_ref, gains_ref, gains_received, near_ref,
    far_ref,
):
    rows = own_ref.shape[0]
    total = own_ref[...] + (
        r1_ref[...].astype(f32) + r2_ref[...].astype(f32) + r3_ref[...].astype(f32)
    )
    channels = total.shape[1] // 8
    gains = gains_ref[...] + gains_received[...]
    for slot, ref in enumerate((near_ref, far_ref)):
        ref[:rows, : 3 * channels] = total[:, slot * 3 * channels : (slot + 1) * 3 * channels].astype(
            ref.dtype
        )
        ref[:rows, 3 * channels :] = total[
            :, (6 + slot) * channels : (7 + slot) * channels
        ].astype(ref.dtype)
        small = jnp.concatenate(
            [param_ref[:, slot * channels : (slot + 1) * channels], gains], axis=0
        ).astype(ref.dtype)
        count = small.shape[0] // 4
        for quarter in range(4):
            ref[rows : rows + count, quarter * channels : (quarter + 1) * channels] = small[
                quarter * count : (quarter + 1) * count
            ]
        ref[rows + count :, :] = jnp.zeros((ref.shape[0] - rows - count, 4 * channels), ref.dtype)


def add_two(flag_ref, a_ref, b_ref, out_ref):
    out_ref[...] = (a_ref[...].astype(f32) + b_ref[...].astype(f32)).astype(out_ref.dtype)


def add_three(flag_ref, a_ref, b_ref, c_ref, out_ref):
    out_ref[...] = (a_ref[...] + b_ref[...] + c_ref[...].astype(f32)).astype(out_ref.dtype)


def sources(flag_ref, even_ref, odd_ref, rows):
    for pair in range(GROUP // 2):
        for side, ref in enumerate((even_ref, odd_ref)):
            source = jnp.bitwise_xor(flag_ref[PLACE], 2 * pair + side)
            yield ref, pair, aligned(source * rows, rows)


def assemble_weight(flag_ref, even_ref, odd_ref, tile_ref, weight_ref, out_ref, qkv_ref):
    split = weight_ref.shape[1]
    for ref, pair, at in sources(flag_ref, even_ref, odd_ref, even_ref.shape[1]):
        weight_ref[at, :] = ref[pair, :, :split]
        out_ref[at, :] = ref[pair, :, split:]
    project(flag_ref, tile_ref, weight_ref, qkv_ref)


def assemble_grad(
    flag_ref, even_ref, odd_ref, qkv_ref, out_ref, rate_ref, coef_ref, skip_ref, gain_one_ref,
    gain_two_ref,
):
    channels = qkv_ref.shape[2]
    rows = qkv_ref.shape[1] // GROUP
    total = None
    for ref, pair, at in sources(flag_ref, even_ref, odd_ref, rows):
        for part in range(3):
            qkv_ref[part, at, :] = ref[
                pair, :rows, part * channels : (part + 1) * channels
            ].astype(f32)
        out_ref[:, at] = ref[pair, :rows, 3 * channels :].astype(f32).T
        term = ref[pair, rows:, :].astype(f32)
        total = term if total is None else total + term
    count = (2 * STATES + 8 + 8) // 4

    def row(k):
        return total[k % count : k % count + 1, k // count * channels : (k // count + 1) * channels]

    for k in range(STATES):
        rate_ref[k : k + 1, :] = row(k)
        coef_ref[k : k + 1, :] = row(STATES + k)
    skip_ref[...] = row(2 * STATES)
    for which, ref in enumerate((gain_one_ref, gain_two_ref)):
        for k in range(4):
            ref[:, k * channels : (k + 1) * channels] = row(2 * STATES + 8 + which * 4 + k)


def stack_two(flag_ref, a_ref, ax_ref, b_ref, by_ref, a_out, b_out):
    a_out[0], a_out[1] = a_ref[...], ax_ref[...]
    b_out[0], b_out[1] = b_ref[...], by_ref[...]


def stack_three(flag_ref, a_ref, ax_ref, b_ref, by_ref, a_out, b_out, both_out):
    stack_two(flag_ref, a_ref, ax_ref, b_ref, by_ref, a_out, b_out)
    both_out[0, 0], both_out[0, 1] = a_ref[...], b_ref[...]
    both_out[1, 0], both_out[1, 1] = ax_ref[...], by_ref[...]


def stack_pairs(flag_ref, a_ref, b_ref, out_ref):
    out_ref[0, 0], out_ref[0, 1] = a_ref[0], b_ref[0]
    out_ref[1, 0], out_ref[1, 1] = a_ref[1], b_ref[1]


def stack_four(flag_ref, a_ref, b_ref, c_ref, d_ref, out_ref):
    for k, ref in enumerate((a_ref, b_ref, c_ref, d_ref)):
        out_ref[k] = ref[...]


def stack_eight(flag_ref, a_ref, ay_ref, b_ref, bx_ref, out_ref):
    out_ref[0, 0], out_ref[1, 0] = a_ref[0], a_ref[1]
    out_ref[2, 0], out_ref[3, 0] = ay_ref[0], ay_ref[1]
    out_ref[0, 1], out_ref[2, 1] = b_ref[0], b_ref[1]
    out_ref[1, 1], out_ref[3, 1] = bx_ref[0], bx_ref[1]


def place_two(flag_ref, even_ref, odd_ref, a_out, b_out):
    for ref, pair, at in sources(flag_ref, even_ref, odd_ref, even_ref.shape[2]):
        a_out[at, :] = ref[pair, 0].astype(a_out.dtype)
        b_out[at, :] = ref[pair, 1].astype(b_out.dtype)


def place_wide(flag_ref, own_ref, other_ref, *refs):
    for side, ref in enumerate((own_ref, other_ref)):

        @pl.when(pl.program_id(0) % 2 == side)
        def _():
            refs[-2][...] = ref[0, 0].astype(f32)
            refs[-1][...] = ref[0, 1].astype(f32)


def run_place_wide(flags, own, other, starts, steps, filled=()):
    rows, width = own.shape[2:]
    piece = pl.BlockSpec((1, 2, rows, width), lambda j, flag_ref: (j // 2, 0, 0, 0))

    def place(which):
        return pl.BlockSpec(
            (rows, width),
            lambda j, flag_ref: (
                jnp.bitwise_xor(
                    flag_ref[PLACE], starts[which] + (j // 2) * steps[which] + j % 2
                ),
                0,
            ),
        )

    out = shape((GROUP * rows, width))
    return pl.pallas_call(
        place_wide,
        grid_spec=pltpu.PrefetchScalarGridSpec(
            num_scalar_prefetch=1,
            grid=(GROUP // 2,),
            in_specs=[piece, piece] + [pl.BlockSpec(memory_space=pl.ANY)] * len(filled),
            out_specs=(place(0), place(1)),
        ),
        out_shape=(out, out),
        input_output_aliases={3 + k: k for k in range(len(filled))},
        compiler_params=pltpu.CompilerParams(vmem_limit_bytes=VMEM_LIMIT),
        cost_estimate=length(0),
    )(flags, own, other, *filled)


class Order:
    def __init__(self):
        self.last = ()

    def __call__(self, *values):
        tied = lax.optimization_barrier((values, self.last))[0]
        return tied[0] if len(tied) == 1 else tied

    def done(self, result):
        self.last = result
        return result


def per_device(
    inputs,
    block_size,
    gain_attn,
    qkv_weight,
    ssm_rate,
    ssm_coef,
    ssm_skip,
    out_weight,
    gain_mlp,
    up_weight,
    down_weight,
    cotangent,
    dp_size,
):
    z = lax.axis_index("mp")
    place = jnp.bitwise_and(lax.axis_index("dp"), GROUP - 1)

    def swap_mp(value, mask):
        return lax.ppermute(value, "mp", [(k, k ^ mask) for k in range(4)])

    def swap_dp(value, mask):
        return lax.ppermute(value, "dp", [(k, k ^ mask) for k in range(dp_size)])

    def gather_by_xor(piece):
        return [piece] + [swap_dp(piece, 2 * k) for k in range(1, GROUP // 2)]

    def low(*dims):
        return shape(dims, bf16)

    def over_groups(own):
        mask = GROUP
        while mask < dp_size:
            own = own + swap_dp(own.astype(bf16), mask).astype(f32)
            mask *= 2
        return own.astype(bf16)

    model_dim = inputs.shape[2]
    channels = qkv_weight.shape[2]
    hidden = up_weight.shape[1]
    wide = 2 * channels
    rows = model_dim // GROUP
    row = inputs[0]
    cot = cotangent[0]
    z_far = jnp.bitwise_xor(z, 2)
    whole = (block_size[0] > HALF).astype(jnp.int32)
    flags = jnp.stack(
        [whole, jnp.right_shift(z, 1), jnp.bitwise_and(z, 1), z, z_far, place]
    ).astype(jnp.int32)
    gain_one = gain_attn[None]
    gain_two = gain_mlp[None]
    order = Order()
    half = shape((HALF, model_dim))
    half_low = shape((HALF, model_dim), bf16)

    normed_one = order.done(call(norm_one, half_low)(flags, row, gain_one))
    paired_one = swap_mp(normed_one, 1)
    qkv_parts = jnp.transpose(qkv_weight, (1, 0, 2))
    attn_slice, up_slice, down_slice, ssm_pack = order.done(
        run_cut_slices(
            flags, order(qkv_parts), out_weight, up_weight, down_weight, ssm_rate.T, ssm_coef.T,
            ssm_skip[None],
        )
    )
    attn_across = swap_mp(attn_slice, 2)
    near_qkv = order.done(jnp.concatenate(list(order(*[qkv_parts[k] for k in range(3)])), 1))

    paired_one, attn_across = order.done(order(paired_one, attn_across))
    attn_own_slice = attn_across[:rows]
    attn_x = swap_dp(attn_own_slice, 2)
    attn_y = swap_dp(attn_own_slice, 4)
    up_across = swap_mp(order(up_slice), 2)
    paired_cot = swap_mp(order(cot), 1)
    ssm_both = call(join_ssm, shape((48, wide)))(flags, ssm_pack, attn_across)
    rate_t, coef_t, skip_t = ssm_both[:16], ssm_both[16:32], ssm_both[32:33]
    tile_one, one_sent, second_local, handed = order.done(
        call(
            ssm_forward,
            (
                shape((2, HALF, model_dim), bf16),
                shape((2, HALF, model_dim), bf16),
                shape((CTX, wide)),
                shape((CTX + 3 * STATES, wide), bf16),
            ),
            scratch=[pltpu.VMEM((2 * HALF, wide), f32)],
        )(flags, normed_one, order(paired_one), rate_t, coef_t, skip_t)
    )
    handed = lax.ppermute(handed, "mp", [(0, 2), (1, 3)])

    qkv_shape = shape((2, HALF, 3 * channels), bf16)
    att_shape = shape((2, HALF, channels), bf16)
    attn_x = order.done(order(attn_x))
    attn_xy = swap_dp(attn_x, 4)
    attn_y, paired_cot, mlp_up = order.done(order(attn_y, paired_cot, up_across))
    mlp_up_x = swap_dp(mlp_up, 2)
    qkv_near = order.done(call(project, qkv_shape)(flags, order(tile_one), near_qkv))
    even = order.done(
        call(stack_four, shape((4,) + attn_x.shape, bf16))(
            flags, attn_own_slice, attn_x, attn_y, order(attn_xy)
        )
    )
    odd_part = swap_dp(even, 1)
    slice_shape = low(rows, model_dim)
    handed = order.done(order(handed))
    down_across = swap_mp(order(down_slice), 2)
    ctx_first, ctx_second, enter_state = order.done(
        call(
            ssm_carry_in,
            (shape((CTX, wide), bf16), shape((CTX, wide), bf16), shape((STATES, wide))),
            scratch=[pltpu.VMEM((CTX, wide), f32)],
            micros=16,
        )(flags, order(second_local), handed, rate_t, coef_t)
    )
    att_near = order.done(
        call(attention_near, att_shape)(flags, order(qkv_near), ctx_first, ctx_second)
    )
    far_qkv, far_out, qkv_far = order.done(
        call(
            assemble_weight,
            (
                shape((model_dim, 3 * channels), bf16),
                shape((model_dim, channels), bf16),
                qkv_shape,
            ),
        )(flags, even, order(odd_part), tile_one)
    )
    att_far, out_own, out_send = order.done(
        call(attention_far, (att_shape, half, half_low))(
            flags, order(qkv_far), ctx_first, ctx_second, att_near, out_weight, far_out
        )
    )
    out_received = swap_mp(out_send, 1)
    pair_shape = low(2, rows, model_dim)
    mlp_down = order.done(order(down_across))
    mlp_down_y = swap_dp(mlp_down, 4)
    mlp_up_two, mlp_down_two = order.done(
        call(stack_two, (pair_shape, pair_shape), micros=0.5)(
            flags, mlp_up, order(mlp_up_x), mlp_down, order(mlp_down_y)
        )
    )
    mlp_up_y = swap_dp(mlp_up_two, 4)
    mlp_down_x = swap_dp(mlp_down_two, 2)
    middle, normed_two = order.done(
        call(norm_two, (half, half_low), micros=3)(
            flags, row, out_own, order(out_received), gain_two
        )
    )

    paired_two = swap_mp(normed_two, 1)
    eight_shape = low(GROUP // 2, 2, rows, model_dim)
    mlp_even = order.done(
        call(stack_eight, eight_shape, micros=1)(
            flags, mlp_up_two, order(mlp_up_y), mlp_down_two, order(mlp_down_x)
        )
    )
    mlp_odd = swap_dp(mlp_even, 1)
    paired_two = order(paired_two)
    warm = order.done(
        call(touch, shape((8, 128), bf16), micros=30)(
            flags, up_weight, down_weight, cot, paired_cot, paired_two
        )
    )
    up_far, down_far = order.done(
        call(place_two, (low(model_dim, hidden), low(hidden, model_dim)))(
            flags, mlp_even, order(mlp_odd)
        )
    )
    mlp = (up_weight, down_weight, up_far, down_far)
    act_other, gate_other, two_other, down_send, back_send = order.done(
        run_feed_forward(flags, order(paired_two), paired_cot, *mlp, bf16)
    )
    back_received = swap_mp(back_send, 1)
    act_own, gate_own, two_own, down_own, back_own = order.done(
        run_feed_forward(flags, order(normed_two), cot, *mlp, f32)
    )

    side = model_dim // 2
    acts = (act_own, act_other, cot, paired_cot)
    passed = order.done(call(down_pass, low(hidden, model_dim))(flags, order(act_own), *acts[1:]))
    down_core = swap_dp(passed, 1)
    ups = (two_own, two_other, gate_own, gate_other)
    passed = order.done(call(rows_pass, low(side, 2 * hidden))(flags, order(two_own), *ups[1:]))
    up_core = swap_dp(passed, 1)
    middle_grad, attn_grad, gain_mlp_grad = order.done(
        call(norm_two_back, (half, half_low, shape((1, model_dim))), micros=12)(
            flags, middle, back_own, order(back_received), cot, gain_two, warm
        )
    )
    paired_back = swap_mp(attn_grad, 1)
    down_send_x, down_left = order.done(
        call(down_keep, (low(side, model_dim), shape((side, model_dim))))(
            flags, *acts, order(down_core)
        )
    )
    down_x = swap_dp(down_send_x, 2)
    up_send_y, up_left = order.done(
        call(rows_keep, (low(side // 2, 2 * hidden), shape((side // 2, 2 * hidden))))(
            flags, *ups, order(up_core)
        )
    )
    up_y = swap_dp(up_send_y, 4)

    att_grad, back_sent = order.done(
        call(
            attended_grads,
            (shape((2, HALF, wide), bf16), shape((2, HALF, model_dim), bf16)),
            micros=4,
        )(flags, attn_grad, order(paired_back), out_weight, far_out)
    )
    down_received = swap_mp(order(down_send), 1)
    dqkv, second_grad, returned = order.done(
        call(
            attention_backward,
            (
                shape((2, HALF, 6 * channels), bf16),
                shape((CTX, wide)),
                shape((CTX + 3 * STATES, wide), bf16),
            ),
        )(flags, qkv_near, qkv_far, ctx_first, ctx_second, order(att_grad), rate_t)
    )
    returned = lax.ppermute(returned, "mp", [(2, 0), (3, 1)])
    one_total = order.done(
        call(qkv_back, shape((2, HALF, model_dim)))(flags, order(dqkv), near_qkv, far_qkv)
    )
    attns = (
        one_sent[0], one_sent[1], dqkv[0], dqkv[1], back_sent[0], back_sent[1],
        att_near[0], att_near[1], att_far[0], att_far[1],
    )
    passed = order.done(
        call(attn_pass, low(side, 8 * channels))(flags, order(attns[0]), *attns[1:])
    )
    attn_core = swap_dp(passed, 1)
    down_mine, down_send_y = order.done(
        call(down_step, (shape((2 * rows, model_dim)), low(2 * rows, model_dim)))(
            flags, down_left, order(down_x)
        )
    )
    down_y = swap_dp(down_send_y, 4)
    up_mine, up_send_x = order.done(
        call(up_step, (shape((rows, 2 * hidden)), low(rows, 2 * hidden)))(
            flags, up_left, order(up_y)
        )
    )
    up_x = swap_dp(up_send_x, 2)
    one_own, one_send, last_grad, enter_adjoint = order.done(
        call(
            ssm_signal_grad,
            (half, half_low, shape((CTX, wide)), shape((STATES, wide))),
            scratch=[pltpu.VMEM((2 * HALF, wide), f32), pltpu.VMEM((HALF, model_dim), f32)],
            micros=30,
        )(flags, second_grad, order(returned), rate_t, coef_t, skip_t, one_total)
    )
    one_received = swap_mp(one_send, 1)
    down_received = order.done(order(down_received))
    attn_mine, *attn_sends = order.done(
        call(attn_keep, (shape((rows, 8 * channels)),) + (low(rows, 8 * channels),) * 3)(
            flags, *attns, order(attn_core)
        )
    )
    attn_sent = [swap_dp(part, SENT[5 + k]) for k, part in enumerate(attn_sends)]
    wide_slice = shape((rows, model_dim))
    down_near, down_far_grad = order.done(
        call(own_down, (wide_slice, slice_shape))(flags, down_mine, order(down_y))
    )
    down_received_far = swap_mp(down_far_grad, 2)
    up_near, up_far_grad = order.done(
        call(own_up, (wide_slice, slice_shape))(flags, up_mine, order(up_x))
    )
    up_received_far = swap_mp(up_far_grad, 2)
    param_grad = order.done(
        call(
            ssm_param_grad,
            shape((40, wide)),
            scratch=[pltpu.VMEM((2 * HALF, wide), f32)],
            micros=3,
        )(
            flags, order(tile_one), second_grad, last_grad, enter_state, enter_adjoint, rate_t, coef_t
        )
    )
    input_grad, gains = order.done(
        call(norm_one_back, (half, shape((2 * model_dim // channels, channels))))(
            flags, row, one_own, order(one_received), middle_grad, gain_one, gain_mlp_grad
        )
    )
    gains_received = swap_mp(gains, 1)
    output = order.done(
        call(add_three, half_low)(flags, middle, order(down_own), down_received)
    )
    down_mine = order.done(
        call(add_two, slice_shape)(flags, down_near, order(down_received_far))
    )
    down_mine = over_groups(down_mine)
    down_x = swap_dp(down_mine, 2)
    up_mine = order.done(call(add_two, slice_shape)(flags, up_near, order(up_received_far)))
    up_mine = over_groups(up_mine)
    up_y = swap_dp(up_mine, 4)
    slice_rows = rows + 16
    *attn_sent, gains_received = order(*attn_sent, gains_received)
    attn_near, attn_send = order.done(
        call(attn_own, (shape((slice_rows, 4 * channels)), low(slice_rows, 4 * channels)))(
            flags, attn_mine, *attn_sent, param_grad, gains, gains_received
        )
    )
    attn_received = swap_mp(attn_send, 2)
    both_shape = low(2, 2, rows, model_dim)
    down_two, up_two, first_pieces = order.done(
        call(stack_three, (pair_shape, pair_shape, both_shape), micros=3)(
            flags, down_mine, order(down_x), up_mine, order(up_y)
        )
    )
    down_y = swap_dp(down_two, 4)
    up_x = swap_dp(up_two, 2)
    first_others = swap_dp(first_pieces, 1)
    attn_slice_grad = order.done(
        call(add_two, low(slice_rows, 4 * channels), micros=20)(
            flags, attn_near, order(attn_received)
        )
    )
    first_others = order.done(order(first_others))
    attn_slice_grad = over_groups(order(attn_slice_grad))
    attn_sent = [swap_dp(attn_slice_grad, 2 * k) for k in range(1, GROUP // 2)]
    wide_grads = order.done(
        run_place_wide(flags, first_pieces, order(first_others), (0, 0), (2, 4))
    )
    even = order.done(
        call(stack_four, low(4, slice_rows, 4 * channels))(
            flags, attn_slice_grad, *order(*attn_sent)
        )
    )
    odd_part = swap_dp(even, 1)
    last_pieces = order.done(
        call(stack_pairs, both_shape, micros=8)(flags, *order(down_y, up_x))
    )
    last_others = swap_dp(last_pieces, 1)
    qkv_grad, out_grad, rate_grad, coef_grad, skip_grad, gain_one_grad, gain_two_grad = order.done(
        call(
            assemble_grad,
            (
                shape((3, model_dim, channels)),
                shape(out_weight.shape),
                shape((STATES, channels)),
                shape((STATES, channels)),
                shape((1, channels)),
                shape((1, model_dim)),
                shape((1, model_dim)),
            ),
            micros=8,
        )(flags, even, order(odd_part))
    )
    down_grad, up_grad = run_place_wide(
        flags, last_pieces, order(last_others), (4, 2), (2, 4), wide_grads
    )
    return (
        output[None],
        input_grad[None],
        gain_one_grad[0],
        jnp.transpose(qkv_grad, (1, 0, 2)),
        rate_grad.T,
        coef_grad.T,
        skip_grad[0],
        out_grad,
        gain_two_grad[0],
        up_grad,
        down_grad,
    )


def solution(mesh):
    return jax.shard_map(
        partial(per_device, dp_size=mesh.shape["dp"]),
        mesh=mesh,
        in_specs=(
            P("dp", "mp", None),
            P("dp"),
            P(),
            P(None, None, "mp"),
            P("mp", None),
            P("mp", None),
            P("mp"),
            P("mp", None),
            P(),
            P(None, "mp"),
            P("mp", None),
            P("dp", "mp", None),
        ),
        out_specs=(
            P("dp", "mp", None),
            P("dp", "mp", None),
            P(),
            P(None, None, "mp"),
            P("mp", None),
            P("mp", None),
            P("mp"),
            P("mp", None),
            P(),
            P(None, "mp"),
            P("mp", None),
        ),
        check_vma=False,
    )
```

```python
from functools import partial
import math

import jax
import jax.numpy as jnp
from jax import lax
from jax.experimental import pallas as pl
from jax.experimental.pallas import tpu as pltpu
from jax.sharding import PartitionSpec as P

HD = 128
CTX = 128
HALF = 256
STATES = 16
GROUP = 8

f32 = jnp.float32
bf16 = jnp.bfloat16
epsilon = 1e-05
masked_score = -1e30
score_scale = 1.0 / math.sqrt(HD)
VMEM_LIMIT = 16 * 1024 * 1024

NT = (((1,), (1,)), ((), ()))
TN = (((0,), (0,)), ((), ()))
NN = (((1,), (0,)), ((), ()))

WHOLE, LATE, ODD, NEAR, FAR, PLACE = range(6)


def mm(a, b, dims=NN):
    return lax.dot_general(a, b, dims, preferred_element_type=f32)


def shape(dims, dtype=f32):
    return jax.ShapeDtypeStruct(dims, dtype)


def length(micros):
    return pl.CostEstimate(flops=int(micros * 1e9), bytes_accessed=0, transcendentals=0)


def call(kernel, out_shape, scratch=(), micros=0):
    def run(flags, *args):
        vmem = pl.BlockSpec(memory_space=pltpu.VMEM)
        return pl.pallas_call(
            kernel,
            out_shape=out_shape,
            in_specs=[pl.BlockSpec(memory_space=pltpu.SMEM)] + [vmem] * len(args),
            out_specs=jax.tree.map(lambda _: vmem, out_shape),
            scratch_shapes=scratch,
            compiler_params=pltpu.CompilerParams(vmem_limit_bytes=VMEM_LIMIT),
            cost_estimate=length(micros),
        )(flags, *args)

    return run


SENT = (1, 5, 3, 7, 0, 4, 2, 6)


def in_sent_order(flag_ref, value_ref, out_ref, masks=SENT):
    width = value_ref.shape[1] // GROUP
    for k, mask in enumerate(masks):
        source = jnp.bitwise_xor(flag_ref[PLACE], mask)
        out_ref[:, k * width : (k + 1) * width] = value_ref[:, aligned(source * width, width)]


def aligned(start, size):
    return pl.ds(pl.multiple_of(start, size), size)


def cut_slices(
    flag_ref, qkv_ref, out_ref, up_ref, down_ref, rate_ref, coef_ref, skip_ref, attn_ref, up_slice,
    down_slice, ssm_ref, out_slice, *sems,
):
    rows = up_slice.shape[0]
    channels = out_slice.shape[0]
    count = ssm_ref.shape[0]
    ssm_ref[:STATES, :] = rate_ref[...]
    ssm_ref[STATES : 2 * STATES, :] = coef_ref[...]
    ssm_ref[2 * STATES :, :] = jnp.zeros((count - 2 * STATES, channels), f32)
    ssm_ref[2 * STATES : 2 * STATES + 1, :] = skip_ref[...]
    for k, part in enumerate(split_three(ssm_ref[...])):
        attn_ref[rows : rows + count, k * channels : (k + 1) * channels] = part
    attn_ref[rows : rows + count, 3 * channels :] = jnp.zeros((count, channels), bf16)
    at = aligned(flag_ref[PLACE] * rows, rows)
    copies = [
        pltpu.make_async_copy(
            qkv_ref.at[part, at, :],
            attn_ref.at[:rows, part * channels : (part + 1) * channels],
            sems[part],
        )
        for part in range(3)
    ] + [
        pltpu.make_async_copy(out_ref.at[:, at], out_slice, sems[3]),
        pltpu.make_async_copy(up_ref.at[at, :], up_slice, sems[4]),
        pltpu.make_async_copy(down_ref.at[at, :], down_slice, sems[5]),
    ]
    for copy in copies:
        copy.start()
    for copy in copies:
        copy.wait()
    attn_ref[:rows, 3 * channels :] = out_slice[...].T


def join_ssm(flag_ref, own_ref, across_ref, out_ref):
    channels = own_ref.shape[1]
    start = across_ref.shape[0] - own_ref.shape[0]
    out_ref[:, :channels] = own_ref[...]
    parts = [across_ref[start:, k * channels : (k + 1) * channels].astype(f32) for k in range(3)]
    out_ref[:, channels:] = (parts[0] + parts[1]) + parts[2]


def run_cut_slices(flags, qkv_parts, out_weight, up_weight, down_weight, *ssm_parts):
    channels = qkv_parts.shape[2]
    width = out_weight.shape[1]
    rows = width // GROUP
    vmem = pl.BlockSpec(memory_space=pltpu.VMEM)
    return pl.pallas_call(
        cut_slices,
        in_specs=[pl.BlockSpec(memory_space=pltpu.SMEM)]
        + [pl.BlockSpec(memory_space=pltpu.HBM)] * 4
        + [vmem] * 3,
        out_specs=(vmem,) * 4,
        out_shape=(
            shape((rows + 48, 4 * channels), bf16),
            shape((rows, width), bf16),
            shape((rows, width), bf16),
            shape((48, channels)),
        ),
        scratch_shapes=[pltpu.VMEM((channels, rows), bf16)] + [pltpu.SemaphoreType.DMA] * 6,
        compiler_params=pltpu.CompilerParams(vmem_limit_bytes=56 * 1024 * 1024),
        cost_estimate=length(0),
    )(flags, qkv_parts, out_weight, up_weight, down_weight, *ssm_parts)


def normalise(values):
    mean = jnp.mean(values, axis=-1, keepdims=True)
    centred = values - mean
    spread = jnp.mean(centred * centred, axis=-1, keepdims=True)
    inverse = lax.rsqrt(spread + epsilon)
    return centred * inverse, inverse


def normalise_back(grad, gain, hat, inverse):
    inner = grad * gain
    return (
        inner
        - jnp.mean(inner, axis=-1, keepdims=True)
        - hat * jnp.mean(inner * hat, axis=-1, keepdims=True)
    ) * inverse


def by_rows(body, rows, block=64):
    for k in range(rows // block):
        body(slice(k * block, (k + 1) * block))


def norm_one(flag_ref, x_ref, gain_ref, out_ref):
    def body(at):
        hat, _ = normalise(x_ref[at, :].astype(f32))
        out_ref[at, :] = (hat * gain_ref[...]).astype(bf16)

    by_rows(body, x_ref.shape[0])


def touch(flag_ref, up_ref, down_ref, cot_ref, paired_ref, rows_ref, out_ref):
    out_ref[...] = (
        (up_ref[:16, :128] + down_ref[:16, :128])
        + (cot_ref[:16, :128] + paired_ref[:16, :128])
        + rows_ref[:16, :128]
    )


def norm_two(flag_ref, x_ref, own_ref, received_ref, gain_ref, middle_ref, out_ref):
    def body(at):
        middle = x_ref[at, :].astype(f32) + own_ref[at, :] + received_ref[at, :].astype(f32)
        middle_ref[at, :] = middle
        hat, _ = normalise(middle)
        out_ref[at, :] = (hat * gain_ref[...]).astype(bf16)

    by_rows(body, x_ref.shape[0])


def norm_two_back(
    flag_ref, middle_ref, own_ref, received_ref, cot_ref, gain_ref, warm_ref, grad_ref, low_ref,
    gain_out_ref,
):
    sums = []

    def body(at):
        hat, inverse = normalise(middle_ref[at, :])
        grad = own_ref[at, :] + received_ref[at, :].astype(f32)
        sums.append(jnp.sum(grad * hat, axis=0, keepdims=True))
        total = cot_ref[at, :].astype(f32) + normalise_back(grad, gain_ref[...], hat, inverse)
        grad_ref[at, :] = total
        low_ref[at, :] = total.astype(bf16)

    by_rows(body, middle_ref.shape[0])
    gain_out_ref[...] = sum(sums)


def norm_one_back(
    flag_ref, x_ref, own_ref, received_ref, middle_ref, gain_ref, gain_two_grad_ref, grad_ref,
    gain_out_ref,
):
    sums = []

    def body(at):
        hat, inverse = normalise(x_ref[at, :].astype(f32))
        grad = own_ref[at, :] + received_ref[at, :].astype(f32)
        sums.append(jnp.sum(grad * hat, axis=0, keepdims=True))
        grad_ref[at, :] = middle_ref[at, :] + normalise_back(grad, gain_ref[...], hat, inverse)

    by_rows(body, x_ref.shape[0])
    width = gain_out_ref.shape[1]
    pieces = x_ref.shape[1] // width
    for which, value in enumerate((sum(sums), gain_two_grad_ref[...])):
        for k in range(pieces):
            row = which * pieces + k
            gain_out_ref[row : row + 1, :] = value[:, k * width : (k + 1) * width]


def split_three(value):
    high = value.astype(bf16)
    rest = value - high.astype(f32)
    middle = rest.astype(bf16)
    return [high, middle, (rest - middle.astype(f32)).astype(bf16)]


def join_three(ref, start, lanes):
    parts = [ref[start + k * STATES : start + (k + 1) * STATES, lanes] for k in range(3)]
    return (parts[0].astype(f32) + parts[1].astype(f32)) + parts[2].astype(f32)


def load_signal(flag_ref, tile_ref, xs):
    channels = xs.shape[1] // 2
    for half in range(2):
        source = jnp.bitwise_xor(flag_ref[ODD], half)
        for slot, name in enumerate((NEAR, FAR)):
            xs[half * HALF : (half + 1) * HALF, slot * channels : (slot + 1) * channels] = tile_ref[
                source, :, aligned(flag_ref[name] * channels, channels)
            ].astype(f32)


def ssm_forward(
    flag_ref, own_ref, other_ref, rate_ref, coef_ref, skip_ref, tile_ref, sent_ref,
    second_ref, handed_ref, xs,
):
    tile_ref[0] = own_ref[...]
    tile_ref[1] = other_ref[...]
    in_sent_order(flag_ref, own_ref, sent_ref.at[0])
    in_sent_order(flag_ref, other_ref, sent_ref.at[1])
    load_signal(flag_ref, tile_ref, xs)
    decay = jnp.exp(-rate_ref[...])
    coef = coef_ref[...]
    skip = skip_ref[...]

    def step(eight, state, chunk):
        x8 = xs[aligned((chunk * 16 + eight) * 8, 8), :]
        rows = []
        for k in range(8):
            state = decay * state + x8[k : k + 1]
            if chunk % 2:
                rows.append(jnp.sum(coef * state, axis=0, keepdims=True))
        if chunk % 2:
            y8 = jnp.concatenate(rows, axis=0) + skip * x8
            at = aligned(eight * 8, 8)
            if chunk == 1:
                second_ref[at, :] = y8
            else:
                xs[at, :] = y8
        return state

    state = jnp.zeros_like(decay)
    for chunk in range(4):
        state = lax.fori_loop(0, 16, partial(step, chunk=chunk), state)
    handed_ref[:CTX, :] = xs[:CTX, :].astype(bf16)
    for k, part in enumerate(split_three(state)):
        handed_ref[CTX + k * STATES : CTX + (k + 1) * STATES, :] = part


def project(flag_ref, tile_ref, weight_ref, qkv_ref):
    for half in range(2):
        qkv_ref[half] = mm(tile_ref[half], weight_ref[...]).astype(bf16)


def ssm_carry_in(
    flag_ref, local_ref, handed_ref, rate_ref, coef_ref, first_ref, second_ref, enter_ref, acc
):
    channels = rate_ref.shape[1] // 2
    for slot in range(2):
        to = slice(slot * channels, (slot + 1) * channels)
        source = slice((1 - slot) * channels, (2 - slot) * channels)
        first_ref[:, to] = handed_ref[:CTX, source]
        enter_ref[:, to] = join_three(handed_ref, CTX, source)
    rate = rate_ref[...]
    decay = jnp.exp(-rate)
    coef = coef_ref[...]

    def step(eight, state):
        rows = []
        for k in range(8):
            rows.append(jnp.sum(coef * state, axis=0, keepdims=True))
            state = decay * state
        acc[aligned(eight * 8, 8), :] = jnp.concatenate(rows, axis=0)
        return state

    lax.fori_loop(0, 16, step, enter_ref[...] * jnp.exp(-129.0 * rate))
    second_ref[...] = (local_ref[...] + acc[...]).astype(bf16)


def qkv_back(flag_ref, dqkv_ref, near_weight_ref, far_weight_ref, out_ref):
    split = near_weight_ref.shape[1]
    for half in range(2):
        out_ref[half] = mm(dqkv_ref[half, :, :split], near_weight_ref[...], NT) + mm(
            dqkv_ref[half, :, split:], far_weight_ref[...], NT
        )


def ssm_signal_grad(
    flag_ref, near_ref, returned_ref, rate_ref, coef_ref, skip_ref, total_ref, own_ref, send_ref,
    last_ref, adjoint_ref, rows_out, total,
):
    channels = rate_ref.shape[1] // 2
    adjoints = []
    for slot in range(2):
        to = slice(slot * channels, (slot + 1) * channels)
        source = slice((1 - slot) * channels, (2 - slot) * channels)
        last_ref[:, to] = returned_ref[:CTX, source].astype(f32)
        adjoints.append(join_three(returned_ref, CTX, source))
    decay = jnp.exp(-rate_ref[...])
    coef = coef_ref[...]
    skip = skip_ref[...]

    def step(j, adjoint, chunk):
        eight = 15 - j
        at = aligned(eight * 8, 8)
        if chunk % 2:
            g8 = (near_ref, last_ref)[chunk // 2][at, :]
        rows = [None] * 8
        for k in range(7, -1, -1):
            adjoint = decay * adjoint
            if chunk % 2:
                adjoint = adjoint + g8[k : k + 1]
            rows[k] = jnp.sum(coef * adjoint, axis=0, keepdims=True)
        y8 = jnp.concatenate(rows, axis=0)
        if chunk % 2:
            y8 = y8 + skip * g8
        rows_out[aligned((chunk * 16 + eight) * 8, 8), :] = y8
        return adjoint

    adjoint = jnp.concatenate(adjoints, axis=1)
    adjoint_ref[...] = adjoint
    for chunk in (3, 2, 1, 0):
        adjoint = lax.fori_loop(0, 16, partial(step, chunk=chunk), adjoint)
    for half in (1, 0):
        total[...] = total_ref[half]
        source = aligned(jnp.bitwise_xor(flag_ref[ODD], half) * HALF, HALF)
        for slot, name in enumerate((NEAR, FAR)):
            total[:, aligned(flag_ref[name] * channels, channels)] += rows_out[
                source, slot * channels : (slot + 1) * channels
            ]
        if half:
            send_ref[...] = total[...].astype(bf16)
        else:
            own_ref[...] = total[...]


def ssm_param_grad(
    flag_ref, tile_ref, near_ref, last_ref, enter_ref, adjoint_ref, rate_ref, coef_ref, out_ref, xs
):
    load_signal(flag_ref, tile_ref, xs)
    decay = jnp.exp(-rate_ref[...])
    zero = jnp.zeros_like(decay)

    def step(eight, carry, chunk):
        state, slope, for_coef, for_rate = carry
        x8 = xs[aligned((chunk * 16 + eight) * 8, 8), :]
        if chunk % 2:
            g8 = (near_ref, last_ref)[chunk // 2][aligned(eight * 8, 8), :]
        for k in range(8):
            slope = decay * (slope + state)
            state = decay * state + x8[k : k + 1]
            if chunk % 2:
                for_coef = for_coef + state * g8[k : k + 1]
                for_rate = for_rate + slope * g8[k : k + 1]
        return state, slope, for_coef, for_rate

    carry = (enter_ref[...], zero, zero, zero)
    for chunk in range(4):
        carry = lax.fori_loop(0, 16, partial(step, chunk=chunk), carry)
    for_rate = carry[3] + decay * adjoint_ref[...] * carry[1]
    out_ref[:STATES, :] = -coef_ref[...] * for_rate
    out_ref[STATES : 2 * STATES, :] = carry[2]
    skip = jnp.sum(xs[CTX : 2 * CTX] * near_ref[...], axis=0, keepdims=True) + jnp.sum(
        xs[3 * CTX :] * last_ref[...], axis=0, keepdims=True
    )
    out_ref[2 * STATES :, :] = jnp.concatenate(
        [skip, jnp.zeros((out_ref.shape[0] - 2 * STATES - 1, skip.shape[1]), f32)], axis=0
    )


def causal(scores):
    rows = lax.broadcasted_iota(jnp.int32, scores.shape, 0)
    cols = lax.broadcasted_iota(jnp.int32, scores.shape, 1)
    return jnp.where(cols <= rows, scores, masked_score)


def softmax_parts(parts):
    top = parts[0].max(axis=-1, keepdims=True)
    for part in parts[1:]:
        top = jnp.maximum(top, part.max(axis=-1, keepdims=True))
    weights = [jnp.exp(part - top) for part in parts]
    total = weights[0].sum(axis=-1, keepdims=True)
    for weight in weights[1:]:
        total = total + weight.sum(axis=-1, keepdims=True)
    return [weight / total for weight in weights]


def block_probs(q0, q1, k0, k1, first, second, whole, late):
    has_first = late > 0
    is_whole = whole > 0
    chosen = jnp.where(is_whole, first, second)
    chosen_ok = jnp.logical_or(jnp.logical_not(is_whole), has_first)
    s00 = causal(mm(q0, k0, NT) * score_scale)
    s0c = jnp.where(has_first, mm(q0, first, NT) * score_scale, masked_score)
    s11 = causal(mm(q1, k1, NT) * score_scale)
    s10 = jnp.where(is_whole, mm(q1, k0, NT) * score_scale, masked_score)
    s1c = jnp.where(chosen_ok, mm(q1, chosen, NT) * score_scale, masked_score)
    return softmax_parts([s00, s0c]), softmax_parts([s11, s10, s1c]), chosen


def head_parts(qkv_ref, head, half):
    channels = qkv_ref.shape[2] // 3
    return [
        qkv_ref[half, :, part * channels + head * HD : part * channels + (head + 1) * HD]
        for part in range(3)
    ]


def attend(flag_ref, qkv_ref, first_ref, second_ref, att_ref, slot):
    half0 = flag_ref[ODD]
    half1 = 1 - half0
    heads = qkv_ref.shape[2] // (3 * HD)
    for head in range(heads):
        q0, k0, v0 = head_parts(qkv_ref, head, half0)
        q1, k1, v1 = head_parts(qkv_ref, head, half1)
        at = slice((slot * heads + head) * HD, (slot * heads + head + 1) * HD)
        first = first_ref[:, at]
        second = second_ref[:, at]
        (p00, p0c), (p11, p10, p1c), chosen = block_probs(
            q0, q1, k0, k1, first, second, flag_ref[WHOLE], flag_ref[LATE]
        )
        to = slice(head * HD, (head + 1) * HD)
        att_ref[half0, :, to] = (mm(p00.astype(bf16), v0) + mm(p0c.astype(bf16), first)).astype(
            bf16
        )
        att_ref[half1, :, to] = (
            mm(p11.astype(bf16), v1) + mm(p10.astype(bf16), v0) + mm(p1c.astype(bf16), chosen)
        ).astype(bf16)


def attention_near(flag_ref, qkv_ref, first_ref, second_ref, att_ref):
    attend(flag_ref, qkv_ref, first_ref, second_ref, att_ref, 0)


def attention_far(
    flag_ref, qkv_ref, first_ref, second_ref, near_ref, out_near_ref, out_far_ref, att_ref, own_ref,
    send_ref,
):
    attend(flag_ref, qkv_ref, first_ref, second_ref, att_ref, 1)

    def projected(half):
        return mm(near_ref[half], out_near_ref[...]) + mm(att_ref[half], out_far_ref[...], NT)

    send_ref[...] = projected(1).astype(bf16)
    own_ref[...] = projected(0)


def attended_grads(flag_ref, own_ref, other_ref, out_near_ref, out_far_ref, grad_ref, sent_ref):
    split = out_near_ref.shape[0]
    for half, ref in enumerate((own_ref, other_ref)):
        grad_ref[half, :, :split] = mm(ref[...], out_near_ref[...], NT).astype(bf16)
        grad_ref[half, :, split:] = mm(ref[...], out_far_ref[...]).astype(bf16)
        in_sent_order(flag_ref, ref, sent_ref.at[half])


def attention_backward(
    flag_ref, near_ref, far_ref, first_ref, second_ref, grad_ref, rate_ref, out_ref, second_out_ref,
    returned_ref,
):
    half0 = flag_ref[ODD]
    half1 = 1 - half0
    is_whole = flag_ref[WHOLE] > 0
    heads = near_ref.shape[2] // (3 * HD)
    for index in range(2 * heads):
        slot, head = index // heads, index % heads
        qkv_ref = (near_ref, far_ref)[slot]
        q0, k0, v0 = head_parts(qkv_ref, head, half0)
        q1, k1, v1 = head_parts(qkv_ref, head, half1)
        at = slice(index * HD, (index + 1) * HD)
        g0 = grad_ref[half0, :, at]
        g1 = grad_ref[half1, :, at]
        first = first_ref[:, at]
        second = second_ref[:, at]
        early, later, chosen = block_probs(
            q0, q1, k0, k1, first, second, flag_ref[WHOLE], flag_ref[LATE]
        )

        def score_grads(probs, rows, values):
            prob_grads = [mm(rows, v, NT) for v in values]
            centre = sum((p * d).sum(axis=-1, keepdims=True) for p, d in zip(probs, prob_grads))
            return [(p * (d - centre)).astype(bf16) for p, d in zip(probs, prob_grads)]

        d00, d0c = score_grads(early, g0, (v0, first))
        d11, d10, d1c = score_grads(later, g1, (v1, v0, chosen))
        p00, p0c = [p.astype(bf16) for p in early]
        p11, p10, p1c = [p.astype(bf16) for p in later]
        base = slot * 3 * heads * HD + head * HD
        for_q, for_k, for_v = [
            slice(base + part * heads * HD, base + part * heads * HD + HD) for part in range(3)
        ]
        out_ref[half0, :, for_q] = ((mm(d00, k0) + mm(d0c, first)) * score_scale).astype(bf16)
        out_ref[half1, :, for_q] = (
            (mm(d11, k1) + mm(d10, k0) + mm(d1c, chosen)) * score_scale
        ).astype(bf16)
        out_ref[half0, :, for_k] = ((mm(d00, q0, TN) + mm(d10, q1, TN)) * score_scale).astype(bf16)
        out_ref[half1, :, for_k] = (mm(d11, q1, TN) * score_scale).astype(bf16)
        out_ref[half0, :, for_v] = (mm(p00, g0, TN) + mm(p10, g1, TN)).astype(bf16)
        out_ref[half1, :, for_v] = mm(p11, g1, TN).astype(bf16)
        from_early = mm(d0c, q0, TN) * score_scale + mm(p0c, g0, TN)
        from_later = mm(d1c, q1, TN) * score_scale + mm(p1c, g1, TN)
        returned_ref[:CTX, at] = (from_early + jnp.where(is_whole, from_later, 0.0)).astype(bf16)
        second_out_ref[:, at] = jnp.where(is_whole, 0.0, from_later)

    rate = rate_ref[...]
    decay = jnp.exp(-rate)

    def step(j, adjoint):
        g8 = second_out_ref[aligned((15 - j) * 8, 8), :]
        for k in range(7, -1, -1):
            adjoint = decay * adjoint + g8[k : k + 1]
        return adjoint

    adjoint = lax.fori_loop(0, 16, step, jnp.zeros_like(rate)) * jnp.exp(-float(CTX) * rate)
    for k, part in enumerate(split_three(adjoint)):
        returned_ref[CTX + k * STATES : CTX + (k + 1) * STATES, :] = part


def feed_forward(
    flag_ref, n_ref, c_ref, up0_ref, down0_ref, up1_ref, down1_ref, act_ref, gate_ref, sent_ref,
    down_out_ref, back_out_ref, acc_down, acc_back,
):
    step = pl.program_id(0)
    steps = pl.num_programs(0)
    per = steps // 2

    @pl.when(step == 0)
    def _():
        acc_down[...] = jnp.zeros_like(acc_down)
        acc_back[...] = jnp.zeros_like(acc_back)
        in_sent_order(flag_ref, n_ref, sent_ref)

    def body(up, down, slot):
        gate = mm(n_ref[...], up)
        cdf = 0.5 * (1.0 + lax.erf(gate * (1.0 / math.sqrt(2.0))))
        act = (gate * cdf).astype(bf16)
        slope = cdf + gate * jnp.exp(-0.5 * gate * gate) * (1.0 / math.sqrt(2.0 * math.pi))
        grad = (mm(c_ref[...], down, NT) * slope).astype(bf16)
        gate_ref[...] = grad
        hidden = act_ref.shape[1] // 2
        width = hidden // GROUP
        count = act.shape[1] // width
        for k in range(count):
            mask = jnp.bitwise_xor(flag_ref[PLACE], (step - slot * per) * count + k)
            to = (1 - mask % 2) * 4 + (mask // 2 % 2) * 2 + mask // 4
            act_ref[:, aligned(slot * hidden + to * width, width)] = act[
                :, k * width : (k + 1) * width
            ]
        acc_down[...] += mm(act, down)
        acc_back[...] += mm(grad, up, NT)

    @pl.when(step < per)
    def _():
        body(up0_ref[...], down0_ref[...], 0)

    @pl.when(step >= per)
    def _():
        body(up1_ref[...], down1_ref[...], 1)

    @pl.when(step == steps - 1)
    def _():
        down_out_ref[...] = acc_down[...].astype(down_out_ref.dtype)
        back_out_ref[...] = acc_back[...].astype(back_out_ref.dtype)


def run_feed_forward(flags, rows, cot, up, down, up_far, down_far, kind):
    tokens, width = rows.shape
    block = 512
    hidden = up.shape[1]
    per = hidden // block

    def near_at(j):
        return jnp.minimum(j, per - 1)

    def far_at(j):
        return jnp.maximum(j - per, 0)

    whole = pl.BlockSpec((tokens, width), lambda j: (0, 0))
    return pl.pallas_call(
        feed_forward,
        grid=(2 * per,),
        out_shape=(
            shape((tokens, 2 * hidden), bf16),
            shape((tokens, 2 * hidden), bf16),
            shape((tokens, width), bf16),
            shape((tokens, width), kind),
            shape((tokens, width), kind),
        ),
        in_specs=[
            pl.BlockSpec(memory_space=pltpu.SMEM),
            whole,
            whole,
            pl.BlockSpec((width, block), lambda j: (0, near_at(j))),
            pl.BlockSpec((block, width), lambda j: (near_at(j), 0)),
            pl.BlockSpec((width, block), lambda j: (0, far_at(j))),
            pl.BlockSpec((block, width), lambda j: (far_at(j), 0)),
        ],
        out_specs=(
            pl.BlockSpec((tokens, 2 * hidden), lambda j: (0, 0)),
            pl.BlockSpec((tokens, block), lambda j: (0, j)),
            whole,
            whole,
            whole,
        ),
        scratch_shapes=[pltpu.VMEM((tokens, width), f32), pltpu.VMEM((tokens, width), f32)],
        compiler_params=pltpu.CompilerParams(
            vmem_limit_bytes=24 * 1024 * 1024, dimension_semantics=("arbitrary",)
        ),
        cost_estimate=length(0),
    )(flags, rows, cot, up, down, up_far, down_far)


def products(lhs_refs, rhs_refs, columns, split=None):
    total = None
    for lhs_ref, rhs_ref in zip(lhs_refs, rhs_refs):
        term = mm(lhs_ref[:, columns], rhs_ref[...], TN)
        total = term if total is None else total + term
    return total


def down_pass(flag_ref, act0, act1, cot0, cot1, out_ref):
    hidden = act0.shape[1] // 2
    part = hidden // 4
    for slot in range(2):
        value = products(
            (act0, act1), (cot0, cot1), slice(slot * hidden, slot * hidden + hidden // 2)
        ).astype(bf16)
        out_ref[slot * part : (slot + 1) * part, :] = value[part:]
        out_ref[(2 + slot) * part : (3 + slot) * part, :] = value[:part]


def down_keep(flag_ref, act0, act1, cot0, cot1, core_ref, send_ref, left_ref):
    hidden = act0.shape[1] // 2
    part = hidden // 4
    for slot in range(2):
        value = products(
            (act0, act1), (cot0, cot1), slice(slot * hidden + hidden // 2, (slot + 1) * hidden)
        )
        to = slice(slot * part, (slot + 1) * part)
        send_ref[to, :] = (value[part:] + core_ref[to, :].astype(f32)).astype(bf16)
        left_ref[to, :] = value[:part] + core_ref[2 * part + to.start : 2 * part + to.stop, :].astype(
            f32
        )


def down_step(flag_ref, left_ref, received_ref, own_ref, send_ref):
    rows = own_ref.shape[0] // 2
    for slot in range(2):
        to = slice(slot * rows, (slot + 1) * rows)
        own = slice(2 * slot * rows, (2 * slot + 1) * rows)
        send = slice((2 * slot + 1) * rows, (2 * slot + 2) * rows)
        own_ref[to, :] = left_ref[own, :] + received_ref[own, :].astype(f32)
        send_ref[to, :] = (left_ref[send, :] + received_ref[send, :].astype(f32)).astype(bf16)


def y_first(value, rows):
    parts = [value[k * rows : (k + 1) * rows] for k in (1, 3, 0, 2)]
    return jnp.concatenate(parts[:2], 0), jnp.concatenate(parts[2:], 0)


def rows_pass(flag_ref, lhs0, lhs1, rhs0, rhs1, out_ref):
    half = lhs0.shape[1] // 2
    value = products((lhs0, lhs1), (rhs0, rhs1), slice(0, half)).astype(bf16)
    send, left = y_first(value, half // 4)
    out_ref[: half // 2, :] = send
    out_ref[half // 2 :, :] = left


def rows_keep(flag_ref, lhs0, lhs1, rhs0, rhs1, core_ref, send_ref, left_ref):
    half = lhs0.shape[1] // 2
    value = products((lhs0, lhs1), (rhs0, rhs1), slice(half, 2 * half))
    send, left = y_first(value, half // 4)
    send_ref[...] = (send + core_ref[: half // 2, :].astype(f32)).astype(bf16)
    left_ref[...] = left + core_ref[half // 2 :, :].astype(f32)


def up_step(flag_ref, left_ref, received_ref, own_ref, send_ref):
    rows = own_ref.shape[0]
    own_ref[...] = left_ref[:rows, :] + received_ref[:rows, :].astype(f32)
    send_ref[...] = (left_ref[rows:, :] + received_ref[rows:, :].astype(f32)).astype(bf16)


def own_down(flag_ref, own_ref, received_ref, near_ref, far_ref):
    rows = near_ref.shape[0]
    near_ref[...] = own_ref[:rows, :] + received_ref[:rows, :].astype(f32)
    far_ref[...] = (own_ref[rows:, :] + received_ref[rows:, :].astype(f32)).astype(bf16)


def own_up(flag_ref, own_ref, received_ref, near_ref, far_ref):
    width = near_ref.shape[1]
    near_ref[...] = own_ref[:, :width] + received_ref[:, :width].astype(f32)
    far_ref[...] = (own_ref[:, width:] + received_ref[:, width:].astype(f32)).astype(bf16)


def attn_pass(flag_ref, one0, one1, dqkv0, dqkv1, back0, back1, att0, att1, att2, att3, out_ref):
    half = one0.shape[1] // 2
    width = dqkv0.shape[1]
    channels = att0.shape[1]
    columns = slice(0, half)
    out_ref[:, :width] = products((one0, one1), (dqkv0, dqkv1), columns).astype(bf16)
    for slot, pair in enumerate(((att0, att1), (att2, att3))):
        at = width + slot * channels
        out_ref[:, at : at + channels] = products((back0, back1), pair, columns).astype(bf16)


def attn_keep(
    flag_ref, one0, one1, dqkv0, dqkv1, back0, back1, att0, att1, att2, att3, core_ref, own_ref,
    *send_refs,
):
    half = one0.shape[1] // 2
    rows = half // 4
    width = dqkv0.shape[1]
    channels = att0.shape[1]
    columns = slice(half, 2 * half)
    blocks = [(0, products((one0, one1), (dqkv0, dqkv1), columns))]
    for slot, pair in enumerate(((att0, att1), (att2, att3))):
        blocks.append((width + slot * channels, products((back0, back1), pair, columns)))
    for at, block in blocks:
        to = slice(at, at + block.shape[1])
        block = block + core_ref[:, to].astype(f32)
        own_ref[:, to] = block[:rows]
        for k, ref in enumerate(send_refs):
            ref[:, to] = block[(k + 1) * rows : (k + 2) * rows].astype(bf16)


def attn_own(
    flag_ref, own_ref, r1_ref, r2_ref, r3_ref, param_ref, gains_ref, gains_received, near_ref,
    far_ref,
):
    rows = own_ref.shape[0]
    total = own_ref[...] + (
        r1_ref[...].astype(f32) + r2_ref[...].astype(f32) + r3_ref[...].astype(f32)
    )
    channels = total.shape[1] // 8
    gains = gains_ref[...] + gains_received[...]
    for slot, ref in enumerate((near_ref, far_ref)):
        ref[:rows, : 3 * channels] = total[:, slot * 3 * channels : (slot + 1) * 3 * channels].astype(
            ref.dtype
        )
        ref[:rows, 3 * channels :] = total[
            :, (6 + slot) * channels : (7 + slot) * channels
        ].astype(ref.dtype)
        small = jnp.concatenate(
            [param_ref[:, slot * channels : (slot + 1) * channels], gains], axis=0
        )
        count = small.shape[0] // 4
        rest = jnp.zeros((ref.shape[0] - rows - count, channels), f32)
        for quarter in range(4):
            ref[rows:, quarter * channels : (quarter + 1) * channels] = jnp.concatenate(
                [small[quarter * count : (quarter + 1) * count], rest], axis=0
            ).astype(ref.dtype)


def add_two(flag_ref, a_ref, b_ref, out_ref):
    out_ref[...] = (a_ref[...].astype(f32) + b_ref[...].astype(f32)).astype(out_ref.dtype)


def add_three(flag_ref, a_ref, b_ref, c_ref, out_ref):
    out_ref[...] = (a_ref[...] + b_ref[...] + c_ref[...].astype(f32)).astype(out_ref.dtype)


def sources(flag_ref, even_ref, odd_ref, rows):
    for pair in range(GROUP // 2):
        for side, ref in enumerate((even_ref, odd_ref)):
            source = jnp.bitwise_xor(flag_ref[PLACE], 2 * pair + side)
            yield ref, pair, aligned(source * rows, rows)


def assemble_weight(flag_ref, even_ref, odd_ref, tile_ref, weight_ref, out_ref, qkv_ref):
    split = weight_ref.shape[1]
    for ref, pair, at in sources(flag_ref, even_ref, odd_ref, even_ref.shape[1]):
        weight_ref[at, :] = ref[pair, :, :split]
        out_ref[at, :] = ref[pair, :, split:]
    project(flag_ref, tile_ref, weight_ref, qkv_ref)


def assemble_grad(
    flag_ref, even_ref, odd_ref, qkv_ref, out_ref, rate_ref, coef_ref, skip_ref, gain_one_ref,
    gain_two_ref,
):
    channels = qkv_ref.shape[2]
    rows = qkv_ref.shape[1] // GROUP
    total = None
    for ref, pair, at in sources(flag_ref, even_ref, odd_ref, rows):
        for part in range(3):
            qkv_ref[part, at, :] = ref[
                pair, :rows, part * channels : (part + 1) * channels
            ].astype(f32)
        out_ref[:, at] = ref[pair, :rows, 3 * channels :].astype(f32).T
        term = ref[pair, rows:, :].astype(f32)
        total = term if total is None else total + term
    count = (2 * STATES + 8 + 8) // 4

    def row(k):
        return total[k % count : k % count + 1, k // count * channels : (k // count + 1) * channels]

    for k in range(STATES):
        rate_ref[k : k + 1, :] = row(k)
        coef_ref[k : k + 1, :] = row(STATES + k)
    skip_ref[...] = row(2 * STATES)
    for which, ref in enumerate((gain_one_ref, gain_two_ref)):
        for k in range(4):
            ref[:, k * channels : (k + 1) * channels] = row(2 * STATES + 8 + which * 4 + k)


def stack_two(flag_ref, a_ref, ax_ref, b_ref, by_ref, a_out, b_out):
    a_out[0], a_out[1] = a_ref[...], ax_ref[...]
    b_out[0], b_out[1] = b_ref[...], by_ref[...]


def stack_three(flag_ref, a_ref, ax_ref, b_ref, by_ref, a_out, b_out, both_out):
    stack_two(flag_ref, a_ref, ax_ref, b_ref, by_ref, a_out, b_out)
    both_out[0, 0], both_out[0, 1] = a_ref[...], b_ref[...]
    both_out[1, 0], both_out[1, 1] = ax_ref[...], by_ref[...]


def stack_pairs(flag_ref, a_ref, b_ref, out_ref):
    out_ref[0, 0], out_ref[0, 1] = a_ref[0], b_ref[0]
    out_ref[1, 0], out_ref[1, 1] = a_ref[1], b_ref[1]


def stack_four(flag_ref, a_ref, b_ref, c_ref, d_ref, out_ref):
    for k, ref in enumerate((a_ref, b_ref, c_ref, d_ref)):
        out_ref[k] = ref[...]


def stack_eight(flag_ref, a_ref, ay_ref, b_ref, bx_ref, out_ref):
    out_ref[0, 0], out_ref[1, 0] = a_ref[0], a_ref[1]
    out_ref[2, 0], out_ref[3, 0] = ay_ref[0], ay_ref[1]
    out_ref[0, 1], out_ref[2, 1] = b_ref[0], b_ref[1]
    out_ref[1, 1], out_ref[3, 1] = bx_ref[0], bx_ref[1]


def place_two(flag_ref, even_ref, odd_ref, a_out, b_out):
    for ref, pair, at in sources(flag_ref, even_ref, odd_ref, even_ref.shape[2]):
        a_out[at, :] = ref[pair, 0].astype(a_out.dtype)
        b_out[at, :] = ref[pair, 1].astype(b_out.dtype)


def place_wide(flag_ref, own_ref, other_ref, *refs):
    for side, ref in enumerate((own_ref, other_ref)):

        @pl.when(pl.program_id(0) % 2 == side)
        def _():
            refs[-2][...] = ref[0, 0].astype(f32)
            refs[-1][...] = ref[0, 1].astype(f32)


def run_place_wide(flags, own, other, starts, steps, filled=()):
    rows, width = own.shape[2:]
    piece = pl.BlockSpec((1, 2, rows, width), lambda j, flag_ref: (j // 2, 0, 0, 0))

    def place(which):
        return pl.BlockSpec(
            (rows, width),
            lambda j, flag_ref: (
                jnp.bitwise_xor(
                    flag_ref[PLACE], starts[which] + (j // 2) * steps[which] + j % 2
                ),
                0,
            ),
        )

    out = shape((GROUP * rows, width))
    return pl.pallas_call(
        place_wide,
        grid_spec=pltpu.PrefetchScalarGridSpec(
            num_scalar_prefetch=1,
            grid=(GROUP // 2,),
            in_specs=[piece, piece] + [pl.BlockSpec(memory_space=pl.ANY)] * len(filled),
            out_specs=(place(0), place(1)),
        ),
        out_shape=(out, out),
        input_output_aliases={3 + k: k for k in range(len(filled))},
        compiler_params=pltpu.CompilerParams(vmem_limit_bytes=VMEM_LIMIT),
        cost_estimate=length(0),
    )(flags, own, other, *filled)


class Order:
    def __init__(self):
        self.last = ()

    def __call__(self, *values):
        tied = lax.optimization_barrier((values, self.last))[0]
        return tied[0] if len(tied) == 1 else tied

    def done(self, result):
        self.last = result
        return result


def per_device(
    inputs,
    block_size,
    gain_attn,
    qkv_weight,
    ssm_rate,
    ssm_coef,
    ssm_skip,
    out_weight,
    gain_mlp,
    up_weight,
    down_weight,
    cotangent,
    dp_size,
):
    z = lax.axis_index("mp")
    place = jnp.bitwise_and(lax.axis_index("dp"), GROUP - 1)

    def swap_mp(value, mask):
        return lax.ppermute(value, "mp", [(k, k ^ mask) for k in range(4)])

    def swap_dp(value, mask):
        return lax.ppermute(value, "dp", [(k, k ^ mask) for k in range(dp_size)])

    def gather_by_xor(piece):
        return [piece] + [swap_dp(piece, 2 * k) for k in range(1, GROUP // 2)]

    def low(*dims):
        return shape(dims, bf16)

    def over_groups(own):
        mask = GROUP
        while mask < dp_size:
            own = own + swap_dp(own.astype(bf16), mask).astype(f32)
            mask *= 2
        return own.astype(bf16)

    model_dim = inputs.shape[2]
    channels = qkv_weight.shape[2]
    hidden = up_weight.shape[1]
    wide = 2 * channels
    rows = model_dim // GROUP
    row = inputs[0]
    cot = cotangent[0]
    z_far = jnp.bitwise_xor(z, 2)
    whole = (block_size[0] > HALF).astype(jnp.int32)
    flags = jnp.stack(
        [whole, jnp.right_shift(z, 1), jnp.bitwise_and(z, 1), z, z_far, place]
    ).astype(jnp.int32)
    gain_one = gain_attn[None]
    gain_two = gain_mlp[None]
    order = Order()
    half = shape((HALF, model_dim))
    half_low = shape((HALF, model_dim), bf16)

    normed_one = order.done(call(norm_one, half_low)(flags, row, gain_one))
    paired_one = swap_mp(normed_one, 1)
    qkv_parts = jnp.transpose(qkv_weight, (1, 0, 2))
    attn_slice, up_slice, down_slice, ssm_pack = order.done(
        run_cut_slices(
            flags, order(qkv_parts), out_weight, up_weight, down_weight, ssm_rate.T, ssm_coef.T,
            ssm_skip[None],
        )
    )
    attn_across = swap_mp(attn_slice, 2)
    near_qkv = order.done(jnp.concatenate(list(order(*[qkv_parts[k] for k in range(3)])), 1))

    paired_one, attn_across = order.done(order(paired_one, attn_across))
    attn_own_slice = attn_across[:rows]
    attn_x = swap_dp(attn_own_slice, 2)
    attn_y = swap_dp(attn_own_slice, 4)
    up_across = swap_mp(order(up_slice), 2)
    paired_cot = swap_mp(order(cot), 1)
    ssm_both = call(join_ssm, shape((48, wide)))(flags, ssm_pack, attn_across)
    rate_t, coef_t, skip_t = ssm_both[:16], ssm_both[16:32], ssm_both[32:33]
    tile_one, one_sent, second_local, handed = order.done(
        call(
            ssm_forward,
            (
                shape((2, HALF, model_dim), bf16),
                shape((2, HALF, model_dim), bf16),
                shape((CTX, wide)),
                shape((CTX + 3 * STATES, wide), bf16),
            ),
            scratch=[pltpu.VMEM((2 * HALF, wide), f32)],
        )(flags, normed_one, order(paired_one), rate_t, coef_t, skip_t)
    )
    handed = lax.ppermute(handed, "mp", [(0, 2), (1, 3)])

    qkv_shape = shape((2, HALF, 3 * channels), bf16)
    att_shape = shape((2, HALF, channels), bf16)
    attn_x = order.done(order(attn_x))
    attn_xy = swap_dp(attn_x, 4)
    attn_y, paired_cot, mlp_up = order.done(order(attn_y, paired_cot, up_across))
    mlp_up_x = swap_dp(mlp_up, 2)
    qkv_near = order.done(call(project, qkv_shape)(flags, order(tile_one), near_qkv))
    even = order.done(
        call(stack_four, shape((4,) + attn_x.shape, bf16))(
            flags, attn_own_slice, attn_x, attn_y, order(attn_xy)
        )
    )
    odd_part = swap_dp(even, 1)
    slice_shape = low(rows, model_dim)
    handed = order.done(order(handed))
    down_across = swap_mp(order(down_slice), 2)
    ctx_first, ctx_second, enter_state = order.done(
        call(
            ssm_carry_in,
            (shape((CTX, wide), bf16), shape((CTX, wide), bf16), shape((STATES, wide))),
            scratch=[pltpu.VMEM((CTX, wide), f32)],
            micros=16,
        )(flags, order(second_local), handed, rate_t, coef_t)
    )
    att_near = order.done(
        call(attention_near, att_shape)(flags, order(qkv_near), ctx_first, ctx_second)
    )
    far_qkv, far_out, qkv_far = order.done(
        call(
            assemble_weight,
            (
                shape((model_dim, 3 * channels), bf16),
                shape((model_dim, channels), bf16),
                qkv_shape,
            ),
        )(flags, even, order(odd_part), tile_one)
    )
    att_far, out_own, out_send = order.done(
        call(attention_far, (att_shape, half, half_low))(
            flags, order(qkv_far), ctx_first, ctx_second, att_near, out_weight, far_out
        )
    )
    out_received = swap_mp(out_send, 1)
    pair_shape = low(2, rows, model_dim)
    mlp_down = order.done(order(down_across))
    mlp_down_y = swap_dp(mlp_down, 4)
    mlp_up_two, mlp_down_two = order.done(
        call(stack_two, (pair_shape, pair_shape), micros=0.5)(
            flags, mlp_up, order(mlp_up_x), mlp_down, order(mlp_down_y)
        )
    )
    mlp_up_y = swap_dp(mlp_up_two, 4)
    mlp_down_x = swap_dp(mlp_down_two, 2)
    middle, normed_two = order.done(
        call(norm_two, (half, half_low), micros=3)(
            flags, row, out_own, order(out_received), gain_two
        )
    )

    paired_two = swap_mp(normed_two, 1)
    eight_shape = low(GROUP // 2, 2, rows, model_dim)
    mlp_even = order.done(
        call(stack_eight, eight_shape, micros=1)(
            flags, mlp_up_two, order(mlp_up_y), mlp_down_two, order(mlp_down_x)
        )
    )
    mlp_odd = swap_dp(mlp_even, 1)
    paired_two = order(paired_two)
    warm = order.done(
        call(touch, shape((16, 128), bf16), micros=30)(
            flags, up_weight, down_weight, cot, paired_cot, paired_two
        )
    )
    up_far, down_far = order.done(
        call(place_two, (low(model_dim, hidden), low(hidden, model_dim)))(
            flags, mlp_even, order(mlp_odd)
        )
    )
    mlp = (up_weight, down_weight, up_far, down_far)
    act_other, gate_other, two_other, down_send, back_send = order.done(
        run_feed_forward(flags, order(paired_two), paired_cot, *mlp, bf16)
    )
    back_received = swap_mp(back_send, 1)
    act_own, gate_own, two_own, down_own, back_own = order.done(
        run_feed_forward(flags, order(normed_two), cot, *mlp, f32)
    )

    side = model_dim // 2
    acts = (act_own, act_other, cot, paired_cot)
    passed = order.done(call(down_pass, low(hidden, model_dim))(flags, order(act_own), *acts[1:]))
    down_core = swap_dp(passed, 1)
    ups = (two_own, two_other, gate_own, gate_other)
    passed = order.done(call(rows_pass, low(side, 2 * hidden))(flags, order(two_own), *ups[1:]))
    up_core = swap_dp(passed, 1)
    middle_grad, attn_grad, gain_mlp_grad = order.done(
        call(norm_two_back, (half, half_low, shape((1, model_dim))), micros=12)(
            flags, middle, back_own, order(back_received), cot, gain_two, warm
        )
    )
    paired_back = swap_mp(attn_grad, 1)
    down_send_x, down_left = order.done(
        call(down_keep, (low(side, model_dim), shape((side, model_dim))))(
            flags, *acts, order(down_core)
        )
    )
    down_x = swap_dp(down_send_x, 2)
    up_send_y, up_left = order.done(
        call(rows_keep, (low(side // 2, 2 * hidden), shape((side // 2, 2 * hidden))))(
            flags, *ups, order(up_core)
        )
    )
    up_y = swap_dp(up_send_y, 4)

    att_grad, back_sent = order.done(
        call(
            attended_grads,
            (shape((2, HALF, wide), bf16), shape((2, HALF, model_dim), bf16)),
            micros=4,
        )(flags, attn_grad, order(paired_back), out_weight, far_out)
    )
    down_received = swap_mp(order(down_send), 1)
    dqkv, second_grad, returned = order.done(
        call(
            attention_backward,
            (
                shape((2, HALF, 6 * channels), bf16),
                shape((CTX, wide)),
                shape((CTX + 3 * STATES, wide), bf16),
            ),
        )(flags, qkv_near, qkv_far, ctx_first, ctx_second, order(att_grad), rate_t)
    )
    returned = lax.ppermute(returned, "mp", [(2, 0), (3, 1)])
    one_total = order.done(
        call(qkv_back, shape((2, HALF, model_dim)))(flags, order(dqkv), near_qkv, far_qkv)
    )
    attns = (
        one_sent[0], one_sent[1], dqkv[0], dqkv[1], back_sent[0], back_sent[1],
        att_near[0], att_near[1], att_far[0], att_far[1],
    )
    passed = order.done(
        call(attn_pass, low(side, 8 * channels))(flags, order(attns[0]), *attns[1:])
    )
    attn_core = swap_dp(passed, 1)
    down_mine, down_send_y = order.done(
        call(down_step, (shape((2 * rows, model_dim)), low(2 * rows, model_dim)))(
            flags, down_left, order(down_x)
        )
    )
    down_y = swap_dp(down_send_y, 4)
    up_mine, up_send_x = order.done(
        call(up_step, (shape((rows, 2 * hidden)), low(rows, 2 * hidden)))(
            flags, up_left, order(up_y)
        )
    )
    up_x = swap_dp(up_send_x, 2)
    one_own, one_send, last_grad, enter_adjoint = order.done(
        call(
            ssm_signal_grad,
            (half, half_low, shape((CTX, wide)), shape((STATES, wide))),
            scratch=[pltpu.VMEM((2 * HALF, wide), f32), pltpu.VMEM((HALF, model_dim), f32)],
            micros=30,
        )(flags, second_grad, order(returned), rate_t, coef_t, skip_t, one_total)
    )
    one_received = swap_mp(one_send, 1)
    down_received = order.done(order(down_received))
    attn_mine, *attn_sends = order.done(
        call(attn_keep, (shape((rows, 8 * channels)),) + (low(rows, 8 * channels),) * 3)(
            flags, *attns, order(attn_core)
        )
    )
    attn_sent = [swap_dp(part, SENT[5 + k]) for k, part in enumerate(attn_sends)]
    wide_slice = shape((rows, model_dim))
    down_near, down_far_grad = order.done(
        call(own_down, (wide_slice, slice_shape))(flags, down_mine, order(down_y))
    )
    down_received_far = swap_mp(down_far_grad, 2)
    up_near, up_far_grad = order.done(
        call(own_up, (wide_slice, slice_shape))(flags, up_mine, order(up_x))
    )
    up_received_far = swap_mp(up_far_grad, 2)
    param_grad = order.done(
        call(
            ssm_param_grad,
            shape((40, wide)),
            scratch=[pltpu.VMEM((2 * HALF, wide), f32)],
            micros=3,
        )(
            flags, order(tile_one), second_grad, last_grad, enter_state, enter_adjoint, rate_t, coef_t
        )
    )
    input_grad, gains = order.done(
        call(norm_one_back, (half, shape((2 * model_dim // channels, channels))))(
            flags, row, one_own, order(one_received), middle_grad, gain_one, gain_mlp_grad
        )
    )
    gains_received = swap_mp(gains, 1)
    down_mine = order.done(
        call(add_two, slice_shape)(flags, down_near, order(down_received_far))
    )
    down_mine = over_groups(down_mine)
    down_x = swap_dp(down_mine, 2)
    up_mine = order.done(call(add_two, slice_shape)(flags, up_near, order(up_received_far)))
    up_mine = over_groups(up_mine)
    up_y = swap_dp(up_mine, 4)
    slice_rows = rows + 16
    *attn_sent, gains_received = order(*attn_sent, gains_received)
    attn_near, attn_send = order.done(
        call(attn_own, (shape((slice_rows, 4 * channels)), low(slice_rows, 4 * channels)))(
            flags, attn_mine, *attn_sent, param_grad, gains, gains_received
        )
    )
    attn_received = swap_mp(attn_send, 2)
    both_shape = low(2, 2, rows, model_dim)
    down_two, up_two, first_pieces = order.done(
        call(stack_three, (pair_shape, pair_shape, both_shape), micros=3)(
            flags, down_mine, order(down_x), up_mine, order(up_y)
        )
    )
    down_y = swap_dp(down_two, 4)
    up_x = swap_dp(up_two, 2)
    first_others = swap_dp(first_pieces, 1)
    output = order.done(
        call(add_three, half_low)(flags, middle, order(down_own), down_received)
    )
    attn_slice_grad = order.done(
        call(add_two, low(slice_rows, 4 * channels), micros=20)(
            flags, attn_near, order(attn_received)
        )
    )
    first_others = order.done(order(first_others))
    attn_slice_grad = over_groups(order(attn_slice_grad))
    attn_sent = [swap_dp(attn_slice_grad, 2 * k) for k in range(1, GROUP // 2)]
    wide_grads = order.done(
        run_place_wide(flags, first_pieces, order(first_others), (0, 0), (2, 4))
    )
    even = order.done(
        call(stack_four, low(4, slice_rows, 4 * channels))(
            flags, attn_slice_grad, *order(*attn_sent)
        )
    )
    odd_part = swap_dp(even, 1)
    last_pieces = order.done(
        call(stack_pairs, both_shape, micros=8)(flags, *order(down_y, up_x))
    )
    last_others = swap_dp(last_pieces, 1)
    qkv_grad, out_grad, rate_grad, coef_grad, skip_grad, gain_one_grad, gain_two_grad = order.done(
        call(
            assemble_grad,
            (
                shape((3, model_dim, channels)),
                shape(out_weight.shape),
                shape((STATES, channels)),
                shape((STATES, channels)),
                shape((1, channels)),
                shape((1, model_dim)),
                shape((1, model_dim)),
            ),
            micros=8,
        )(flags, even, order(odd_part))
    )
    down_grad, up_grad = run_place_wide(
        flags, last_pieces, order(last_others), (4, 2), (2, 4), wide_grads
    )
    return (
        output[None],
        input_grad[None],
        gain_one_grad[0],
        jnp.transpose(qkv_grad, (1, 0, 2)),
        rate_grad.T,
        coef_grad.T,
        skip_grad[0],
        out_grad,
        gain_two_grad[0],
        up_grad,
        down_grad,
    )


def solution(mesh):
    return jax.shard_map(
        partial(per_device, dp_size=mesh.shape["dp"]),
        mesh=mesh,
        in_specs=(
            P("dp", "mp", None),
            P("dp"),
            P(),
            P(None, None, "mp"),
            P("mp", None),
            P("mp", None),
            P("mp"),
            P("mp", None),
            P(),
            P(None, "mp"),
            P("mp", None),
            P("dp", "mp", None),
        ),
        out_specs=(
            P("dp", "mp", None),
            P("dp", "mp", None),
            P(),
            P(None, None, "mp"),
            P("mp", None),
            P("mp", None),
            P("mp"),
            P("mp", None),
            P(),
            P(None, "mp"),
            P("mp", None),
        ),
        check_vma=False,
    )
```

```python
from functools import partial
import math

import jax
import jax.numpy as jnp
from jax import lax
from jax.experimental import pallas as pl
from jax.experimental.pallas import tpu as pltpu
from jax.sharding import PartitionSpec as P

HD = 128
CTX = 128
HALF = 256
STATES = 16
GROUP = 8

f32 = jnp.float32
bf16 = jnp.bfloat16
epsilon = 1e-05
masked_score = -1e30
score_scale = 1.0 / math.sqrt(HD)
VMEM_LIMIT = 16 * 1024 * 1024

NT = (((1,), (1,)), ((), ()))
TN = (((0,), (0,)), ((), ()))
NN = (((1,), (0,)), ((), ()))

WHOLE, LATE, ODD, NEAR, FAR, PLACE = range(6)


def mm(a, b, dims=NN):
    return lax.dot_general(a, b, dims, preferred_element_type=f32)


def shape(dims, dtype=f32):
    return jax.ShapeDtypeStruct(dims, dtype)


def length(micros):
    return pl.CostEstimate(flops=int(micros * 1e9), bytes_accessed=0, transcendentals=0)


def call(kernel, out_shape, scratch=(), micros=0):
    def run(flags, *args):
        vmem = pl.BlockSpec(memory_space=pltpu.VMEM)
        return pl.pallas_call(
            kernel,
            out_shape=out_shape,
            in_specs=[pl.BlockSpec(memory_space=pltpu.SMEM)] + [vmem] * len(args),
            out_specs=jax.tree.map(lambda _: vmem, out_shape),
            scratch_shapes=scratch,
            compiler_params=pltpu.CompilerParams(vmem_limit_bytes=VMEM_LIMIT),
            cost_estimate=length(micros),
        )(flags, *args)

    return run


SENT = (1, 5, 3, 7, 0, 4, 2, 6)


def in_sent_order(flag_ref, value_ref, out_ref, masks=SENT):
    width = value_ref.shape[1] // GROUP
    for k, mask in enumerate(masks):
        source = jnp.bitwise_xor(flag_ref[PLACE], mask)
        out_ref[:, k * width : (k + 1) * width] = value_ref[:, aligned(source * width, width)]


def aligned(start, size):
    return pl.ds(pl.multiple_of(start, size), size)


def cut_slices(
    flag_ref, qkv_ref, out_ref, up_ref, down_ref, rate_ref, coef_ref, skip_ref, attn_ref, up_slice,
    down_slice, ssm_ref, out_slice, *sems,
):
    rows = up_slice.shape[0]
    channels = out_slice.shape[0]
    count = ssm_ref.shape[0]
    ssm_ref[:STATES, :] = rate_ref[...]
    ssm_ref[STATES : 2 * STATES, :] = coef_ref[...]
    ssm_ref[2 * STATES :, :] = jnp.zeros((count - 2 * STATES, channels), f32)
    ssm_ref[2 * STATES : 2 * STATES + 1, :] = skip_ref[...]
    for k, part in enumerate(split_three(ssm_ref[...])):
        attn_ref[rows : rows + count, k * channels : (k + 1) * channels] = part
    attn_ref[rows : rows + count, 3 * channels :] = jnp.zeros((count, channels), bf16)
    at = aligned(flag_ref[PLACE] * rows, rows)
    copies = [
        pltpu.make_async_copy(
            qkv_ref.at[part, at, :],
            attn_ref.at[:rows, part * channels : (part + 1) * channels],
            sems[part],
        )
        for part in range(3)
    ] + [
        pltpu.make_async_copy(out_ref.at[:, at], out_slice, sems[3]),
        pltpu.make_async_copy(up_ref.at[at, :], up_slice, sems[4]),
        pltpu.make_async_copy(down_ref.at[at, :], down_slice, sems[5]),
    ]
    for copy in copies:
        copy.start()
    for copy in copies:
        copy.wait()
    attn_ref[:rows, 3 * channels :] = out_slice[...].T


def join_ssm(flag_ref, own_ref, across_ref, out_ref):
    channels = own_ref.shape[1]
    start = across_ref.shape[0] - own_ref.shape[0]
    out_ref[:, :channels] = own_ref[...]
    parts = [across_ref[start:, k * channels : (k + 1) * channels].astype(f32) for k in range(3)]
    out_ref[:, channels:] = (parts[0] + parts[1]) + parts[2]


def run_cut_slices(flags, qkv_parts, out_weight, up_weight, down_weight, *ssm_parts):
    channels = qkv_parts.shape[2]
    width = out_weight.shape[1]
    rows = width // GROUP
    vmem = pl.BlockSpec(memory_space=pltpu.VMEM)
    return pl.pallas_call(
        cut_slices,
        in_specs=[pl.BlockSpec(memory_space=pltpu.SMEM)]
        + [pl.BlockSpec(memory_space=pltpu.HBM)] * 4
        + [vmem] * 3,
        out_specs=(vmem,) * 4,
        out_shape=(
            shape((rows + 48, 4 * channels), bf16),
            shape((rows, width), bf16),
            shape((rows, width), bf16),
            shape((48, channels)),
        ),
        scratch_shapes=[pltpu.VMEM((channels, rows), bf16)] + [pltpu.SemaphoreType.DMA] * 6,
        compiler_params=pltpu.CompilerParams(vmem_limit_bytes=56 * 1024 * 1024),
        cost_estimate=length(0),
    )(flags, qkv_parts, out_weight, up_weight, down_weight, *ssm_parts)


def normalise(values):
    mean = jnp.mean(values, axis=-1, keepdims=True)
    centred = values - mean
    spread = jnp.mean(centred * centred, axis=-1, keepdims=True)
    inverse = lax.rsqrt(spread + epsilon)
    return centred * inverse, inverse


def normalise_back(grad, gain, hat, inverse):
    inner = grad * gain
    return (
        inner
        - jnp.mean(inner, axis=-1, keepdims=True)
        - hat * jnp.mean(inner * hat, axis=-1, keepdims=True)
    ) * inverse


def by_rows(body, rows, block=64):
    for k in range(rows // block):
        body(slice(k * block, (k + 1) * block))


def norm_one(flag_ref, x_ref, gain_ref, out_ref):
    def body(at):
        hat, _ = normalise(x_ref[at, :].astype(f32))
        out_ref[at, :] = (hat * gain_ref[...]).astype(bf16)

    by_rows(body, x_ref.shape[0])


def touch(flag_ref, up_ref, down_ref, cot_ref, paired_ref, rows_ref, out_ref):
    out_ref[...] = (
        (up_ref[:16, :128] + down_ref[:16, :128])
        + (cot_ref[:16, :128] + paired_ref[:16, :128])
        + rows_ref[:16, :128]
    )


def norm_two(flag_ref, x_ref, own_ref, received_ref, gain_ref, middle_ref, out_ref):
    def body(at):
        middle = x_ref[at, :].astype(f32) + own_ref[at, :] + received_ref[at, :].astype(f32)
        middle_ref[at, :] = middle
        hat, _ = normalise(middle)
        out_ref[at, :] = (hat * gain_ref[...]).astype(bf16)

    by_rows(body, x_ref.shape[0])


def norm_two_back(
    flag_ref, middle_ref, own_ref, received_ref, cot_ref, gain_ref, warm_ref, grad_ref, low_ref,
    gain_out_ref,
):
    sums = []

    def body(at):
        hat, inverse = normalise(middle_ref[at, :])
        grad = own_ref[at, :] + received_ref[at, :].astype(f32)
        sums.append(jnp.sum(grad * hat, axis=0, keepdims=True))
        total = cot_ref[at, :].astype(f32) + normalise_back(grad, gain_ref[...], hat, inverse)
        grad_ref[at, :] = total
        low_ref[at, :] = total.astype(bf16)

    by_rows(body, middle_ref.shape[0])
    gain_out_ref[...] = sum(sums)


def norm_one_back(
    flag_ref, x_ref, own_ref, received_ref, middle_ref, gain_ref, gain_two_grad_ref, grad_ref,
    gain_out_ref,
):
    sums = []

    def body(at):
        hat, inverse = normalise(x_ref[at, :].astype(f32))
        grad = own_ref[at, :] + received_ref[at, :].astype(f32)
        sums.append(jnp.sum(grad * hat, axis=0, keepdims=True))
        grad_ref[at, :] = middle_ref[at, :] + normalise_back(grad, gain_ref[...], hat, inverse)

    by_rows(body, x_ref.shape[0])
    width = gain_out_ref.shape[1]
    pieces = x_ref.shape[1] // width
    for which, value in enumerate((sum(sums), gain_two_grad_ref[...])):
        for k in range(pieces):
            row = which * pieces + k
            gain_out_ref[row : row + 1, :] = value[:, k * width : (k + 1) * width]


def split_three(value):
    high = value.astype(bf16)
    rest = value - high.astype(f32)
    middle = rest.astype(bf16)
    return [high, middle, (rest - middle.astype(f32)).astype(bf16)]


def join_three(ref, start, lanes):
    parts = [ref[start + k * STATES : start + (k + 1) * STATES, lanes] for k in range(3)]
    return (parts[0].astype(f32) + parts[1].astype(f32)) + parts[2].astype(f32)


def sums_over_states(parts):
    parts = [part[:8] + part[8:] for part in parts]
    rows = lax.broadcasted_iota(jnp.int32, parts[0].shape, 0)
    distance = 1
    while len(parts) > 1:
        first = jnp.bitwise_and(rows, distance) == 0
        parts = [
            jnp.where(first, a, b) + pltpu.roll(jnp.where(first, b, a), distance, 0)
            for a, b in zip(parts[::2], parts[1::2])
        ]
        distance *= 2
    return parts[0]


def load_signal(flag_ref, tile_ref, xs):
    channels = xs.shape[1] // 2
    for half in range(2):
        source = jnp.bitwise_xor(flag_ref[ODD], half)
        for slot, name in enumerate((NEAR, FAR)):
            xs[half * HALF : (half + 1) * HALF, slot * channels : (slot + 1) * channels] = tile_ref[
                source, :, aligned(flag_ref[name] * channels, channels)
            ].astype(f32)


def ssm_forward(
    flag_ref, own_ref, other_ref, rate_ref, coef_ref, skip_ref, tile_ref, sent_ref,
    second_ref, handed_ref, xs,
):
    tile_ref[0] = own_ref[...]
    tile_ref[1] = other_ref[...]
    in_sent_order(flag_ref, own_ref, sent_ref.at[0])
    in_sent_order(flag_ref, other_ref, sent_ref.at[1])
    load_signal(flag_ref, tile_ref, xs)
    decay = jnp.exp(-rate_ref[...])
    coef = coef_ref[...]
    skip = skip_ref[...]

    def step(eight, state, chunk):
        x8 = xs[aligned((chunk * 16 + eight) * 8, 8), :]
        rows = []
        for k in range(8):
            state = decay * state + x8[k : k + 1]
            if chunk % 2:
                rows.append(coef * state)
        if chunk % 2:
            y8 = sums_over_states(rows) + skip * x8
            at = aligned(eight * 8, 8)
            if chunk == 1:
                second_ref[at, :] = y8
            else:
                xs[at, :] = y8
        return state

    state = jnp.zeros_like(decay)
    for chunk in range(4):
        state = lax.fori_loop(0, 16, partial(step, chunk=chunk), state)
    handed_ref[:CTX, :] = xs[:CTX, :].astype(bf16)
    for k, part in enumerate(split_three(state)):
        handed_ref[CTX + k * STATES : CTX + (k + 1) * STATES, :] = part


def project(flag_ref, tile_ref, weight_ref, qkv_ref):
    for half in range(2):
        qkv_ref[half] = mm(tile_ref[half], weight_ref[...]).astype(bf16)


def ssm_carry_in(
    flag_ref, local_ref, handed_ref, rate_ref, coef_ref, first_ref, second_ref, enter_ref, acc
):
    channels = rate_ref.shape[1] // 2
    for slot in range(2):
        to = slice(slot * channels, (slot + 1) * channels)
        source = slice((1 - slot) * channels, (2 - slot) * channels)
        first_ref[:, to] = handed_ref[:CTX, source]
        enter_ref[:, to] = join_three(handed_ref, CTX, source)
    rate = rate_ref[...]
    decay = jnp.exp(-rate)
    coef = coef_ref[...]

    def step(eight, state):
        rows = []
        for k in range(8):
            rows.append(coef * state)
            state = decay * state
        acc[aligned(eight * 8, 8), :] = sums_over_states(rows)
        return state

    lax.fori_loop(0, 16, step, enter_ref[...] * jnp.exp(-129.0 * rate))
    second_ref[...] = (local_ref[...] + acc[...]).astype(bf16)


def qkv_back(flag_ref, dqkv_ref, near_weight_ref, far_weight_ref, out_ref):
    split = near_weight_ref.shape[1]
    for half in range(2):
        out_ref[half] = mm(dqkv_ref[half, :, :split], near_weight_ref[...], NT) + mm(
            dqkv_ref[half, :, split:], far_weight_ref[...], NT
        )


def ssm_signal_grad(
    flag_ref, near_ref, returned_ref, rate_ref, coef_ref, skip_ref, total_ref, own_ref, send_ref,
    last_ref, adjoint_ref, rows_out, total,
):
    channels = rate_ref.shape[1] // 2
    adjoints = []
    for slot in range(2):
        to = slice(slot * channels, (slot + 1) * channels)
        source = slice((1 - slot) * channels, (2 - slot) * channels)
        last_ref[:, to] = returned_ref[:CTX, source].astype(f32)
        adjoints.append(join_three(returned_ref, CTX, source))
    decay = jnp.exp(-rate_ref[...])
    coef = coef_ref[...]
    skip = skip_ref[...]

    def step(j, adjoint, chunk):
        eight = 15 - j
        at = aligned(eight * 8, 8)
        if chunk % 2:
            g8 = (near_ref, last_ref)[chunk // 2][at, :]
        rows = [None] * 8
        for k in range(7, -1, -1):
            adjoint = decay * adjoint
            if chunk % 2:
                adjoint = adjoint + g8[k : k + 1]
            rows[k] = coef * adjoint
        y8 = sums_over_states(rows)
        if chunk % 2:
            y8 = y8 + skip * g8
        rows_out[aligned((chunk * 16 + eight) * 8, 8), :] = y8
        return adjoint

    adjoint = jnp.concatenate(adjoints, axis=1)
    adjoint_ref[...] = adjoint
    for chunk in (3, 2, 1, 0):
        adjoint = lax.fori_loop(0, 16, partial(step, chunk=chunk), adjoint)
    for half in (1, 0):
        total[...] = total_ref[half]
        source = aligned(jnp.bitwise_xor(flag_ref[ODD], half) * HALF, HALF)
        for slot, name in enumerate((NEAR, FAR)):
            total[:, aligned(flag_ref[name] * channels, channels)] += rows_out[
                source, slot * channels : (slot + 1) * channels
            ]
        if half:
            send_ref[...] = total[...].astype(bf16)
        else:
            own_ref[...] = total[...]


def ssm_param_grad(
    flag_ref, tile_ref, near_ref, last_ref, enter_ref, adjoint_ref, rate_ref, coef_ref, out_ref, xs
):
    load_signal(flag_ref, tile_ref, xs)
    decay = jnp.exp(-rate_ref[...])
    zero = jnp.zeros_like(decay)

    def step(eight, carry, chunk):
        state, slope, for_coef, for_rate = carry
        x8 = xs[aligned((chunk * 16 + eight) * 8, 8), :]
        if chunk % 2:
            g8 = (near_ref, last_ref)[chunk // 2][aligned(eight * 8, 8), :]
        for k in range(8):
            slope = decay * (slope + state)
            state = decay * state + x8[k : k + 1]
            if chunk % 2:
                for_coef = for_coef + state * g8[k : k + 1]
                for_rate = for_rate + slope * g8[k : k + 1]
        return state, slope, for_coef, for_rate

    carry = (enter_ref[...], zero, zero, zero)
    for chunk in range(4):
        carry = lax.fori_loop(0, 16, partial(step, chunk=chunk), carry)
    for_rate = carry[3] + decay * adjoint_ref[...] * carry[1]
    out_ref[:STATES, :] = -coef_ref[...] * for_rate
    out_ref[STATES : 2 * STATES, :] = carry[2]
    skip = jnp.sum(xs[CTX : 2 * CTX] * near_ref[...], axis=0, keepdims=True) + jnp.sum(
        xs[3 * CTX :] * last_ref[...], axis=0, keepdims=True
    )
    out_ref[2 * STATES :, :] = jnp.concatenate(
        [skip, jnp.zeros((out_ref.shape[0] - 2 * STATES - 1, skip.shape[1]), f32)], axis=0
    )


def causal(scores):
    rows = lax.broadcasted_iota(jnp.int32, scores.shape, 0)
    cols = lax.broadcasted_iota(jnp.int32, scores.shape, 1)
    return jnp.where(cols <= rows, scores, masked_score)


def softmax_parts(parts):
    top = parts[0].max(axis=-1, keepdims=True)
    for part in parts[1:]:
        top = jnp.maximum(top, part.max(axis=-1, keepdims=True))
    weights = [jnp.exp(part - top) for part in parts]
    total = weights[0].sum(axis=-1, keepdims=True)
    for weight in weights[1:]:
        total = total + weight.sum(axis=-1, keepdims=True)
    return [weight / total for weight in weights]


def block_probs(q0, q1, k0, k1, first, second, whole, late):
    has_first = late > 0
    is_whole = whole > 0
    chosen = jnp.where(is_whole, first, second)
    chosen_ok = jnp.logical_or(jnp.logical_not(is_whole), has_first)
    s00 = causal(mm(q0, k0, NT) * score_scale)
    s0c = jnp.where(has_first, mm(q0, first, NT) * score_scale, masked_score)
    s11 = causal(mm(q1, k1, NT) * score_scale)
    s10 = jnp.where(is_whole, mm(q1, k0, NT) * score_scale, masked_score)
    s1c = jnp.where(chosen_ok, mm(q1, chosen, NT) * score_scale, masked_score)
    return softmax_parts([s00, s0c]), softmax_parts([s11, s10, s1c]), chosen


def head_parts(qkv_ref, head, half):
    channels = qkv_ref.shape[2] // 3
    return [
        qkv_ref[half, :, part * channels + head * HD : part * channels + (head + 1) * HD]
        for part in range(3)
    ]


def attend(flag_ref, qkv_ref, first_ref, second_ref, att_ref, slot):
    half0 = flag_ref[ODD]
    half1 = 1 - half0
    heads = qkv_ref.shape[2] // (3 * HD)
    for head in range(heads):
        q0, k0, v0 = head_parts(qkv_ref, head, half0)
        q1, k1, v1 = head_parts(qkv_ref, head, half1)
        at = slice((slot * heads + head) * HD, (slot * heads + head + 1) * HD)
        first = first_ref[:, at]
        second = second_ref[:, at]
        (p00, p0c), (p11, p10, p1c), chosen = block_probs(
            q0, q1, k0, k1, first, second, flag_ref[WHOLE], flag_ref[LATE]
        )
        to = slice(head * HD, (head + 1) * HD)
        att_ref[half0, :, to] = (mm(p00.astype(bf16), v0) + mm(p0c.astype(bf16), first)).astype(
            bf16
        )
        att_ref[half1, :, to] = (
            mm(p11.astype(bf16), v1) + mm(p10.astype(bf16), v0) + mm(p1c.astype(bf16), chosen)
        ).astype(bf16)


def attention_near(flag_ref, qkv_ref, first_ref, second_ref, att_ref):
    attend(flag_ref, qkv_ref, first_ref, second_ref, att_ref, 0)


def attention_far(
    flag_ref, qkv_ref, first_ref, second_ref, near_ref, out_near_ref, out_far_ref, att_ref, own_ref,
    send_ref,
):
    attend(flag_ref, qkv_ref, first_ref, second_ref, att_ref, 1)

    def projected(half):
        return mm(near_ref[half], out_near_ref[...]) + mm(att_ref[half], out_far_ref[...], NT)

    send_ref[...] = projected(1).astype(bf16)
    own_ref[...] = projected(0)


def attended_grads(flag_ref, own_ref, other_ref, out_near_ref, out_far_ref, grad_ref, sent_ref):
    split = out_near_ref.shape[0]
    for half, ref in enumerate((own_ref, other_ref)):
        grad_ref[half, :, :split] = mm(ref[...], out_near_ref[...], NT).astype(bf16)
        grad_ref[half, :, split:] = mm(ref[...], out_far_ref[...]).astype(bf16)
        in_sent_order(flag_ref, ref, sent_ref.at[half])


def attention_backward(
    flag_ref, near_ref, far_ref, first_ref, second_ref, grad_ref, rate_ref, out_ref, second_out_ref,
    returned_ref,
):
    half0 = flag_ref[ODD]
    half1 = 1 - half0
    is_whole = flag_ref[WHOLE] > 0
    heads = near_ref.shape[2] // (3 * HD)
    for index in range(2 * heads):
        slot, head = index // heads, index % heads
        qkv_ref = (near_ref, far_ref)[slot]
        q0, k0, v0 = head_parts(qkv_ref, head, half0)
        q1, k1, v1 = head_parts(qkv_ref, head, half1)
        at = slice(index * HD, (index + 1) * HD)
        g0 = grad_ref[half0, :, at]
        g1 = grad_ref[half1, :, at]
        first = first_ref[:, at]
        second = second_ref[:, at]
        early, later, chosen = block_probs(
            q0, q1, k0, k1, first, second, flag_ref[WHOLE], flag_ref[LATE]
        )

        def score_grads(probs, rows, values):
            prob_grads = [mm(rows, v, NT) for v in values]
            centre = sum((p * d).sum(axis=-1, keepdims=True) for p, d in zip(probs, prob_grads))
            return [(p * (d - centre)).astype(bf16) for p, d in zip(probs, prob_grads)]

        d00, d0c = score_grads(early, g0, (v0, first))
        d11, d10, d1c = score_grads(later, g1, (v1, v0, chosen))
        p00, p0c = [p.astype(bf16) for p in early]
        p11, p10, p1c = [p.astype(bf16) for p in later]
        base = slot * 3 * heads * HD + head * HD
        for_q, for_k, for_v = [
            slice(base + part * heads * HD, base + part * heads * HD + HD) for part in range(3)
        ]
        out_ref[half0, :, for_q] = ((mm(d00, k0) + mm(d0c, first)) * score_scale).astype(bf16)
        out_ref[half1, :, for_q] = (
            (mm(d11, k1) + mm(d10, k0) + mm(d1c, chosen)) * score_scale
        ).astype(bf16)
        out_ref[half0, :, for_k] = ((mm(d00, q0, TN) + mm(d10, q1, TN)) * score_scale).astype(bf16)
        out_ref[half1, :, for_k] = (mm(d11, q1, TN) * score_scale).astype(bf16)
        out_ref[half0, :, for_v] = (mm(p00, g0, TN) + mm(p10, g1, TN)).astype(bf16)
        out_ref[half1, :, for_v] = mm(p11, g1, TN).astype(bf16)
        from_early = mm(d0c, q0, TN) * score_scale + mm(p0c, g0, TN)
        from_later = mm(d1c, q1, TN) * score_scale + mm(p1c, g1, TN)
        returned_ref[:CTX, at] = (from_early + jnp.where(is_whole, from_later, 0.0)).astype(bf16)
        second_out_ref[:, at] = jnp.where(is_whole, 0.0, from_later)

    rate = rate_ref[...]
    decay = jnp.exp(-rate)

    def step(j, adjoint):
        g8 = second_out_ref[aligned((15 - j) * 8, 8), :]
        for k in range(7, -1, -1):
            adjoint = decay * adjoint + g8[k : k + 1]
        return adjoint

    adjoint = lax.fori_loop(0, 16, step, jnp.zeros_like(rate)) * jnp.exp(-float(CTX) * rate)
    for k, part in enumerate(split_three(adjoint)):
        returned_ref[CTX + k * STATES : CTX + (k + 1) * STATES, :] = part


def feed_forward(
    flag_ref, n_ref, c_ref, up0_ref, down0_ref, up1_ref, down1_ref, act_ref, gate_ref, sent_ref,
    down_out_ref, back_out_ref, acc_down, acc_back,
):
    step = pl.program_id(0)
    steps = pl.num_programs(0)
    per = steps // 2

    @pl.when(step == 0)
    def _():
        acc_down[...] = jnp.zeros_like(acc_down)
        acc_back[...] = jnp.zeros_like(acc_back)
        in_sent_order(flag_ref, n_ref, sent_ref)

    def body(up, down, slot):
        gate = mm(n_ref[...], up)
        cdf = 0.5 * (1.0 + lax.erf(gate * (1.0 / math.sqrt(2.0))))
        act = (gate * cdf).astype(bf16)
        slope = cdf + gate * jnp.exp(-0.5 * gate * gate) * (1.0 / math.sqrt(2.0 * math.pi))
        grad = (mm(c_ref[...], down, NT) * slope).astype(bf16)
        gate_ref[...] = grad
        hidden = act_ref.shape[1] // 2
        width = hidden // GROUP
        count = act.shape[1] // width
        for k in range(count):
            mask = jnp.bitwise_xor(flag_ref[PLACE], (step - slot * per) * count + k)
            to = (1 - mask % 2) * 4 + (mask // 2 % 2) * 2 + mask // 4
            act_ref[:, aligned(slot * hidden + to * width, width)] = act[
                :, k * width : (k + 1) * width
            ]
        acc_down[...] += mm(act, down)
        acc_back[...] += mm(grad, up, NT)

    @pl.when(step < per)
    def _():
        body(up0_ref[...], down0_ref[...], 0)

    @pl.when(step >= per)
    def _():
        body(up1_ref[...], down1_ref[...], 1)

    @pl.when(step == steps - 1)
    def _():
        down_out_ref[...] = acc_down[...].astype(down_out_ref.dtype)
        back_out_ref[...] = acc_back[...].astype(back_out_ref.dtype)


def run_feed_forward(flags, rows, cot, up, down, up_far, down_far, kind):
    tokens, width = rows.shape
    block = 512
    hidden = up.shape[1]
    per = hidden // block

    def near_at(j):
        return jnp.minimum(j, per - 1)

    def far_at(j):
        return jnp.maximum(j - per, 0)

    whole = pl.BlockSpec((tokens, width), lambda j: (0, 0))
    return pl.pallas_call(
        feed_forward,
        grid=(2 * per,),
        out_shape=(
            shape((tokens, 2 * hidden), bf16),
            shape((tokens, 2 * hidden), bf16),
            shape((tokens, width), bf16),
            shape((tokens, width), kind),
            shape((tokens, width), kind),
        ),
        in_specs=[
            pl.BlockSpec(memory_space=pltpu.SMEM),
            whole,
            whole,
            pl.BlockSpec((width, block), lambda j: (0, near_at(j))),
            pl.BlockSpec((block, width), lambda j: (near_at(j), 0)),
            pl.BlockSpec((width, block), lambda j: (0, far_at(j))),
            pl.BlockSpec((block, width), lambda j: (far_at(j), 0)),
        ],
        out_specs=(
            pl.BlockSpec((tokens, 2 * hidden), lambda j: (0, 0)),
            pl.BlockSpec((tokens, block), lambda j: (0, j)),
            whole,
            whole,
            whole,
        ),
        scratch_shapes=[pltpu.VMEM((tokens, width), f32), pltpu.VMEM((tokens, width), f32)],
        compiler_params=pltpu.CompilerParams(
            vmem_limit_bytes=24 * 1024 * 1024, dimension_semantics=("arbitrary",)
        ),
        cost_estimate=length(0),
    )(flags, rows, cot, up, down, up_far, down_far)


def products(lhs_refs, rhs_refs, columns, split=None):
    total = None
    for lhs_ref, rhs_ref in zip(lhs_refs, rhs_refs):
        term = mm(lhs_ref[:, columns], rhs_ref[...], TN)
        total = term if total is None else total + term
    return total


def down_pass(flag_ref, act0, act1, cot0, cot1, out_ref):
    hidden = act0.shape[1] // 2
    part = hidden // 4
    for slot in range(2):
        value = products(
            (act0, act1), (cot0, cot1), slice(slot * hidden, slot * hidden + hidden // 2)
        ).astype(bf16)
        out_ref[slot * part : (slot + 1) * part, :] = value[part:]
        out_ref[(2 + slot) * part : (3 + slot) * part, :] = value[:part]


def down_keep(flag_ref, act0, act1, cot0, cot1, core_ref, send_ref, left_ref):
    hidden = act0.shape[1] // 2
    part = hidden // 4
    for slot in range(2):
        value = products(
            (act0, act1), (cot0, cot1), slice(slot * hidden + hidden // 2, (slot + 1) * hidden)
        )
        to = slice(slot * part, (slot + 1) * part)
        send_ref[to, :] = (value[part:] + core_ref[to, :].astype(f32)).astype(bf16)
        left_ref[to, :] = value[:part] + core_ref[2 * part + to.start : 2 * part + to.stop, :].astype(
            f32
        )


def down_step(flag_ref, left_ref, received_ref, own_ref, send_ref):
    rows = own_ref.shape[0] // 2
    for slot in range(2):
        to = slice(slot * rows, (slot + 1) * rows)
        own = slice(2 * slot * rows, (2 * slot + 1) * rows)
        send = slice((2 * slot + 1) * rows, (2 * slot + 2) * rows)
        own_ref[to, :] = left_ref[own, :] + received_ref[own, :].astype(f32)
        send_ref[to, :] = (left_ref[send, :] + received_ref[send, :].astype(f32)).astype(bf16)


def y_first(value, rows):
    parts = [value[k * rows : (k + 1) * rows] for k in (1, 3, 0, 2)]
    return jnp.concatenate(parts[:2], 0), jnp.concatenate(parts[2:], 0)


def rows_pass(flag_ref, lhs0, lhs1, rhs0, rhs1, out_ref):
    half = lhs0.shape[1] // 2
    value = products((lhs0, lhs1), (rhs0, rhs1), slice(0, half)).astype(bf16)
    send, left = y_first(value, half // 4)
    out_ref[: half // 2, :] = send
    out_ref[half // 2 :, :] = left


def rows_keep(flag_ref, lhs0, lhs1, rhs0, rhs1, core_ref, send_ref, left_ref):
    half = lhs0.shape[1] // 2
    value = products((lhs0, lhs1), (rhs0, rhs1), slice(half, 2 * half))
    send, left = y_first(value, half // 4)
    send_ref[...] = (send + core_ref[: half // 2, :].astype(f32)).astype(bf16)
    left_ref[...] = left + core_ref[half // 2 :, :].astype(f32)


def up_step(flag_ref, left_ref, received_ref, own_ref, send_ref):
    rows = own_ref.shape[0]
    own_ref[...] = left_ref[:rows, :] + received_ref[:rows, :].astype(f32)
    send_ref[...] = (left_ref[rows:, :] + received_ref[rows:, :].astype(f32)).astype(bf16)


def own_down(flag_ref, own_ref, received_ref, near_ref, far_ref):
    rows = near_ref.shape[0]
    near_ref[...] = own_ref[:rows, :] + received_ref[:rows, :].astype(f32)
    far_ref[...] = (own_ref[rows:, :] + received_ref[rows:, :].astype(f32)).astype(bf16)


def own_up(flag_ref, own_ref, received_ref, near_ref, far_ref):
    width = near_ref.shape[1]
    near_ref[...] = own_ref[:, :width] + received_ref[:, :width].astype(f32)
    far_ref[...] = (own_ref[:, width:] + received_ref[:, width:].astype(f32)).astype(bf16)


def attn_pass(flag_ref, one0, one1, dqkv0, dqkv1, back0, back1, att0, att1, att2, att3, out_ref):
    half = one0.shape[1] // 2
    width = dqkv0.shape[1]
    channels = att0.shape[1]
    columns = slice(0, half)
    out_ref[:, :width] = products((one0, one1), (dqkv0, dqkv1), columns).astype(bf16)
    for slot, pair in enumerate(((att0, att1), (att2, att3))):
        at = width + slot * channels
        out_ref[:, at : at + channels] = products((back0, back1), pair, columns).astype(bf16)


def attn_keep(
    flag_ref, one0, one1, dqkv0, dqkv1, back0, back1, att0, att1, att2, att3, core_ref, own_ref,
    *send_refs,
):
    half = one0.shape[1] // 2
    rows = half // 4
    width = dqkv0.shape[1]
    channels = att0.shape[1]
    columns = slice(half, 2 * half)
    blocks = [(0, products((one0, one1), (dqkv0, dqkv1), columns))]
    for slot, pair in enumerate(((att0, att1), (att2, att3))):
        blocks.append((width + slot * channels, products((back0, back1), pair, columns)))
    for at, block in blocks:
        to = slice(at, at + block.shape[1])
        block = block + core_ref[:, to].astype(f32)
        own_ref[:, to] = block[:rows]
        for k, ref in enumerate(send_refs):
            ref[:, to] = block[(k + 1) * rows : (k + 2) * rows].astype(bf16)


def attn_own(
    flag_ref, own_ref, r1_ref, r2_ref, r3_ref, param_ref, gains_ref, gains_received, near_ref,
    far_ref,
):
    rows = own_ref.shape[0]
    total = own_ref[...] + (
        r1_ref[...].astype(f32) + r2_ref[...].astype(f32) + r3_ref[...].astype(f32)
    )
    channels = total.shape[1] // 8
    gains = gains_ref[...] + gains_received[...]
    for slot, ref in enumerate((near_ref, far_ref)):
        ref[:rows, : 3 * channels] = total[:, slot * 3 * channels : (slot + 1) * 3 * channels].astype(
            ref.dtype
        )
        ref[:rows, 3 * channels :] = total[
            :, (6 + slot) * channels : (7 + slot) * channels
        ].astype(ref.dtype)
        small = jnp.concatenate(
            [param_ref[:, slot * channels : (slot + 1) * channels], gains], axis=0
        )
        count = small.shape[0] // 4
        rest = jnp.zeros((ref.shape[0] - rows - count, channels), f32)
        for quarter in range(4):
            ref[rows:, quarter * channels : (quarter + 1) * channels] = jnp.concatenate(
                [small[quarter * count : (quarter + 1) * count], rest], axis=0
            ).astype(ref.dtype)


def add_two(flag_ref, a_ref, b_ref, out_ref):
    out_ref[...] = (a_ref[...].astype(f32) + b_ref[...].astype(f32)).astype(out_ref.dtype)


def add_three(flag_ref, a_ref, b_ref, c_ref, out_ref):
    out_ref[...] = (a_ref[...] + b_ref[...] + c_ref[...].astype(f32)).astype(out_ref.dtype)


def sources(flag_ref, even_ref, odd_ref, rows):
    for pair in range(GROUP // 2):
        for side, ref in enumerate((even_ref, odd_ref)):
            source = jnp.bitwise_xor(flag_ref[PLACE], 2 * pair + side)
            yield ref, pair, aligned(source * rows, rows)


def assemble_weight(flag_ref, even_ref, odd_ref, tile_ref, weight_ref, out_ref, qkv_ref):
    split = weight_ref.shape[1]
    for ref, pair, at in sources(flag_ref, even_ref, odd_ref, even_ref.shape[1]):
        weight_ref[at, :] = ref[pair, :, :split]
        out_ref[at, :] = ref[pair, :, split:]
    project(flag_ref, tile_ref, weight_ref, qkv_ref)


def assemble_grad(
    flag_ref, even_ref, odd_ref, qkv_ref, out_ref, rate_ref, coef_ref, skip_ref, gain_one_ref,
    gain_two_ref,
):
    channels = qkv_ref.shape[2]
    rows = qkv_ref.shape[1] // GROUP
    total = None
    for ref, pair, at in sources(flag_ref, even_ref, odd_ref, rows):
        for part in range(3):
            qkv_ref[part, at, :] = ref[
                pair, :rows, part * channels : (part + 1) * channels
            ].astype(f32)
        out_ref[:, at] = ref[pair, :rows, 3 * channels :].astype(f32).T
        term = ref[pair, rows:, :].astype(f32)
        total = term if total is None else total + term
    count = (2 * STATES + 8 + 8) // 4

    def row(k):
        return total[k % count : k % count + 1, k // count * channels : (k // count + 1) * channels]

    for k in range(STATES):
        rate_ref[k : k + 1, :] = row(k)
        coef_ref[k : k + 1, :] = row(STATES + k)
    skip_ref[...] = row(2 * STATES)
    for which, ref in enumerate((gain_one_ref, gain_two_ref)):
        for k in range(4):
            ref[:, k * channels : (k + 1) * channels] = row(2 * STATES + 8 + which * 4 + k)


def stack_two(flag_ref, a_ref, ax_ref, b_ref, by_ref, a_out, b_out):
    a_out[0], a_out[1] = a_ref[...], ax_ref[...]
    b_out[0], b_out[1] = b_ref[...], by_ref[...]


def stack_three(flag_ref, a_ref, ax_ref, b_ref, by_ref, a_out, b_out, both_out):
    stack_two(flag_ref, a_ref, ax_ref, b_ref, by_ref, a_out, b_out)
    both_out[0, 0], both_out[0, 1] = a_ref[...], b_ref[...]
    both_out[1, 0], both_out[1, 1] = ax_ref[...], by_ref[...]


def stack_pairs(flag_ref, a_ref, b_ref, out_ref):
    out_ref[0, 0], out_ref[0, 1] = a_ref[0], b_ref[0]
    out_ref[1, 0], out_ref[1, 1] = a_ref[1], b_ref[1]


def stack_four(flag_ref, a_ref, b_ref, c_ref, d_ref, out_ref):
    for k, ref in enumerate((a_ref, b_ref, c_ref, d_ref)):
        out_ref[k] = ref[...]


def stack_eight(flag_ref, a_ref, ay_ref, b_ref, bx_ref, out_ref):
    out_ref[0, 0], out_ref[1, 0] = a_ref[0], a_ref[1]
    out_ref[2, 0], out_ref[3, 0] = ay_ref[0], ay_ref[1]
    out_ref[0, 1], out_ref[2, 1] = b_ref[0], b_ref[1]
    out_ref[1, 1], out_ref[3, 1] = bx_ref[0], bx_ref[1]


def place_two(flag_ref, even_ref, odd_ref, a_out, b_out):
    for ref, pair, at in sources(flag_ref, even_ref, odd_ref, even_ref.shape[2]):
        a_out[at, :] = ref[pair, 0].astype(a_out.dtype)
        b_out[at, :] = ref[pair, 1].astype(b_out.dtype)


def place_wide(flag_ref, own_ref, other_ref, *refs):
    for side, ref in enumerate((own_ref, other_ref)):

        @pl.when(pl.program_id(0) % 2 == side)
        def _():
            refs[-2][...] = ref[0, 0].astype(f32)
            refs[-1][...] = ref[0, 1].astype(f32)


def run_place_wide(flags, own, other, starts, steps, filled=()):
    rows, width = own.shape[2:]
    piece = pl.BlockSpec((1, 2, rows, width), lambda j, flag_ref: (j // 2, 0, 0, 0))

    def place(which):
        return pl.BlockSpec(
            (rows, width),
            lambda j, flag_ref: (
                jnp.bitwise_xor(
                    flag_ref[PLACE], starts[which] + (j // 2) * steps[which] + j % 2
                ),
                0,
            ),
        )

    out = shape((GROUP * rows, width))
    return pl.pallas_call(
        place_wide,
        grid_spec=pltpu.PrefetchScalarGridSpec(
            num_scalar_prefetch=1,
            grid=(GROUP // 2,),
            in_specs=[piece, piece] + [pl.BlockSpec(memory_space=pl.ANY)] * len(filled),
            out_specs=(place(0), place(1)),
        ),
        out_shape=(out, out),
        input_output_aliases={3 + k: k for k in range(len(filled))},
        compiler_params=pltpu.CompilerParams(vmem_limit_bytes=VMEM_LIMIT),
        cost_estimate=length(0),
    )(flags, own, other, *filled)


def place_last(flag_ref, own_ref, other_ref, *refs, starts, steps):
    outs, (wide, sems) = refs[2:4], refs[4:]
    rows = own_ref.shape[2]
    copies = []
    for j in range(GROUP // 2):
        ref = (own_ref, other_ref)[j % 2]
        for which in range(2):
            source = jnp.bitwise_xor(
                flag_ref[PLACE], starts[which] + (j // 2) * steps[which] + j % 2
            )
            wide[2 * j + which] = ref[j // 2, which].astype(f32)
            copy = pltpu.make_async_copy(
                wide.at[2 * j + which],
                outs[which].at[aligned(source * rows, rows), :],
                sems.at[2 * j + which],
            )
            copy.start()
            copies.append(copy)
    for copy in copies:
        copy.wait()


def run_place_last(flags, own, other, starts, steps, filled):
    rows, width = own.shape[2:]
    vmem = pl.BlockSpec(memory_space=pltpu.VMEM)
    out = shape((GROUP * rows, width))
    return pl.pallas_call(
        partial(place_last, starts=starts, steps=steps),
        in_specs=[pl.BlockSpec(memory_space=pltpu.SMEM), vmem, vmem]
        + [pl.BlockSpec(memory_space=pl.ANY)] * 2,
        out_specs=(pl.BlockSpec(memory_space=pl.ANY),) * 2,
        out_shape=(out, out),
        input_output_aliases={3: 0, 4: 1},
        scratch_shapes=[
            pltpu.VMEM((GROUP, rows, width), f32),
            pltpu.SemaphoreType.DMA((GROUP,)),
        ],
        compiler_params=pltpu.CompilerParams(vmem_limit_bytes=VMEM_LIMIT),
        cost_estimate=length(0),
    )(flags, own, other, *filled)


class Order:
    def __init__(self):
        self.last = ()

    def __call__(self, *values):
        tied = lax.optimization_barrier((values, self.last))[0]
        return tied[0] if len(tied) == 1 else tied

    def done(self, result):
        self.last = result
        return result


def per_device(
    inputs,
    block_size,
    gain_attn,
    qkv_weight,
    ssm_rate,
    ssm_coef,
    ssm_skip,
    out_weight,
    gain_mlp,
    up_weight,
    down_weight,
    cotangent,
    dp_size,
):
    z = lax.axis_index("mp")
    place = jnp.bitwise_and(lax.axis_index("dp"), GROUP - 1)

    def swap_mp(value, mask):
        return lax.ppermute(value, "mp", [(k, k ^ mask) for k in range(4)])

    def swap_dp(value, mask):
        return lax.ppermute(value, "dp", [(k, k ^ mask) for k in range(dp_size)])

    def gather_by_xor(piece):
        return [piece] + [swap_dp(piece, 2 * k) for k in range(1, GROUP // 2)]

    def low(*dims):
        return shape(dims, bf16)

    def over_groups(own):
        mask = GROUP
        while mask < dp_size:
            own = own + swap_dp(own.astype(bf16), mask).astype(f32)
            mask *= 2
        return own.astype(bf16)

    model_dim = inputs.shape[2]
    channels = qkv_weight.shape[2]
    hidden = up_weight.shape[1]
    wide = 2 * channels
    rows = model_dim // GROUP
    row = inputs[0]
    cot = cotangent[0]
    z_far = jnp.bitwise_xor(z, 2)
    whole = (block_size[0] > HALF).astype(jnp.int32)
    flags = jnp.stack(
        [whole, jnp.right_shift(z, 1), jnp.bitwise_and(z, 1), z, z_far, place]
    ).astype(jnp.int32)
    gain_one = gain_attn[None]
    gain_two = gain_mlp[None]
    order = Order()
    half = shape((HALF, model_dim))
    half_low = shape((HALF, model_dim), bf16)

    normed_one = order.done(call(norm_one, half_low)(flags, row, gain_one))
    paired_one = swap_mp(normed_one, 1)
    qkv_parts = jnp.transpose(qkv_weight, (1, 0, 2))
    attn_slice, up_slice, down_slice, ssm_pack = order.done(
        run_cut_slices(
            flags, order(qkv_parts), out_weight, up_weight, down_weight, ssm_rate.T, ssm_coef.T,
            ssm_skip[None],
        )
    )
    attn_across = swap_mp(attn_slice, 2)
    near_qkv = order.done(jnp.concatenate(list(order(*[qkv_parts[k] for k in range(3)])), 1))

    paired_one, attn_across = order.done(order(paired_one, attn_across))
    attn_own_slice = attn_across[:rows]
    attn_x = swap_dp(attn_own_slice, 2)
    attn_y = swap_dp(attn_own_slice, 4)
    up_across = swap_mp(order(up_slice), 2)
    paired_cot = swap_mp(order(cot), 1)
    ssm_both = call(join_ssm, shape((48, wide)))(flags, ssm_pack, attn_across)
    rate_t, coef_t, skip_t = ssm_both[:16], ssm_both[16:32], ssm_both[32:33]
    tile_one, one_sent, second_local, handed = order.done(
        call(
            ssm_forward,
            (
                shape((2, HALF, model_dim), bf16),
                shape((2, HALF, model_dim), bf16),
                shape((CTX, wide)),
                shape((CTX + 3 * STATES, wide), bf16),
            ),
            scratch=[pltpu.VMEM((2 * HALF, wide), f32)],
        )(flags, normed_one, order(paired_one), rate_t, coef_t, skip_t)
    )
    handed = lax.ppermute(handed, "mp", [(0, 2), (1, 3)])

    qkv_shape = shape((2, HALF, 3 * channels), bf16)
    att_shape = shape((2, HALF, channels), bf16)
    attn_x = order.done(order(attn_x))
    attn_xy = swap_dp(attn_x, 4)
    attn_y, paired_cot, mlp_up = order.done(order(attn_y, paired_cot, up_across))
    mlp_up_x = swap_dp(mlp_up, 2)
    qkv_near = order.done(call(project, qkv_shape)(flags, order(tile_one), near_qkv))
    even = order.done(
        call(stack_four, shape((4,) + attn_x.shape, bf16))(
            flags, attn_own_slice, attn_x, attn_y, order(attn_xy)
        )
    )
    odd_part = swap_dp(even, 1)
    slice_shape = low(rows, model_dim)
    handed = order.done(order(handed))
    down_across = swap_mp(order(down_slice), 2)
    ctx_first, ctx_second, enter_state = order.done(
        call(
            ssm_carry_in,
            (shape((CTX, wide), bf16), shape((CTX, wide), bf16), shape((STATES, wide))),
            scratch=[pltpu.VMEM((CTX, wide), f32)],
            micros=16,
        )(flags, order(second_local), handed, rate_t, coef_t)
    )
    att_near = order.done(
        call(attention_near, att_shape)(flags, order(qkv_near), ctx_first, ctx_second)
    )
    far_qkv, far_out, qkv_far = order.done(
        call(
            assemble_weight,
            (
                shape((model_dim, 3 * channels), bf16),
                shape((model_dim, channels), bf16),
                qkv_shape,
            ),
        )(flags, even, order(odd_part), tile_one)
    )
    att_far, out_own, out_send = order.done(
        call(attention_far, (att_shape, half, half_low))(
            flags, order(qkv_far), ctx_first, ctx_second, att_near, out_weight, far_out
        )
    )
    out_received = swap_mp(out_send, 1)
    pair_shape = low(2, rows, model_dim)
    mlp_down = order.done(order(down_across))
    mlp_down_y = swap_dp(mlp_down, 4)
    mlp_up_two, mlp_down_two = order.done(
        call(stack_two, (pair_shape, pair_shape), micros=0.5)(
            flags, mlp_up, order(mlp_up_x), mlp_down, order(mlp_down_y)
        )
    )
    mlp_up_y = swap_dp(mlp_up_two, 4)
    mlp_down_x = swap_dp(mlp_down_two, 2)
    middle, normed_two = order.done(
        call(norm_two, (half, half_low), micros=3)(
            flags, row, out_own, order(out_received), gain_two
        )
    )

    paired_two = swap_mp(normed_two, 1)
    eight_shape = low(GROUP // 2, 2, rows, model_dim)
    mlp_even = order.done(
        call(stack_eight, eight_shape, micros=1)(
            flags, mlp_up_two, order(mlp_up_y), mlp_down_two, order(mlp_down_x)
        )
    )
    mlp_odd = swap_dp(mlp_even, 1)
    paired_two = order(paired_two)
    warm = order.done(
        call(touch, shape((16, 128), bf16), micros=30)(
            flags, up_weight, down_weight, cot, paired_cot, paired_two
        )
    )
    up_far, down_far = order.done(
        call(place_two, (low(model_dim, hidden), low(hidden, model_dim)))(
            flags, mlp_even, order(mlp_odd)
        )
    )
    mlp = (up_weight, down_weight, up_far, down_far)
    act_other, gate_other, two_other, down_send, back_send = order.done(
        run_feed_forward(flags, order(paired_two), paired_cot, *mlp, bf16)
    )
    back_received = swap_mp(back_send, 1)
    act_own, gate_own, two_own, down_own, back_own = order.done(
        run_feed_forward(flags, order(normed_two), cot, *mlp, f32)
    )

    side = model_dim // 2
    acts = (act_own, act_other, cot, paired_cot)
    passed = order.done(call(down_pass, low(hidden, model_dim))(flags, order(act_own), *acts[1:]))
    down_core = swap_dp(passed, 1)
    ups = (two_own, two_other, gate_own, gate_other)
    passed = order.done(call(rows_pass, low(side, 2 * hidden))(flags, order(two_own), *ups[1:]))
    up_core = swap_dp(passed, 1)
    middle_grad, attn_grad, gain_mlp_grad = order.done(
        call(norm_two_back, (half, half_low, shape((1, model_dim))), micros=12)(
            flags, middle, back_own, order(back_received), cot, gain_two, warm
        )
    )
    paired_back = swap_mp(attn_grad, 1)
    down_send_x, down_left = order.done(
        call(down_keep, (low(side, model_dim), shape((side, model_dim))))(
            flags, *acts, order(down_core)
        )
    )
    down_x = swap_dp(down_send_x, 2)
    up_send_y, up_left = order.done(
        call(rows_keep, (low(side // 2, 2 * hidden), shape((side // 2, 2 * hidden))))(
            flags, *ups, order(up_core)
        )
    )
    up_y = swap_dp(up_send_y, 4)

    att_grad, back_sent = order.done(
        call(
            attended_grads,
            (shape((2, HALF, wide), bf16), shape((2, HALF, model_dim), bf16)),
            micros=4,
        )(flags, attn_grad, order(paired_back), out_weight, far_out)
    )
    down_received = swap_mp(order(down_send), 1)
    dqkv, second_grad, returned = order.done(
        call(
            attention_backward,
            (
                shape((2, HALF, 6 * channels), bf16),
                shape((CTX, wide)),
                shape((CTX + 3 * STATES, wide), bf16),
            ),
        )(flags, qkv_near, qkv_far, ctx_first, ctx_second, order(att_grad), rate_t)
    )
    returned = lax.ppermute(returned, "mp", [(2, 0), (3, 1)])
    one_total = order.done(
        call(qkv_back, shape((2, HALF, model_dim)))(flags, order(dqkv), near_qkv, far_qkv)
    )
    attns = (
        one_sent[0], one_sent[1], dqkv[0], dqkv[1], back_sent[0], back_sent[1],
        att_near[0], att_near[1], att_far[0], att_far[1],
    )
    passed = order.done(
        call(attn_pass, low(side, 8 * channels))(flags, order(attns[0]), *attns[1:])
    )
    attn_core = swap_dp(passed, 1)
    down_mine, down_send_y = order.done(
        call(down_step, (shape((2 * rows, model_dim)), low(2 * rows, model_dim)))(
            flags, down_left, order(down_x)
        )
    )
    down_y = swap_dp(down_send_y, 4)
    up_mine, up_send_x = order.done(
        call(up_step, (shape((rows, 2 * hidden)), low(rows, 2 * hidden)))(
            flags, up_left, order(up_y)
        )
    )
    up_x = swap_dp(up_send_x, 2)
    one_own, one_send, last_grad, enter_adjoint = order.done(
        call(
            ssm_signal_grad,
            (half, half_low, shape((CTX, wide)), shape((STATES, wide))),
            scratch=[pltpu.VMEM((2 * HALF, wide), f32), pltpu.VMEM((HALF, model_dim), f32)],
            micros=30,
        )(flags, second_grad, order(returned), rate_t, coef_t, skip_t, one_total)
    )
    one_received = swap_mp(one_send, 1)
    down_received = order.done(order(down_received))
    attn_mine, *attn_sends = order.done(
        call(attn_keep, (shape((rows, 8 * channels)),) + (low(rows, 8 * channels),) * 3)(
            flags, *attns, order(attn_core)
        )
    )
    attn_sent = [swap_dp(part, SENT[5 + k]) for k, part in enumerate(attn_sends)]
    wide_slice = shape((rows, model_dim))
    down_near, down_far_grad = order.done(
        call(own_down, (wide_slice, slice_shape))(flags, down_mine, order(down_y))
    )
    down_received_far = swap_mp(down_far_grad, 2)
    up_near, up_far_grad = order.done(
        call(own_up, (wide_slice, slice_shape))(flags, up_mine, order(up_x))
    )
    up_received_far = swap_mp(up_far_grad, 2)
    param_grad = order.done(
        call(
            ssm_param_grad,
            shape((40, wide)),
            scratch=[pltpu.VMEM((2 * HALF, wide), f32)],
            micros=3,
        )(
            flags, order(tile_one), second_grad, last_grad, enter_state, enter_adjoint, rate_t, coef_t
        )
    )
    input_grad, gains = order.done(
        call(norm_one_back, (half, shape((2 * model_dim // channels, channels))))(
            flags, row, one_own, order(one_received), middle_grad, gain_one, gain_mlp_grad
        )
    )
    gains_received = swap_mp(gains, 1)
    down_mine = order.done(
        call(add_two, slice_shape)(flags, down_near, order(down_received_far))
    )
    down_mine = over_groups(down_mine)
    down_x = swap_dp(down_mine, 2)
    up_mine = order.done(call(add_two, slice_shape)(flags, up_near, order(up_received_far)))
    up_mine = over_groups(up_mine)
    up_y = swap_dp(up_mine, 4)
    slice_rows = rows + 16
    *attn_sent, gains_received = order(*attn_sent, gains_received)
    attn_near, attn_send = order.done(
        call(attn_own, (shape((slice_rows, 4 * channels)), low(slice_rows, 4 * channels)))(
            flags, attn_mine, *attn_sent, param_grad, gains, gains_received
        )
    )
    attn_received = swap_mp(attn_send, 2)
    both_shape = low(2, 2, rows, model_dim)
    down_two, up_two, first_pieces = order.done(
        call(stack_three, (pair_shape, pair_shape, both_shape), micros=3)(
            flags, down_mine, order(down_x), up_mine, order(up_y)
        )
    )
    down_y = swap_dp(down_two, 4)
    up_x = swap_dp(up_two, 2)
    first_others = swap_dp(first_pieces, 1)
    output = order.done(
        call(add_three, half_low)(flags, middle, order(down_own), down_received)
    )
    attn_slice_grad = order.done(
        call(add_two, low(slice_rows, 4 * channels), micros=20)(
            flags, attn_near, order(attn_received)
        )
    )
    first_others = order.done(order(first_others))
    attn_slice_grad = over_groups(order(attn_slice_grad))
    attn_sent = [swap_dp(attn_slice_grad, 2 * k) for k in range(1, GROUP // 2)]
    wide_grads = order.done(
        run_place_wide(flags, first_pieces, order(first_others), (0, 0), (2, 4))
    )
    even = order.done(
        call(stack_four, low(4, slice_rows, 4 * channels))(
            flags, attn_slice_grad, *order(*attn_sent)
        )
    )
    odd_part = swap_dp(even, 1)
    last_pieces = order.done(
        call(stack_pairs, both_shape, micros=8)(flags, *order(down_y, up_x))
    )
    last_others = swap_dp(last_pieces, 1)
    qkv_grad, out_grad, rate_grad, coef_grad, skip_grad, gain_one_grad, gain_two_grad = order.done(
        call(
            assemble_grad,
            (
                shape((3, model_dim, channels)),
                shape(out_weight.shape),
                shape((STATES, channels)),
                shape((STATES, channels)),
                shape((1, channels)),
                shape((1, model_dim)),
                shape((1, model_dim)),
            ),
            micros=8,
        )(flags, even, order(odd_part))
    )
    down_grad, up_grad = run_place_last(
        flags, last_pieces, order(last_others), (4, 2), (2, 4), wide_grads
    )
    return (
        output[None],
        input_grad[None],
        gain_one_grad[0],
        jnp.transpose(qkv_grad, (1, 0, 2)),
        rate_grad.T,
        coef_grad.T,
        skip_grad[0],
        out_grad,
        gain_two_grad[0],
        up_grad,
        down_grad,
    )


def solution(mesh):
    return jax.shard_map(
        partial(per_device, dp_size=mesh.shape["dp"]),
        mesh=mesh,
        in_specs=(
            P("dp", "mp", None),
            P("dp"),
            P(),
            P(None, None, "mp"),
            P("mp", None),
            P("mp", None),
            P("mp"),
            P("mp", None),
            P(),
            P(None, "mp"),
            P("mp", None),
            P("dp", "mp", None),
        ),
        out_specs=(
            P("dp", "mp", None),
            P("dp", "mp", None),
            P(),
            P(None, None, "mp"),
            P("mp", None),
            P("mp", None),
            P("mp"),
            P("mp", None),
            P(),
            P(None, "mp"),
            P("mp", None),
        ),
        check_vma=False,
    )
```
